32 devices in a mesh: replica: 4 (over z), shard: 4 (over y, x), half: 2 (over core).
Axes of the slice: x: 2, y: 2, z: 4, core: 2. Of those that a mesh axis runs over, the one named last changes fastest.
Arguments:
- images: bfloat16 [64, 24, 24, 768], P(('replica', 'shard'), 'half'), may hold values from -6 to 6
- cotangent: bfloat16 [64, 24, 24, 768], P(('replica', 'shard'), 'half'), may hold values from -6 to 6
- present: int32 [64], P(('replica', 'shard')), may hold values 0 or 1
- threshold: float32 [24], replicated, may hold values from 3 to 12
- inner_weight: bfloat16 [768, 2304], P('shard'), may hold values from -0.3125 to 0.3125
- inner_bias: bfloat16 [1536], P('shard'), may hold values from -3 to 3
- outer_weight: bfloat16 [768, 768], P('shard'), may hold values from -0.625 to 0.625
- outer_bias: bfloat16 [768], P('shard'), may hold values from -2 to 2
- expand_weight: bfloat16 [768, 3072], P('shard'), may hold values from -0.21875 to 0.21875
- expand_bias: bfloat16 [3072], P('shard'), may hold values from -2 to 2
- reduce_weight: bfloat16 [3072, 768], P('shard'), may hold values from -0.15625 to 0.15625
- reduce_bias: bfloat16 [768], P('shard'), may hold values from -2 to 2
- first_gain: bfloat16 [768], P('shard'), may hold values from 0.5 to 1.5
- first_shift: bfloat16 [768], P('shard'), may hold values from -2 to 2
- second_gain: bfloat16 [768], P('shard'), may hold values from 0.5 to 1.5
- second_shift: bfloat16 [768], P('shard'), may hold values from -2 to 2
- bias_table: bfloat16 [529, 24], replicated, may hold values from -4 to 4
Outputs:
- block_out: bfloat16 [64, 24, 24, 768], P(('replica', 'shard'), 'half')
- grad_images: bfloat16 [64, 24, 24, 768], P(('replica', 'shard'), 'half')
- grad_inner_weight: float32 [768, 2304], P('shard')
- grad_inner_bias: float32 [1536], P('shard')
- grad_outer_weight: float32 [768, 768], P('shard')
- grad_outer_bias: float32 [768], P('shard')
- grad_expand_weight: float32 [768, 3072], P('shard')
- grad_expand_bias: float32 [3072], P('shard')
- grad_reduce_weight: float32 [3072, 768], P('shard')
- grad_reduce_bias: float32 [768], P('shard')
- grad_first_gain: float32 [768], P('shard')
- grad_first_shift: float32 [768], P('shard')
- grad_second_gain: float32 [768], P('shard')
- grad_second_shift: float32 [768], P('shard')
- grad_bias_table: float32 [529, 24], replicated
- clipped_inner: bfloat16 [768, 2304], P('shard')
- factors: float32 [24], replicated
- maxima: float32 [24], replicated
The draws below stay inside these ranges and needn't reach their ends.
All inputs are finite; a program needn't handle non-finite values. No bound on the sum of `present` on one device may be relied on, other than what follows from the above.
Results may differ from the reference program's by a relative error of at most 0.019.
Values may be sent and summed in bfloat16 or wider, within the bound.
No kernel may reach another device: no remote copies, remote signals or barrier semaphores. Data moves between devices by JAX's collectives and lax.ppermute only.
A program may use at most 320 MiB of HBM per device.

```python
import math
import jax
import jax.numpy as jnp
from jax import lax

D = 768
HEADS = 24
FF = 3072
HEAD_DIM = 32
WIN = 12
GRID = 24
SHIFT = 6
TABLE = 529
IMAGES = 64


def place_ends(values, own_key, least, largest):
    longest = values.shape.index(max(values.shape))
    spots = []
    for shift in (0, 1):
        where = [jax.random.randint(jax.random.fold_in(own_key, axis), (), 0, length) for axis, length in enumerate(values.shape)]
        where[longest] = (where[longest] + shift) % values.shape[longest]
        spots.append(tuple(where))
    return values.at[spots[0]].set(least).at[spots[1]].set(largest)


def steps_of(rng, extent, cuts, least, largest):
    gain, own = 1.0, jax.random.fold_in(rng, 6)
    for dim, blocks in cuts:
        draws = jnp.exp(jax.random.uniform(jax.random.fold_in(own, dim), (blocks,), jnp.float32, least / len(cuts), largest / len(cuts)))
        gain = gain * jnp.repeat(draws, extent[dim] // blocks).reshape([-1 if axis == dim else 1 for axis in range(len(extent))])
    return gain


def normal_values(rng, dims, width, most, cuts=(), kind=jnp.bfloat16):
    values = width * jax.random.normal(rng, dims, jnp.float32)
    if cuts:
        values = values * steps_of(rng, dims, cuts, -0.22, 0.18)
    return jnp.clip(values, -most, most).astype(kind)


def setup_inputs(seed: int = 0) -> dict:
    seeds = jax.random.split(jax.random.key(seed), 18)
    images = normal_values(seeds[0], (IMAGES, GRID, GRID, D), 1.0, 6.0, ((0, 16), (1, 2)))
    cotangent = normal_values(seeds[1], (IMAGES, GRID, GRID, D), 1.0, 6.0, ((0, 16), (1, 2)))
    present = place_ends((jax.random.randint(seeds[2], (IMAGES,), 0, 8) < 7).astype(jnp.int32), jax.random.fold_in(seeds[2], 1), 0, 1)
    threshold = jnp.clip(jnp.exp(jax.random.uniform(seeds[3], (HEADS,), jnp.float32, math.log(3.0), math.log(12.0))), 3.0, 12.0)
    inner_weight = normal_values(seeds[4], (D, 3 * D), (D // 2) ** -0.5, 0.3125, ((0, 4),))
    inner_bias = normal_values(seeds[5], (2 * D,), 0.5, 3.0, ((0, 4),))
    outer_weight = normal_values(seeds[6], (D, D), (D // 8) ** -0.5, 0.625, ((0, 4),))
    outer_bias = normal_values(seeds[7], (D,), 0.3, 2.0, ((0, 4),))
    expand_weight = normal_values(seeds[8], (D, FF), D ** -0.5, 0.21875, ((0, 4),))
    expand_bias = normal_values(seeds[9], (FF,), 0.3, 2.0, ((0, 4),))
    reduce_weight = normal_values(seeds[10], (FF, D), (FF // 2) ** -0.5, 0.15625, ((0, 4),))
    reduce_bias = normal_values(seeds[11], (D,), 0.3, 2.0, ((0, 4),))
    first_gain = jnp.clip(1.0 + 0.1 * jax.random.normal(seeds[12], (D,), jnp.float32), 0.5, 1.5).astype(jnp.bfloat16)
    first_shift = normal_values(seeds[13], (D,), 0.3, 2.0, ((0, 4),))
    second_gain = jnp.clip(1.0 + 0.1 * jax.random.normal(seeds[14], (D,), jnp.float32), 0.5, 1.5).astype(jnp.bfloat16)
    second_shift = normal_values(seeds[15], (D,), 0.3, 2.0, ((0, 4),))
    bias_table = normal_values(seeds[16], (TABLE, HEADS), 1.0, 4.0)
    return {"images": images, "cotangent": cotangent, "present": present, "threshold": threshold, "inner_weight": inner_weight, "inner_bias": inner_bias, "outer_weight": outer_weight, "outer_bias": outer_bias, "expand_weight": expand_weight, "expand_bias": expand_bias, "reduce_weight": reduce_weight, "reduce_bias": reduce_bias, "first_gain": first_gain, "first_shift": first_shift, "second_gain": second_gain, "second_shift": second_shift, "bias_table": bias_table}


@jax.custom_vjp
def low(v):
    return lax.optimization_barrier(v.astype(jnp.bfloat16)).astype(jnp.float32)

@jax.custom_vjp
def low_back(v):
    return v

def low_keep(v):
    return (low(v), None)

def low_pass(kept, grad):
    return (grad,)

def back_keep(v):
    return (v, None)

def back_low(kept, grad):
    return (low(grad),)
low.defvjp(low_keep, low_pass)
low_back.defvjp(back_keep, back_low)
EPSILON = 1e-05
MASKED = -100.0
NEGATIVE = -1e+30
PRECISE = lax.Precision.HIGHEST

def matmul(left_side, right_side):
    return jnp.dot(left_side, right_side, precision=PRECISE, preferred_element_type=jnp.float32)

def layer_norm(rows_in, gain_row, shifts):
    centre = rows_in - lax.optimization_barrier(jnp.mean(rows_in, axis=-1, keepdims=True))
    spread_sq = lax.optimization_barrier(jnp.mean(centre * centre, axis=-1, keepdims=True))
    return centre * lax.rsqrt(spread_sq + EPSILON) * gain_row + shifts

def window_tables():
    across = GRID // WIN
    cells = jnp.arange(WIN * WIN, dtype=jnp.int32)
    row_of = cells // WIN
    col_of = cells % WIN
    offsets = (row_of[:, None] - row_of[None, :] + WIN - 1) * (2 * WIN - 1) + (col_of[:, None] - col_of[None, :] + WIN - 1)
    line_index = jnp.arange(GRID, dtype=jnp.int32)
    region = (line_index >= GRID - WIN).astype(jnp.int32) + (line_index >= GRID - SHIFT).astype(jnp.int32)
    labels = 3 * region[:, None] + region[None, :]
    labels = labels.reshape(across, WIN, across, WIN).transpose(0, 2, 1, 3).reshape(across * across, WIN * WIN)
    region_masks = jnp.where(labels[:, :, None] != labels[:, None, :], MASKED, 0.0).astype(jnp.float32)
    return (offsets, region_masks)

def forward(params, images_now, present_now):
    inner_weight, inner_bias, outer_weight, outer_bias, expand_weight, expand_bias, reduce_weight, reduce_bias, first_gain, first_shift, second_gain, second_shift, bias_table = params
    amount = images_now.shape[0]
    across = GRID // WIN
    offsets, region_masks = window_tables()
    rolled = jnp.roll(images_now, (-SHIFT, -SHIFT), (1, 2))
    tokens = rolled.reshape(amount, across, WIN, across, WIN, D).transpose(0, 1, 3, 2, 4, 5).reshape(-1, D)
    normed = low(layer_norm(tokens, first_gain, first_shift))
    bias_in = jnp.concatenate([inner_bias[:D], jnp.zeros((D,), jnp.float32), inner_bias[D:]])
    projected = low(low_back(matmul(normed, inner_weight) + bias_in))
    windows = amount * across * across
    projected = projected.reshape(windows, WIN * WIN, 3, HEADS, HEAD_DIM)
    queries = projected[:, :, 0]
    key_rows = projected[:, :, 1]
    values = projected[:, :, 2]
    logits = jnp.einsum('wqhd,wkhd->whqk', queries, key_rows, precision=PRECISE) * HEAD_DIM ** (-0.5)
    alive_windows = jnp.repeat(present_now > 0, across * across)
    peak_now = lax.optimization_barrier(jnp.max(jnp.where(alive_windows[:, None, None, None], logits, NEGATIVE), axis=(0, 2, 3)))
    bias_heads = bias_table[offsets].transpose(2, 0, 1)
    masks_all = jnp.tile(region_masks, (amount, 1, 1))
    scores = low_back(logits + bias_heads[None] + masks_all[:, None])
    weights = jax.nn.softmax(scores, axis=-1)
    mixed_out = jnp.einsum('whqk,wkhd->wqhd', low(weights), values, precision=PRECISE).reshape(-1, D)
    mixed_out = low(low_back(mixed_out))
    branch = low_back(matmul(mixed_out, outer_weight) + outer_bias)
    middle = tokens + branch
    second_normed = low(layer_norm(middle, second_gain, second_shift))
    hidden = low_back(matmul(second_normed, expand_weight) + expand_bias)
    active = low(jax.nn.gelu(hidden, approximate=False))
    last_branch = low_back(matmul(active, reduce_weight) + reduce_bias)
    result = (middle + last_branch).reshape(amount, across, across, WIN, WIN, D)
    result = result.transpose(0, 1, 3, 2, 4, 5).reshape(amount, GRID, GRID, D)
    return (jnp.roll(result, (SHIFT, SHIFT), (1, 2)), peak_now)

def reference(images, cotangent, present, threshold, inner_weight, inner_bias, outer_weight, outer_bias, expand_weight, expand_bias, reduce_weight, reduce_bias, first_gain, first_shift, second_gain, second_shift, bias_table):
    params = (inner_weight.astype(jnp.float32), inner_bias.astype(jnp.float32), outer_weight.astype(jnp.float32), outer_bias.astype(jnp.float32), expand_weight.astype(jnp.float32), expand_bias.astype(jnp.float32), reduce_weight.astype(jnp.float32), reduce_bias.astype(jnp.float32), first_gain.astype(jnp.float32), first_shift.astype(jnp.float32), second_gain.astype(jnp.float32), second_shift.astype(jnp.float32), bias_table.astype(jnp.float32))
    per_group = 4
    groups = IMAGES // per_group

    def accumulate(carried, pieces):
        totals, peak_so_far = carried
        images_now, grad_now, present_now = pieces

        def runner(param_tuple, images_in):
            return forward(param_tuple, images_in, present_now)
        result, pullback, peak_now = jax.vjp(runner, params, images_now.astype(jnp.float32), has_aux=True)
        weight_now = present_now.astype(jnp.float32)[:, None, None, None]
        gradients, grad_in = pullback(grad_now.astype(jnp.float32) * weight_now)
        totals = jax.tree.map(jnp.add, totals, gradients)
        return ((totals, jnp.maximum(peak_so_far, peak_now)), (result.astype(jnp.bfloat16), grad_in.astype(jnp.bfloat16)))
    zeroes = jax.tree.map(jnp.zeros_like, params)
    initial = jnp.full((HEADS,), NEGATIVE, dtype=jnp.float32)
    (totals, maxima), (outputs, grad_inputs) = lax.scan(accumulate, (zeroes, initial), (images.reshape(groups, per_group, GRID, GRID, D), cotangent.reshape(groups, per_group, GRID, GRID, D), present.reshape(groups, per_group)))
    block_out = outputs.reshape(IMAGES, GRID, GRID, D)
    grad_images = grad_inputs.reshape(IMAGES, GRID, GRID, D)
    factors = threshold / jnp.maximum(maxima, threshold)
    root_factor = jnp.sqrt(factors)
    column_scale = jnp.concatenate([jnp.repeat(root_factor, HEAD_DIM), jnp.repeat(root_factor, HEAD_DIM), jnp.ones((D,), jnp.float32)])
    clipped_inner = (inner_weight.astype(jnp.float32) * column_scale[None, :]).astype(jnp.bfloat16)
    return (block_out, grad_images, totals[0], totals[1], totals[2], totals[3], totals[4], totals[5], totals[6], totals[7], totals[8], totals[9], totals[10], totals[11], totals[12], clipped_inner, factors, maxima)
```

```python
import functools
import math

import numpy as np
import jax
import jax.numpy as jnp
from jax import lax
from jax.experimental import pallas as pl
from jax.experimental.pallas import tpu as pltpu
from jax.sharding import PartitionSpec as P

D = 768
HEADS = 24
HD = 32
WIN = 12
GRID = 24
SHIFT = 6
FF = 3072
TOK = WIN * WIN
ROWS = WIN * GRID
SPAN = 2 * WIN - 1
EPS = 1e-5
MASKED = -100.0
NEGATIVE = -1e30
LOG2E = math.log2(math.e)
BF = jnp.bfloat16
F32 = jnp.float32
MB = 1 << 20
OWN = 192
CH = 384
WIDE = 640
NARROW = 384
TALL = WIN * 16
HB = 4
LB = HB * HD
NB = 384
ONE = dict(pipeline_mode=pl.Buffered(1))
SD = jax.ShapeDtypeStruct


def nn(a, b):
    return lax.dot_general(a, b, (((1,), (0,)), ((), ())), preferred_element_type=F32)


def nt(a, b):
    return lax.dot_general(a, b, (((1,), (1,)), ((), ())), preferred_element_type=F32)


def tn(a, b):
    return lax.dot_general(a, b, (((0,), (0,)), ((), ())), preferred_element_type=F32)


def full(shape, **kw):
    return pl.BlockSpec(shape, lambda *_: (0,) * len(shape), **kw)


def any_space():
    return pl.BlockSpec(memory_space=pl.ANY)


def smem():
    return pl.BlockSpec(memory_space=pltpu.SMEM)


def params(limit=60):
    return pltpu.CompilerParams(vmem_limit_bytes=limit * MB)


def cost(flops, moved, exps=0):
    return pl.CostEstimate(flops=int(flops), bytes_accessed=int(moved), transcendentals=int(exps))


def colsum(v):
    return jnp.sum(v, axis=0, keepdims=True)


def norm_parts(x):
    c = x - jnp.mean(x, axis=-1, keepdims=True)
    r = lax.rsqrt(jnp.mean(c * c, axis=-1, keepdims=True) + EPS)
    return c * r, r


def row_order():
    cells = np.arange(ROWS)
    win, rest = cells // TOK, cells % TOK
    a, b = rest // WIN, rest % WIN
    m = np.zeros((ROWS, ROWS), np.float32)
    m[cells, a * GRID + (win * WIN + b + SHIFT) % GRID] = 1
    return m


def spread_q(reverse):
    q = np.arange(TOK)
    s = SPAN * (q // WIN) + q % WIN
    if reverse:
        s = SPAN * (WIN - 1) + WIN - 1 - s
    m = np.zeros((TOK, NARROW), np.float32)
    m[q, s] = 1
    return m


def spread_k():
    k = np.arange(TOK)
    m = np.zeros((TALL, TOK), np.float32)
    m[16 * (k // WIN) + k % WIN, k] = 1
    return m


def start_pieces(refs, at, target, sems):
    for i, ref in enumerate(refs):
        rows = pl.ds(pl.multiple_of(at[i], 16), ref.shape[0])
        pltpu.make_async_copy(ref, target.at[rows, :], sems.at[i]).start()


def wait_pieces(refs, at, target, sems):
    for i, ref in enumerate(refs):
        rows = pl.ds(pl.multiple_of(at[i], 16), ref.shape[0])
        pltpu.make_async_copy(ref, target.at[rows, :], sems.at[i]).wait()


def bias_kernel(table_ref, mask_ref, sq_ref, sk_ref, out_ref, tall):
    for h in range(HEADS):
        row = pltpu.roll(jnp.broadcast_to(table_ref[h : h + 1, :], (16, WIDE)), 0, 1, stride=1, stride_axis=0)
        for a in range(WIN):
            off = (SPAN * a - SPAN * (WIN - 1) - (WIN - 1)) % WIDE
            tall[16 * a : 16 * a + 16, :] = pltpu.roll(row, off, 1)[:, :NARROW].astype(BF)
        wide = nn(tall[...], sq_ref[...]).astype(BF)
        bias = nn(sk_ref[...], wide)
        for w in range(2):
            out_ref[w, h] = (bias + mask_ref[w]) * LOG2E


def bias_call(table, half):
    t = jnp.pad(table.astype(F32).T, ((0, 0), (0, WIDE - table.shape[0])))
    line = jnp.arange(WIN, dtype=jnp.int32) + half * WIN
    row = (line >= GRID - WIN).astype(jnp.int32) + (line >= GRID - SHIFT).astype(jnp.int32)
    col = np.arange(GRID)
    col = (col >= GRID - WIN).astype(np.int32) + (col >= GRID - SHIFT).astype(np.int32)
    lab = 3 * row[:, None] + jnp.asarray(col)[None, :]
    lab = lab.reshape(WIN, 2, WIN).transpose(1, 0, 2).reshape(2, TOK)
    mask = jnp.where(lab[:, :, None] != lab[:, None, :], MASKED, 0.0).astype(F32)
    return pl.pallas_call(
        bias_kernel,
        out_shape=SD((2, HEADS, TOK, TOK), F32),
        scratch_shapes=[pltpu.VMEM((TALL, NARROW), BF)],
        compiler_params=params(40),
        cost_estimate=cost(4e9, 8 * MB),
        name="bias",
    )(t, mask, jnp.asarray(spread_q(False).T, BF), jnp.asarray(spread_k().T, BF))


def table_kernel(db_ref, sq_ref, sk_ref, out_ref):
    def split(v):
        hi = v.astype(BF)
        return hi, (v - hi.astype(F32)).astype(BF)

    for h in range(HEADS):
        hi, lo = split(db_ref[h])
        tall = nn(sk_ref[...], hi) + nn(sk_ref[...], lo)
        hi, lo = split(tall)
        wide = nn(hi, sq_ref[...]) + nn(lo, sq_ref[...])
        wide = jnp.concatenate([wide, jnp.zeros((TALL, WIDE - NARROW), F32)], axis=1)
        tot = jnp.zeros((16, WIDE), F32)
        for a in range(WIN):
            tot = tot + pltpu.roll(wide[16 * a : 16 * a + 16, :], SPAN * a, 1)
        tot = pltpu.roll(tot, 0, 1, stride=1, stride_axis=0)
        out_ref[h : h + 1, :] = colsum(tot)


def table_call(db):
    return pl.pallas_call(
        table_kernel,
        out_shape=SD((HEADS, WIDE), F32),
        compiler_params=params(40),
        cost_estimate=cost(4e9, 4 * MB),
        name="table",
    )(db, jnp.asarray(spread_q(True), BF), jnp.asarray(spread_k(), BF))


def lane_head(shape):
    return lax.broadcasted_iota(jnp.int32, shape, len(shape) - 1) // HD


def attend_kernel(np_, own_ref, recv_ref, pm_ref, gain_ref, shift_ref, b_ref, bm_ref, at_ref, *rest):
    pieces = rest[:np_]
    tok_ref, n1_ref, proj_ref, pt_ref, att_ref, peak_ref, w_ref, sems = rest[np_:]

    @pl.when(pl.program_id(0) == 0)
    def _():
        start_pieces(pieces, at_ref, w_ref, sems)

    x = jnp.concatenate([own_ref[0, TOK:, :], recv_ref[0]], axis=0)
    tok = nn(pm_ref[...], x)
    tok_ref[0] = tok.astype(BF)
    xh, _ = norm_parts(tok)
    n1_ref[0] = (xh * gain_ref[...] + shift_ref[...]).astype(BF)

    @pl.when(pl.program_id(0) == 0)
    def _():
        wait_pieces(pieces, at_ref, w_ref, sems)

    n1 = n1_ref[0]
    for c in range(0, 3 * D, D):
        proj_ref[0, :, c : c + D] = (nn(n1, w_ref[:, c : c + D]) + b_ref[:, c : c + D]).astype(BF)
    hid = lane_head((TOK, LB))
    scale = HD**-0.5
    for w in range(2):
        r = slice(w * TOK, (w + 1) * TOK)
        for blk in range(D // LB):
            l = blk * LB
            q = proj_ref[0, r, l : l + LB]
            k = proj_ref[0, r, D + l : D + l + LB]
            v = proj_ref[0, r, 2 * D + l : 2 * D + l + LB]
            vt = v.T
            outs = []
            for h in range(HB):
                hh = blk * HB + h
                km = jnp.where(hid == h, k, jnp.zeros_like(k))
                st = nt(km, q)
                peak_ref[0, w, hh : hh + 1, :] = jnp.max(st, axis=0, keepdims=True) * scale
                t = st * (scale * LOG2E) + bm_ref[w, hh]
                e = jnp.exp2(t - jnp.max(t, axis=0, keepdims=True))
                p = (e * (1.0 / colsum(e))).astype(BF)
                pt_ref[0, w, hh] = p
                outs.append(nn(vt[HD * h : HD * h + HD, :], p))
            att_ref[0, r, l : l + LB] = jnp.concatenate(outs, axis=0).astype(BF).T


def attend_call(own, recv, pm, gain, shift, b, bm, at, pieces):
    n = own.shape[0]

    def blk(*s):
        return pl.BlockSpec((1,) + s, lambda i: (i,) + (0,) * len(s))

    return pl.pallas_call(
        functools.partial(attend_kernel, len(pieces)),
        grid=(n,),
        in_specs=[blk(ROWS, D), blk(TOK, D), full((ROWS, ROWS)), full((1, D)), full((1, D)), full((1, 3 * D)),
                  full((2, HEADS, TOK, TOK), **ONE), smem()] + [any_space()] * len(pieces),
        out_specs=[blk(ROWS, D), blk(ROWS, D), blk(ROWS, 3 * D), blk(2, HEADS, TOK, TOK), blk(ROWS, D), blk(2, HEADS, TOK)],
        out_shape=[SD((n, ROWS, D), BF), SD((n, ROWS, D), BF), SD((n, ROWS, 3 * D), BF),
                   SD((n, 2, HEADS, TOK, TOK), BF), SD((n, ROWS, D), BF), SD((n, 2, HEADS, TOK), F32)],
        scratch_shapes=[pltpu.VMEM((D, 3 * D), BF), pltpu.SemaphoreType.DMA((len(pieces),))],
        compiler_params=params(),
        cost_estimate=cost(4e10, 30 * MB, 4e6),
        name="attend",
    )(own, recv, pm, gain, shift, b, bm, at, *pieces)


def gelu_parts(h):
    d = 1.0 + (0.3275911 * 0.5**0.5) * jnp.abs(h)
    t = pl.reciprocal(d, approx=True)
    t = t * (2.0 - d * t)
    e = jnp.exp2(h * h * (-0.5 * LOG2E))
    p = (((0.5 * 1.061405429) * t - 0.5 * 1.453152027) * t + 0.5 * 1.421413741) * t - 0.5 * 0.284496736
    p = (p * t + 0.5 * 0.254829592) * t * e
    cdf = jnp.where(h >= 0, 1.0 - p, p)
    return cdf, cdf + h * (e * ((2 * math.pi) ** -0.5))


def middle_kernel(na, nb_, spot_ref, tok_ref, att_ref, gown_ref, grecv_ref, alive_ref, pm_ref, pmt_ref, ob_ref, gain_ref,
                  shift_ref, rb_ref, eb_ref, ata_ref, atb_ref, *rest):
    pa, pb = rest[:na], rest[na : na + nb_]
    (stay_ref, send_ref, gmid_ref, datt_ref, os_ref, ok_ref, es_ref, ek_ref, rs_ref, rk_ref, geb_ref, small_ref,
     wa, wb, mid, n2, g, n2t, acc, e2, act, gh, sema, semb) = rest[na + nb_ :]
    j = pl.program_id(0)
    n = tok_ref.shape[0]
    N = n * ROWS
    me = spot_ref[0]
    core = spot_ref[1]

    @pl.when(j == 0)
    def _():
        start_pieces(pa, ata_ref, wa, sema)
        start_pieces(pb, atb_ref, wb, semb)
        tot = jnp.zeros((1, D), F32)
        for i in range(n):
            s = slice(i * ROWS, (i + 1) * ROWS)
            x = jnp.concatenate([gown_ref[i, TOK:, :], grecv_ref[i]], axis=0)
            gi = nn(pm_ref[...], x) * alive_ref[0:1, i : i + 1]
            tot = tot + colsum(gi)
            g[s, :] = gi.astype(BF)
        small_ref[0:1, :] = tot
        wait_pieces(pa, ata_ref, wa, sema)
        for i in range(n):
            s = slice(i * ROWS, (i + 1) * ROWS)
            m = tok_ref[i].astype(F32) + nn(att_ref[i], wa[:, :D]) + ob_ref[...]
            mid[s, :] = m
            xh, _ = norm_parts(m)
            x2 = (xh * gain_ref[...] + shift_ref[...]).astype(BF)
            n2[s, :] = x2
            n2t[:, s] = x2.T
            acc[s, :] = m + rb_ref[...]
            e2[s, :] = jnp.zeros((ROWS, D), F32)
        wait_pieces(pb, atb_ref, wb, semb)

    sh = jnp.bitwise_xor(me, j % 4)
    at = (2 * sh + jnp.bitwise_xor(core, 1 - j // 4)) * CH
    ecol = pl.ds(pl.multiple_of(D + at, 128), CH)
    rrow = pl.ds(pl.multiple_of(at, CH), CH)
    tot = jnp.zeros((1, CH), F32)
    for s0 in range(0, N, NB):
        s = slice(s0, s0 + NB)
        h = nn(n2[s, :], wa[:, ecol]) + eb_ref[0]
        cdf, dg = gelu_parts(h)
        act[s, :] = (h * cdf).astype(BF)
        x = (nt(g[s, :], wb[rrow, :]) * dg).astype(BF)
        gh[s, :] = x
        tot = tot + colsum(x.astype(F32))
    geb_ref[0] = tot
    ge = nn(n2t[...], gh[...]).astype(BF)
    gr = tn(act[...], g[...]).astype(BF)

    def put(e_ref, r_ref):
        for b in range(4):
            e_ref[jnp.bitwise_xor(me, b), 0] = ge[b * OWN : (b + 1) * OWN, :]
            r_ref[0, b] = gr[(b // 2) * OWN : (b // 2 + 1) * OWN, (b % 2) * CH : (b % 2 + 1) * CH]

    @pl.when(j < 4)
    def _():
        put(es_ref, rs_ref)

    @pl.when(j >= 4)
    def _():
        put(ek_ref, rk_ref)

    for s0 in range(0, N, NB):
        s = slice(s0, s0 + NB)
        acc[s, :] += nn(act[s, :], wb[rrow, :])
        e2[s, :] += nt(gh[s, :], wa[:, ecol])

    @pl.when(j == 7)
    def _():
        gn = jnp.zeros((1, D), F32)
        shf = gn
        ob = gn
        for i in range(n):
            s = slice(i * ROWS, (i + 1) * ROWS)
            o = nn(pmt_ref[...], acc[s, :].astype(BF)).astype(BF)
            stay_ref[i] = o[:TOK]
            send_ref[i] = o[TOK:]
            xh, r = norm_parts(mid[s, :])
            d = e2[s, :]
            gn = gn + colsum(d * xh)
            shf = shf + colsum(d)
            d = d * gain_ref[...]
            gm = g[s, :].astype(F32) + r * (
                d - jnp.mean(d, axis=-1, keepdims=True) - xh * jnp.mean(d * xh, axis=-1, keepdims=True)
            )
            gmid_ref[i] = gm
            gb = gm.astype(BF)
            ob = ob + colsum(gb.astype(F32))
            g[s, :] = gb
            datt_ref[i] = nt(gb, wa[:, :D]).astype(BF)
            n2[s, :] = att_ref[i]
        for c, ref in ((1 - core, os_ref), (core, ok_ref)):
            go = tn(n2[...], g[:, pl.ds(pl.multiple_of(c * CH, 128), CH)]).astype(BF)
            for b in range(4):
                ref[jnp.bitwise_xor(me, b), 0] = go[b * OWN : (b + 1) * OWN, :]
        small_ref[1:2, :] = gn
        small_ref[2:3, :] = shf
        small_ref[3:4, :] = ob
        small_ref[4:8, :] = jnp.zeros((4, D), F32)


def middle_call(spot, tok, att, gown, grecv, alive, pm, pmt, ob, gain, shift, rb, eb, ata, pa, atb, pb):
    n = tok.shape[0]
    N = n * ROWS
    blocks = SD((4, 4, OWN, CH), BF)

    def chunk(j, spot):
        return 2 * jnp.bitwise_xor(spot[0], j % 4) + jnp.bitwise_xor(spot[1], 1 - j // 4)

    def early(j, spot):
        return jnp.bitwise_xor(spot[0], jnp.minimum(j, 3))

    def late(j, spot):
        return jnp.bitwise_xor(spot[0], jnp.maximum(j, 4) - 4)

    grid_spec = pltpu.PrefetchScalarGridSpec(
        num_scalar_prefetch=1,
        grid=(8,),
        in_specs=[full((n, ROWS, D), **ONE), full((n, ROWS, D), **ONE), full((n, ROWS, D), **ONE), full((n, TOK, D), **ONE),
                  full((1, n)), full((ROWS, ROWS)), full((ROWS, ROWS)), full((1, D)), full((1, D)), full((1, D)), full((1, D)),
                  pl.BlockSpec((1, 1, CH), lambda j, spot: (chunk(j, spot), 0, 0)), smem(), smem()]
        + [any_space()] * (len(pa) + len(pb)),
        out_specs=[full((n, TOK, D), **ONE), full((n, TOK, D), **ONE), full((n, ROWS, D), **ONE), full((n, ROWS, D), **ONE),
                   full((4, 1, OWN, CH), **ONE), full((4, 1, OWN, CH), **ONE),
                   pl.BlockSpec((4, 1, OWN, CH), lambda j, spot: (0, early(j, spot), 0, 0)),
                   pl.BlockSpec((4, 1, OWN, CH), lambda j, spot: (0, late(j, spot), 0, 0)),
                   pl.BlockSpec((1, 4, OWN, CH), lambda j, spot: (jnp.minimum(j, 3), 0, 0, 0)),
                   pl.BlockSpec((1, 4, OWN, CH), lambda j, spot: (jnp.maximum(j, 4) - 4, 0, 0, 0)),
                   pl.BlockSpec((1, 1, CH), lambda j, spot: (chunk(j, spot), 0, 0)), full((8, D))],
        scratch_shapes=[pltpu.VMEM((D, D + FF), BF), pltpu.VMEM((FF, D), BF),
                        pltpu.VMEM((N, D), F32), pltpu.VMEM((N, D), BF), pltpu.VMEM((N, D), BF), pltpu.VMEM((D, N), BF),
                        pltpu.VMEM((N, D), F32), pltpu.VMEM((N, D), F32), pltpu.VMEM((N, CH), BF), pltpu.VMEM((N, CH), BF),
                        pltpu.SemaphoreType.DMA((len(pa),)), pltpu.SemaphoreType.DMA((len(pb),))],
    )
    return pl.pallas_call(
        functools.partial(middle_kernel, len(pa), len(pb)),
        grid_spec=grid_spec,
        out_shape=[SD((n, TOK, D), BF), SD((n, TOK, D), BF), SD((n, ROWS, D), F32), SD((n, ROWS, D), BF),
                   SD((4, 1, OWN, CH), BF), SD((4, 1, OWN, CH), BF), blocks, blocks, blocks, blocks,
                   SD((8, 1, CH), F32), SD((8, D), F32)],
        compiler_params=params(62),
        cost_estimate=cost(6e10, 40 * MB, 7e6),
        name="middle",
    )(spot, tok, att, gown, grecv, alive, pm, pmt, ob, gain, shift, rb, eb, ata, atb, *pa, *pb)


def back_kernel(proj_ref, pt_ref, da_ref, gp_ref, db_ref):
    @pl.when(pl.program_id(0) == 0)
    def _():
        db_ref[...] = jnp.zeros_like(db_ref)

    hid = lane_head((TOK, LB))
    scale = HD**-0.5
    for w in range(2):
        r = slice(w * TOK, (w + 1) * TOK)
        for blk in range(D // LB):
            l = blk * LB
            q = proj_ref[0, r, l : l + LB]
            k = proj_ref[0, r, D + l : D + l + LB]
            v = proj_ref[0, r, 2 * D + l : 2 * D + l + LB]
            do = da_ref[0, r, l : l + LB]
            qt, kt, dt = q.T, k.T, do.T
            dq, dk, dv = [], [], []
            for h in range(HB):
                hh = blk * HB + h
                s = slice(HD * h, HD * h + HD)
                dp = nt(jnp.where(hid == h, v, jnp.zeros_like(v)), do)
                pb = pt_ref[0, w, hh]
                p = pb.astype(F32)
                pd = p * dp
                ds = pd - p * colsum(pd)
                db_ref[hh] += ds
                dsb = ds.astype(BF)
                dq.append(nn(kt[s, :], dsb))
                dk.append(nt(qt[s, :], dsb))
                dv.append(nt(dt[s, :], pb))
            gp_ref[0, r, l : l + LB] = (jnp.concatenate(dq, axis=0) * scale).astype(BF).T
            gp_ref[0, r, D + l : D + l + LB] = (jnp.concatenate(dk, axis=0) * scale).astype(BF).T
            gp_ref[0, r, 2 * D + l : 2 * D + l + LB] = jnp.concatenate(dv, axis=0).astype(BF).T


def back_call(proj, pt, da):
    n = proj.shape[0]

    def blk(*s):
        return pl.BlockSpec((1,) + s, lambda i: (i,) + (0,) * len(s))

    return pl.pallas_call(
        back_kernel,
        grid=(n,),
        in_specs=[blk(ROWS, 3 * D), blk(2, HEADS, TOK, TOK), blk(ROWS, D)],
        out_specs=[blk(ROWS, 3 * D), full((HEADS, TOK, TOK))],
        out_shape=[SD((n, ROWS, 3 * D), BF), SD((HEADS, TOK, TOK), F32)],
        compiler_params=params(),
        cost_estimate=cost(5e10, 30 * MB),
        name="attend_back",
    )(proj, pt, da)


def inner_kernel(spot_ref, n1_ref, gp_ref, is_ref, ik_ref, gb_ref):
    me = spot_ref[0]
    core = spot_ref[1]
    n = n1_ref.shape[0]
    gp = gp_ref[...].reshape(n * ROWS, D)
    gb_ref[0] = colsum(gp.astype(F32))
    gi = tn(n1_ref[...].reshape(n * ROWS, D), gp).astype(BF)

    for c in range(2):
        @pl.when(core == c)
        def _():
            for b in range(4):
                r = slice(b * OWN, (b + 1) * OWN)
                ik_ref[jnp.bitwise_xor(me, b), 0] = gi[r, c * CH : (c + 1) * CH]
                is_ref[jnp.bitwise_xor(me, b), 0] = gi[r, (1 - c) * CH : (2 - c) * CH]


def inner_call(spot, n1, gp):
    n = n1.shape[0]
    out = pl.BlockSpec((4, 1, OWN, CH), lambda j: (0, j, 0, 0))
    return pl.pallas_call(
        inner_kernel,
        grid=(3,),
        in_specs=[smem(), full((n, ROWS, D), **ONE), pl.BlockSpec((n, ROWS, D), lambda j: (0, 0, j))],
        out_specs=[out, out, pl.BlockSpec((1, 1, D), lambda j: (j, 0, 0))],
        out_shape=[SD((4, 3, OWN, CH), BF), SD((4, 3, OWN, CH), BF), SD((3, 1, D), F32)],
        compiler_params=params(),
        cost_estimate=cost(8e9, 15 * MB),
        name="inner_grad",
    )(spot, n1, gp)


def last_kernel(np_, tok_ref, gp_ref, gmid_ref, gain_ref, pmt_ref, at_ref, *rest):
    pieces = rest[:np_]
    small_ref, stay_ref, send_ref, w_ref, sems = rest[np_:]
    i = pl.program_id(0)

    @pl.when(i == 0)
    def _():
        start_pieces(pieces, at_ref, w_ref, sems)
        wait_pieces(pieces, at_ref, w_ref, sems)
        small_ref[...] = jnp.zeros_like(small_ref)

    d = nt(gp_ref[0], w_ref[...])
    xh, r = norm_parts(tok_ref[0].astype(F32))
    small_ref[0:1, :] += colsum(d * xh)
    small_ref[1:2, :] += colsum(d)
    d = d * gain_ref[...]
    gm = gmid_ref[0] + r * (d - jnp.mean(d, axis=-1, keepdims=True) - xh * jnp.mean(d * xh, axis=-1, keepdims=True))
    o = nn(pmt_ref[...], gm.astype(BF)).astype(BF)
    stay_ref[0] = o[:TOK]
    send_ref[0] = o[TOK:]


def last_call(tok, gp, gmid, gain, pmt, at, pieces):
    n = tok.shape[0]

    def blk(*s):
        return pl.BlockSpec((1,) + s, lambda i: (i,) + (0,) * len(s))

    return pl.pallas_call(
        functools.partial(last_kernel, len(pieces)),
        grid=(n,),
        in_specs=[blk(ROWS, D), blk(ROWS, 3 * D), blk(ROWS, D), full((1, D)), full((ROWS, ROWS)), smem()]
        + [any_space()] * len(pieces),
        out_specs=[full((8, D)), blk(TOK, D), blk(TOK, D)],
        out_shape=[SD((8, D), F32), SD((n, TOK, D), BF), SD((n, TOK, D), BF)],
        scratch_shapes=[pltpu.VMEM((D, 3 * D), BF), pltpu.SemaphoreType.DMA((len(pieces),))],
        compiler_params=params(),
        cost_estimate=cost(1e10, 20 * MB),
        name="last",
    )(tok, gp, gmid, gain, pmt, at, *pieces)


def swap(block, axis, bit):
    count = lax.axis_size(axis)
    return lax.ppermute(block, axis, [(i, i ^ bit) for i in range(count) if i ^ bit < count])


def everywhere(value, op):
    for axis in ("half", "shard", "replica"):
        bit = 1
        while bit < lax.axis_size(axis):
            value = op(value, swap(value, axis, bit))
            bit *= 2
    return value


def gather_rows(own, me, core):
    rows = own.shape[0]
    mine = lax.dynamic_slice_in_dim(own, core * (rows // 2), rows // 2, 0)
    by_x = swap(mine, "shard", 1)
    by_y = swap(mine, "shard", 2)
    far_a = swap(by_x[: rows // 4], "shard", 2)
    far_b = swap(by_y[rows // 4 :], "shard", 1)
    got = [by_x, by_y, far_a, far_b]
    other = [swap(v, "half", 1) for v in got]
    at = [me * rows]
    for c in (core, 1 - core):
        base = c * (rows // 2)
        at += [(me ^ 1) * rows + base, (me ^ 2) * rows + base, (me ^ 3) * rows + base, (me ^ 3) * rows + base + rows // 4]
    return [own] + got + other, jnp.stack(at).astype(jnp.int32)


def add(a, b):
    return (a.astype(F32) + b.astype(F32)).astype(BF)


def reduce_blocks(send, keep, replica):
    hlf = OWN // 2
    t = add(keep, swap(send, "half", 1))
    tx = jnp.stack([t[1, :, :hlf], t[3, :, :hlf]])
    ty = jnp.stack([t[2, :, hlf:], t[3, :, hlf:]])
    a = add(jnp.stack([t[0, :, :hlf], t[2, :, :hlf]]), swap(tx, "shard", 1))
    b = add(jnp.stack([t[0, :, hlf:], t[1, :, hlf:]]), swap(ty, "shard", 2))
    z0 = add(a[0], swap(a[1], "shard", 2))
    z1 = add(b[0], swap(b[1], "shard", 1))
    low = (replica & 1) == 0
    u = add(jnp.where(low, z0, z1), swap(jnp.where(low, z1, z0), "replica", 1))
    q = hlf // 2
    low2 = (replica & 2) == 0
    v = add(jnp.where(low2, u[:, :q], u[:, q:]), swap(jnp.where(low2, u[:, q:], u[:, :q]), "replica", 2))
    w = swap(v, "replica", 2)
    u = jnp.concatenate([jnp.where(low2, v, w), jnp.where(low2, w, v)], axis=1)
    w = swap(u, "replica", 1)
    z = jnp.concatenate([jnp.where(low, u, w), jnp.where(low, w, u)], axis=1)
    return z, swap(z, "half", 1)


def shards(images, cotangent, present, threshold, inner_weight, inner_bias, outer_weight, outer_bias, expand_weight,
           expand_bias, reduce_weight, reduce_bias, first_gain, first_shift, second_gain, second_shift, bias_table):
    n = images.shape[0]
    core = lax.axis_index("half")
    shard = lax.axis_index("shard")
    replica = lax.axis_index("replica")
    shard_count = lax.axis_size("shard")
    quick = shard_count == 4 and lax.axis_size("replica") == 4
    own_images = images.reshape(n, ROWS, D)
    own_grad = cotangent.reshape(n, ROWS, D)
    upper_images = swap(own_images[:, :TOK], "half", 1)
    vectors = (inner_bias, outer_bias, expand_bias, reduce_bias, first_gain, first_shift, second_gain, second_shift)
    outer_expand = jnp.concatenate([outer_weight, expand_weight], axis=1)
    if quick:
        me = shard
        packed = jnp.concatenate(vectors).reshape(1, -1)
        near = [packed] + [swap(packed, "shard", bit) for bit in (1, 2, 3)]
        packed = jnp.concatenate([lax.dynamic_index_in_dim(jnp.stack(near), me ^ s, 0, False) for s in range(4)], axis=0)
        inner_pieces, inner_at = gather_rows(inner_weight, me, core)
        outer_pieces, outer_at = gather_rows(outer_expand, me, core)
        reduce_pieces, reduce_at = gather_rows(reduce_weight, me, core)
    else:
        me = jnp.int32(0)
        packed = lax.all_gather(jnp.concatenate(vectors), "shard", axis=0)
        zero = jnp.zeros((1,), jnp.int32)
        inner_pieces, inner_at = [lax.all_gather(inner_weight, "shard", axis=0, tiled=True)], zero
        outer_pieces, outer_at = [lax.all_gather(outer_expand, "shard", axis=0, tiled=True)], zero
        reduce_pieces, reduce_at = [lax.all_gather(reduce_weight, "shard", axis=0, tiled=True)], zero
    wide, start = [], 0
    for v in vectors:
        wide.append(packed[:, start : start + v.shape[0]].reshape(1, -1))
        start += v.shape[0]
    in_bias, out_bias, up_bias, down_bias, gain_1, shift_1, gain_2, shift_2 = (v.astype(F32) for v in wide)
    upper_grad = swap(own_grad[:, :TOK], "half", 1)
    spot = jnp.stack([me, core]).astype(jnp.int32)
    order = jnp.asarray(row_order(), BF)
    back_order = jnp.asarray(row_order().T, BF)
    bias_all = jnp.concatenate([in_bias[:, :D], jnp.zeros((1, D), F32), in_bias[:, D:]], axis=1)

    bias_masks = bias_call(bias_table, core)
    tok, n1, proj, pt, att, peak = attend_call(
        own_images, upper_images, order, gain_1, shift_1, bias_all, bias_masks, inner_at, inner_pieces
    )
    alive = present.astype(F32).reshape(1, n)
    (stay, send, gmid, datt, out_send, out_keep, e_send, e_keep, r_send, r_keep, grad_up, small) = middle_call(
        spot, tok, att, own_grad, upper_grad, alive, order, back_order, out_bias, gain_2, shift_2, down_bias,
        up_bias.reshape(8, 1, CH), outer_at, outer_pieces, reduce_at, reduce_pieces
    )
    lower_out = swap(send, "half", 1)
    gp, db = back_call(proj, pt, datt)
    table = table_call(db)
    i_send, i_keep, in_sums = inner_call(spot, n1, gp)
    small_one, gstay, gsend = last_call(tok, gp, gmid, gain_1, back_order, inner_at, inner_pieces)
    lower_grad = swap(gsend, "half", 1)

    peaks = jnp.max(jnp.where((present > 0)[:, None, None, None], peak, NEGATIVE), axis=(0, 1, 3))
    maxima = everywhere(peaks, jnp.maximum)
    sums = jnp.concatenate(
        [grad_up.reshape(-1), small[:4].reshape(-1), in_sums.reshape(-1), table.reshape(-1)]
    ).reshape(1, -1)
    sums = everywhere(sums, jnp.add).reshape(-1)
    sums_one = everywhere(small_one, jnp.add)

    def part(vec):
        size = vec.shape[0] // shard_count
        return lax.dynamic_slice_in_dim(vec, shard * size, size, 0)

    grad_up = sums[:FF]
    small = sums[FF : FF + 4 * D].reshape(4, D)
    at = FF + 4 * D
    grad_inbias = jnp.concatenate([sums[at : at + D], sums[at + 2 * D : at + 3 * D]])
    at += 3 * D
    grad_table = sums[at : at + HEADS * WIDE].reshape(HEADS, WIDE)[:, : SPAN * SPAN][:, ::-1].T

    def halves(mine, other, axis):
        lo = jnp.where(core == 0, mine, other)
        hi = jnp.where(core == 0, other, mine)
        return jnp.concatenate([lo, hi], axis=axis).astype(F32)

    if quick:
        er = reduce_blocks(jnp.concatenate([r_send, e_send, out_send], axis=1), jnp.concatenate([r_keep, e_keep, out_keep], axis=1), replica)
        ii = reduce_blocks(i_send, i_keep, replica)
        grad_reduce = halves(*(v[:4].reshape(2, 2, OWN, CH).transpose(0, 2, 1, 3).reshape(CH, D) for v in er), 0)
        grad_expand = halves(*(v[4:8].transpose(1, 0, 2)[:, :, None] for v in er), 2).reshape(OWN, FF)
        grad_outer = halves(*(v[8] for v in er), 1)
        grad_inner = halves(*(v.transpose(1, 0, 2)[:, :, None] for v in ii), 2).reshape(OWN, 3 * D)
    else:
        def whole(other, mine):
            both = halves(mine[:, :, :, None], other[:, :, :, None], 3)
            return both.transpose(0, 2, 1, 3, 4).reshape(D, -1)

        def settle(v):
            v = lax.psum_scatter(v.astype(BF), "shard", scatter_dimension=0, tiled=True)
            return lax.psum(v, ("replica", "half")).astype(F32)

        def rows_of(v):
            return v.reshape(4, 1, 2, 2, OWN, CH).transpose(0, 1, 2, 4, 3, 5).reshape(4, 1, CH, D)

        grad_reduce = settle(halves(rows_of(r_keep), rows_of(r_send), 1).reshape(FF, D))
        grad_expand = settle(whole(e_send, e_keep))
        grad_outer = settle(whole(out_send, out_keep))
        grad_inner = settle(whole(i_send, i_keep))

    factors = threshold / jnp.maximum(maxima, threshold)
    root = jnp.repeat(jnp.sqrt(factors), HD)
    column_scale = jnp.concatenate([root, root, jnp.ones((D,), F32)])
    clipped = (inner_weight.astype(F32) * column_scale[None, :]).astype(BF)
    block_out = jnp.concatenate([lower_out, stay], axis=1).reshape(images.shape)
    grad_images = jnp.concatenate([lower_grad, gstay], axis=1).reshape(images.shape)
    return (
        block_out,
        grad_images,
        grad_inner,
        part(grad_inbias),
        grad_outer,
        part(small[3]),
        grad_expand,
        part(grad_up),
        grad_reduce,
        part(small[0]),
        part(sums_one[0]),
        part(sums_one[1]),
        part(small[1]),
        part(small[2]),
        grad_table,
        clipped,
        factors,
        maxima,
    )


def solution(mesh):
    rows = P(("replica", "shard"), "half", None, None)
    cut = P("shard", None)
    line = P("shard")
    return jax.shard_map(
        shards,
        mesh=mesh,
        in_specs=(rows, rows, P(("replica", "shard")), P(), cut, line, cut, line, cut, line, cut, line, line, line, line,
                  line, P()),
        out_specs=(rows, rows, cut, line, cut, line, cut, line, cut, line, line, line, line, line, P(), cut, P(), P()),
        check_vma=False,
    )
```

```python
import functools
import math

import numpy as np
import jax
import jax.numpy as jnp
from jax import lax
from jax.experimental import pallas as pl
from jax.experimental.pallas import tpu as pltpu
from jax.sharding import PartitionSpec as P

D = 768
HEADS = 24
HD = 32
WIN = 12
GRID = 24
SHIFT = 6
FF = 3072
TOK = WIN * WIN
ROWS = WIN * GRID
SPAN = 2 * WIN - 1
EPS = 1e-5
MASKED = -100.0
NEGATIVE = -1e30
LOG2E = math.log2(math.e)
BF = jnp.bfloat16
F32 = jnp.float32
MB = 1 << 20
OWN = 192
CH = 384
WIDE = 640
NARROW = 384
TALL = WIN * 16
HB = 4
LB = HB * HD
HP = 8
LP = HP * HD
NB = 384
SCALE = 1e-3
ONE = dict(pipeline_mode=pl.Buffered(1))
SD = jax.ShapeDtypeStruct


def nn(a, b):
    return lax.dot_general(a, b, (((1,), (0,)), ((), ())), preferred_element_type=F32)


def nt(a, b):
    return lax.dot_general(a, b, (((1,), (1,)), ((), ())), preferred_element_type=F32)


def tn(a, b):
    return lax.dot_general(a, b, (((0,), (0,)), ((), ())), preferred_element_type=F32)


def full(shape, **kw):
    return pl.BlockSpec(shape, lambda *_: (0,) * len(shape), **kw)


def any_space():
    return pl.BlockSpec(memory_space=pl.ANY)


def smem():
    return pl.BlockSpec(memory_space=pltpu.SMEM)


def run(kernel, count, args, after, in_specs, **kw):
    def body(*refs):
        kernel(*refs[:count], *refs[count + len(after) :])

    return pl.pallas_call(body, in_specs=list(in_specs) + [any_space()] * len(after), **kw)(*args, *after)


def params(limit=60):
    return pltpu.CompilerParams(vmem_limit_bytes=limit * MB)


def cost(flops, moved, exps=0):
    return pl.CostEstimate(flops=int(flops * SCALE), bytes_accessed=int(moved * SCALE), transcendentals=0)


def whole(array):
    return full(array.shape, **ONE)


def single(kernel, args, out_shape, after=(), scratch=(), **kw):
    specs = [smem() if v.dtype == jnp.int32 else whole(v) for v in args]
    shapes = out_shape if isinstance(out_shape, (list, tuple)) else [out_shape]
    out = run(
        kernel, len(args), args, after, grid=(1,), in_specs=specs, out_specs=[whole(v) for v in shapes], out_shape=list(shapes),
        scratch_shapes=list(scratch), compiler_params=params(), **kw
    )
    return out if isinstance(out_shape, (list, tuple)) else out[0]


def colsum(v):
    return jnp.sum(v, axis=0, keepdims=True)


def norm_parts(x):
    c = x - jnp.mean(x, axis=-1, keepdims=True)
    r = lax.rsqrt(jnp.mean(c * c, axis=-1, keepdims=True) + EPS)
    return c * r, r


def row_order():
    cells = np.arange(ROWS)
    win, rest = cells // TOK, cells % TOK
    a, b = rest // WIN, rest % WIN
    m = np.zeros((ROWS, ROWS), np.float32)
    m[cells, a * GRID + (win * WIN + b + SHIFT) % GRID] = 1
    return m


def spread_q():
    q = np.arange(TOK)
    m = np.zeros((TOK, NARROW), np.float32)
    m[q, SPAN * (q // WIN) + q % WIN] = 1
    return m


def spread_k(reverse):
    k = np.arange(TOK)
    b = k % WIN
    m = np.zeros((TALL, TOK), np.float32)
    m[16 * (k // WIN) + (WIN - 1 - b if reverse else b), k] = 1
    return m


def copies(plan, refs, at, targets, sems):
    for i, (src, row, rows, col, cols, dst, put) in enumerate(plan):
        place = pl.ds(pl.multiple_of(at[i], 16), rows)
        yield pltpu.make_async_copy(
            refs[src].at[pl.ds(row, rows), pl.ds(col, cols)], targets[dst].at[place, pl.ds(put, cols)], sems.at[i]
        )


def region_masks():
    line = np.arange(GRID)
    region = (line >= GRID - WIN).astype(np.int32) + (line >= GRID - SHIFT).astype(np.int32)
    lab = 3 * region[:, None] + region[None, :]
    lab = lab.reshape(2, WIN, 2, WIN).transpose(0, 2, 1, 3).reshape(2, 2, TOK)
    return np.where(lab[:, :, :, None] != lab[:, :, None, :], MASKED, 0.0).astype(np.float32)


def bias_kernel(spot_ref, table_ref, mask_ref, sq_ref, sk_ref, out_ref, tall):
    masks = [mask_ref[spot_ref[1], w].astype(F32) for w in range(2)]
    for h in range(HP):
        row = pltpu.roll(jnp.broadcast_to(table_ref[h : h + 1, :], (16, WIDE)), 0, 1, stride=1, stride_axis=0)
        for a in range(WIN):
            off = (SPAN * a - SPAN * (WIN - 1) - (WIN - 1)) % WIDE
            tall[16 * a : 16 * a + 16, :] = pltpu.roll(row, off, 1)[:, :NARROW].astype(BF)
        wide = nn(tall[...], sq_ref[...]).astype(BF)
        bias = nn(sk_ref[...], wide)
        for w in range(2):
            out_ref[w, h] = (bias + masks[w]) * LOG2E


def bias_call(group, spot, table):
    args = (spot, table, jnp.asarray(region_masks(), BF), jnp.asarray(spread_q().T, BF), jnp.asarray(spread_k(False).T, BF))
    out = SD((2, HP, TOK, TOK), F32)
    return pl.pallas_call(
        bias_kernel,
        grid=(1,),
        in_specs=[smem(), pl.BlockSpec((HP, WIDE), lambda i: (group, 0))] + [whole(v) for v in args[2:]],
        out_specs=whole(out),
        out_shape=out,
        scratch_shapes=[pltpu.VMEM((TALL, NARROW), BF)],
        compiler_params=params(),
        cost_estimate=cost(2e9, 3 * MB),
        name="bias",
    )(*args)


V_UP, V_SMALL, V_IN, V_ONE, V_PEAK, V_TABLE, V_ROWS = 0, 4, 8, 11, 13, 16, 40


def table_kernel(db0_ref, db1_ref, db2_ref, up_ref, down_ref, small_ref, in01_ref, in2_ref, one_ref, peak_ref, sq_ref, sk_ref, out_ref):
    def split(v):
        hi = v.astype(BF)
        return hi, (v - hi.astype(F32)).astype(BF)

    out_ref[...] = jnp.zeros_like(out_ref)
    for j in range(8):
        out_ref[V_UP + j // 2 : V_UP + j // 2 + 1, (j % 2) * CH : (j % 2 + 1) * CH] = up_ref[j]
    out_ref[V_SMALL : V_SMALL + 1, :] = down_ref[...]
    out_ref[V_SMALL + 1 : V_SMALL + 4, :] = small_ref[1:4, :]
    for p in range(3):
        row = in01_ref[p] if p < 2 else in2_ref[0]
        for k in range(3):
            out_ref[V_IN + k : V_IN + k + 1, p * LP : (p + 1) * LP] = row[:, k * LP : (k + 1) * LP]
    out_ref[V_ONE : V_ONE + 2, :] = one_ref[0:2, :]
    out_ref[V_PEAK : V_PEAK + 1, :HEADS] = peak_ref[...]
    for h in range(HEADS):
        hi, lo = split((db0_ref, db1_ref, db2_ref)[h // HP][h % HP])
        tall = nn(sk_ref[...], hi) + nn(sk_ref[...], lo)
        hi, lo = split(tall)
        wide = nn(hi, sq_ref[...]) + nn(lo, sq_ref[...])
        wide = jnp.concatenate([wide, jnp.zeros((TALL, WIDE - NARROW), F32)], axis=1)
        tot = jnp.zeros((16, WIDE), F32)
        for a in range(WIN):
            tot = tot + pltpu.roll(wide[16 * a : 16 * a + 16, :], SPAN * (WIN - 1 - a), 1)
        tot = pltpu.roll(tot, 0, 1, stride=1, stride_axis=0)
        out_ref[V_TABLE + h : V_TABLE + h + 1, :WIDE] = colsum(tot)


def table_call(dbs, up, down, small, in01, in2, one, peaks, after):
    args = (*dbs, up, down, small, in01, in2, one, peaks, jnp.asarray(spread_q(), BF), jnp.asarray(spread_k(True), BF))
    return single(table_kernel, args, SD((V_ROWS, D), F32), after, cost_estimate=cost(6e9, 4 * MB), name="table")


def lane_head(shape):
    return lax.broadcasted_iota(jnp.int32, shape, len(shape) - 1) // HD


VECTORS = (2 * D, D, FF, D, D, D, D, D)


def first_kernel(spot_ref, *refs):
    vecs, inner_ref, first_ref, others_ref, half_ref = refs[:8], refs[8], refs[9], refs[10], refs[11]
    mine = pl.ds(pl.multiple_of(spot_ref[1] * (OWN // 2), 16), OWN // 2)
    for k in range(3):
        first_ref[:OWN, k * LP : (k + 1) * LP] = inner_ref[:, k * D : k * D + LP]
        for p in (1, 2):
            src = slice(k * D + p * LP, k * D + (p + 1) * LP)
            dst = slice(((p - 1) * 3 + k) * LP, ((p - 1) * 3 + k + 1) * LP)
            others_ref[:, dst] = inner_ref[:, src]
            half_ref[:, dst] = inner_ref[mine, src]
    rows = [jnp.zeros((8, D), F32)]
    for v in vecs:
        row = v[...].astype(F32).reshape(1, v.shape[0])
        if v.shape[0] < D:
            row = jnp.concatenate([row, jnp.zeros((1, D - v.shape[0]), F32)], axis=1)
        rows.insert(-1, row)
    first_ref[OWN:, :] = jnp.concatenate(rows, axis=0).astype(BF)


def first_call(spot, vectors, inner):
    return single(
        first_kernel, (spot, *vectors, inner), [SD((OWN + 16, D), BF), SD((OWN, 6 * LP), BF), SD((OWN // 2, 6 * LP), BF)],
        cost_estimate=cost(1e6, 3 * MB), name="first",
    )


BIG = 4 * (OWN // 2) + OWN // 2 + 2 * OWN


def cut_kernel(spot_ref, outer_ref, expand_ref, reduce_ref, own_ref, gown_ref, big_ref, up_ref):
    core = spot_ref[1]
    hlf = OWN // 2
    n = own_ref.shape[0]
    mine = pl.ds(pl.multiple_of(core * hlf, 16), hlf)
    for k in range(4):
        big_ref[k * hlf : (k + 1) * hlf, :] = expand_ref[mine, k * D : (k + 1) * D]
    big_ref[4 * hlf : 5 * hlf, :] = outer_ref[mine, :]
    big_ref[5 * hlf :, :] = reduce_ref[pl.ds(pl.multiple_of(core * 2 * OWN, 16), 2 * OWN), :]
    up_ref[:n] = own_ref[...]
    up_ref[n:] = gown_ref[...]


def cut_call(spot, outer, expand, reduce, own, gown):
    n = own.shape[0]
    top = full((n, TOK, D))
    shapes = [SD((BIG, D), BF), SD((2 * n, TOK, D), BF)]
    return pl.pallas_call(
        cut_kernel,
        grid=(1,),
        in_specs=[smem(), whole(outer), whole(expand), whole(reduce), top, top],
        out_specs=[whole(v) for v in shapes],
        out_shape=shapes,
        compiler_params=params(),
        cost_estimate=cost(1e6, 8 * MB),
        name="cut",
    )(spot, outer, expand, reduce, own, gown)


def prep_kernel(own_ref, gown_ref, recv_ref, alive_ref, pm_ref, tok_ref, g_ref, sum_ref):
    n = own_ref.shape[0]
    tot = jnp.zeros((1, D), F32)
    for i in range(n):
        tok_ref[i] = nn(pm_ref[...], jnp.concatenate([own_ref[i, TOK:, :], recv_ref[i]], axis=0)).astype(BF)
        g = nn(pm_ref[...], jnp.concatenate([gown_ref[i, TOK:, :], recv_ref[n + i]], axis=0)) * alive_ref[0:1, i : i + 1]
        g_ref[i] = g.astype(BF)
        tot = tot + colsum(g)
    sum_ref[...] = tot


def prep_call(own, gown, recv, alive, pm):
    rows = SD(own.shape, BF)
    return single(
        prep_kernel, (own, gown, recv, alive, pm), [rows, rows, SD((1, D), F32)], cost_estimate=cost(3e9, 16 * MB), name="prep"
    )


def vector_kernel(spot_ref, pa_ref, pb_ref, pc_ref, pd_ref, tok_ref, inb_ref, up_ref, vec_ref, n1_ref, n1t_ref, parts):
    n = tok_ref.shape[0]
    for r, ref in enumerate((pa_ref, pb_ref, pc_ref, pd_ref)):
        parts[jnp.bitwise_xor(spot_ref[0], r)] = ref[:8, :].astype(F32)

    def vector(i):
        size = VECTORS[i] // 4
        return jnp.concatenate([parts[s][i : i + 1, :size] for s in range(4)], axis=1)

    vin = vector(0)
    for p in range(3):
        inb_ref[p] = jnp.concatenate(
            [vin[:, p * LP : (p + 1) * LP], jnp.zeros((1, LP), F32), vin[:, D + p * LP : D + (p + 1) * LP]], axis=1
        )
    vup = vector(2)
    for j in range(8):
        up_ref[j] = vup[:, j * CH : (j + 1) * CH]
    gain, shift = vector(4), vector(5)
    vec_ref[...] = jnp.zeros_like(vec_ref)
    for r, v in enumerate((vector(1), vector(3), gain, vector(6), vector(7))):
        vec_ref[r : r + 1, :] = v
    for i in range(n):
        xh, _ = norm_parts(tok_ref[i].astype(F32))
        n1 = (xh * gain + shift).astype(BF)
        n1_ref[i] = n1
        n1t_ref[:, i * ROWS : (i + 1) * ROWS] = n1.T


def vector_call(spot, parts, tok):
    n = tok.shape[0]
    last = parts[0].shape[0] // 16 - 1
    shapes = [SD((3, 1, 3 * LP), F32), SD((8, 1, CH), F32), SD((8, D), F32), SD(tok.shape, BF), SD((D, n * ROWS), BF)]
    return pl.pallas_call(
        vector_kernel,
        grid=(1,),
        in_specs=[smem()] + [pl.BlockSpec((16, D), lambda i: (last, 0))] * 4 + [whole(tok)],
        out_specs=[whole(v) for v in shapes],
        out_shape=shapes,
        scratch_shapes=[pltpu.VMEM((4, 8, D), F32)],
        compiler_params=params(),
        cost_estimate=cost(5e9, 8 * MB),
        name="vectors",
    )(spot, *parts, tok)


def attend_kernel(plan, count, n1_ref, b_ref, bm_ref, at_ref, *rest):
    pieces = rest[:count]
    proj_ref, pt_ref, att_ref, peak_ref, w_ref, sems = rest[count:]

    @pl.when(pl.program_id(0) == 0)
    def _():
        for c in copies(plan, pieces, at_ref, (w_ref,), sems):
            c.start()
        for c in copies(plan, pieces, at_ref, (w_ref,), sems):
            c.wait()

    proj_ref[0] = (nn(n1_ref[0], w_ref[...]) + b_ref[0]).astype(BF)
    hid = lane_head((TOK, LB))
    scale = HD**-0.5
    for w in range(2):
        r = slice(w * TOK, (w + 1) * TOK)
        for blk in range(LP // LB):
            l = blk * LB
            q = proj_ref[0, r, l : l + LB]
            k = proj_ref[0, r, LP + l : LP + l + LB]
            v = proj_ref[0, r, 2 * LP + l : 2 * LP + l + LB]
            vt = v.T
            outs = []
            for h in range(HB):
                hh = blk * HB + h
                km = jnp.where(hid == h, k, jnp.zeros_like(k))
                st = nt(km, q)
                peak_ref[0, w, hh : hh + 1, :] = jnp.max(st, axis=0, keepdims=True) * scale
                t = st * (scale * LOG2E) + bm_ref[w, hh]
                e = jnp.exp2(t - jnp.max(t, axis=0, keepdims=True))
                p = (e * (1.0 / colsum(e))).astype(BF)
                pt_ref[0, w, hh] = p
                outs.append(nn(vt[HD * h : HD * h + HD, :], p))
            att_ref[0, r, l : l + LB] = jnp.concatenate(outs, axis=0).astype(BF).T


def attend_call(group, n1, b, bm, at, plan, pieces, after):
    n = n1.shape[0]

    def blk(*s):
        return pl.BlockSpec((1,) + s, lambda i: (i,) + (0,) * len(s))

    return run(
        functools.partial(attend_kernel, plan, len(pieces)), 4 + len(pieces), (n1, b, bm, at, *pieces), after,
        grid=(n,),
        in_specs=[blk(ROWS, D), pl.BlockSpec((1, 1, 3 * LP), lambda i: (group, 0, 0)), full((2, HP, TOK, TOK), **ONE), smem()]
        + [any_space()] * len(pieces),
        out_specs=[blk(ROWS, 3 * LP), blk(2, HP, TOK, TOK), blk(ROWS, LP), blk(2, HP, TOK), full((D, 3 * LP), **ONE)],
        out_shape=[SD((n, ROWS, 3 * LP), BF), SD((n, 2, HP, TOK, TOK), BF), SD((n, ROWS, LP), BF), SD((n, 2, HP, TOK), F32),
                   SD((D, 3 * LP), BF)],
        scratch_shapes=[pltpu.SemaphoreType.DMA((len(plan),))],
        compiler_params=params(),
        cost_estimate=cost(1.3e10, 12 * MB, 1.4e6),
        name="attend",
    )


def gelu_parts(h):
    d = 1.0 + (0.3275911 * 0.5**0.5) * jnp.abs(h)
    t = pl.reciprocal(d, approx=True)
    t = t * (2.0 - d * t)
    e = jnp.exp2(h * h * (-0.5 * LOG2E))
    p = (((0.5 * 1.061405429) * t - 0.5 * 1.453152027) * t + 0.5 * 1.421413741) * t - 0.5 * 0.284496736
    p = (p * t + 0.5 * 0.254829592) * t * e
    cdf = jnp.where(h >= 0, 1.0 - p, p)
    return cdf, cdf + h * (e * ((2 * math.pi) ** -0.5))


def middle_kernel(plan, count, spot_ref, tok_ref, att0_ref, att1_ref, att2_ref, gin_ref, pmt_ref, vec_ref, eb_ref,
                  at_ref, *rest):
    pieces = rest[:count]
    (stay_ref, send_ref, gmid_ref, datt_ref, os_ref, ok_ref, es_ref, ek_ref, rs_ref, rk_ref, geb_ref, small_ref,
     wo, we, wr, mid, n2, g, n2t, acc, e2, act, gh, sems) = rest[count:]
    j = pl.program_id(0)
    n = tok_ref.shape[0]
    N = n * ROWS
    me = spot_ref[0]
    core = spot_ref[1]
    early = [k for k, entry in enumerate(plan) if entry[5] == 0]
    out_b, red_b, gain, shift = vec_ref[0:1, :], vec_ref[1:2, :], vec_ref[3:4, :], vec_ref[4:5, :]

    def attended(i):
        return jnp.concatenate([att0_ref[i], att1_ref[i], att2_ref[i]], axis=-1)

    @pl.when(j == 0)
    def _():
        moves = list(copies(plan, pieces, at_ref, (wo, we, wr), sems))
        for c in moves:
            c.start()
        for k in early:
            moves[k].wait()
        for i in range(n):
            s = slice(i * ROWS, (i + 1) * ROWS)
            g[s, :] = gin_ref[i]
            m = tok_ref[i].astype(F32) + nn(attended(i), wo[...]) + out_b
            mid[s, :] = m
            xh, _ = norm_parts(m)
            x2 = (xh * gain + shift).astype(BF)
            n2[s, :] = x2
            n2t[:, s] = x2.T
            acc[s, :] = m + red_b
            e2[s, :] = jnp.zeros((ROWS, D), F32)
        for k, c in enumerate(moves):
            if k not in early:
                c.wait()

    sh = jnp.bitwise_xor(me, j % 4)
    at = (2 * sh + jnp.bitwise_xor(core, 1 - j // 4)) * CH
    ecol = pl.ds(pl.multiple_of(at, CH), CH)
    tot = jnp.zeros((1, CH), F32)
    for s0 in range(0, N, NB):
        s = slice(s0, s0 + NB)
        h = nn(n2[s, :], we[:, ecol]) + eb_ref[0]
        cdf, dg = gelu_parts(h)
        act[s, :] = (h * cdf).astype(BF)
        x = (nt(g[s, :], wr[ecol, :]) * dg).astype(BF)
        gh[s, :] = x
        tot = tot + colsum(x.astype(F32))
    geb_ref[0] = tot
    ge = nn(n2t[...], gh[...]).astype(BF)
    gr = tn(act[...], g[...]).astype(BF)

    def put(e_ref, r_ref):
        for b in range(4):
            e_ref[jnp.bitwise_xor(me, b), 0] = ge[b * OWN : (b + 1) * OWN, :]
            r_ref[0, b] = gr[(b // 2) * OWN : (b // 2 + 1) * OWN, (b % 2) * CH : (b % 2 + 1) * CH]

    @pl.when(j < 4)
    def _():
        put(es_ref, rs_ref)

    @pl.when(j >= 4)
    def _():
        put(ek_ref, rk_ref)

    for s0 in range(0, N, NB):
        s = slice(s0, s0 + NB)
        acc[s, :] += nn(act[s, :], wr[ecol, :])
        e2[s, :] += nt(gh[s, :], we[:, ecol])

    @pl.when(j == 7)
    def _():
        gn = jnp.zeros((1, D), F32)
        shf = gn
        ob = gn
        for i in range(n):
            s = slice(i * ROWS, (i + 1) * ROWS)
            o = nn(pmt_ref[...], acc[s, :].astype(BF)).astype(BF)
            stay_ref[i] = o[:TOK]
            send_ref[i] = o[TOK:]
            xh, r = norm_parts(mid[s, :])
            d = e2[s, :]
            gn = gn + colsum(d * xh)
            shf = shf + colsum(d)
            d = d * gain
            gm = g[s, :].astype(F32) + r * (
                d - jnp.mean(d, axis=-1, keepdims=True) - xh * jnp.mean(d * xh, axis=-1, keepdims=True)
            )
            gmid_ref[i] = gm
            gb = gm.astype(BF)
            ob = ob + colsum(gb.astype(F32))
            g[s, :] = gb
            datt_ref[i] = nt(gb, wo[...]).astype(BF)
            n2[s, :] = attended(i)
        for c, ref in ((1 - core, os_ref), (core, ok_ref)):
            go = tn(n2[...], g[:, pl.ds(pl.multiple_of(c * CH, 128), CH)]).astype(BF)
            for b in range(4):
                ref[jnp.bitwise_xor(me, b), 0] = go[b * OWN : (b + 1) * OWN, :]
        small_ref[1:2, :] = gn
        small_ref[2:3, :] = shf
        small_ref[3:4, :] = ob


def crossed(r):
    return 2 * (r % 2) + r // 2


def middle_call(spot, tok, atts, g, pmt, vecs, eb, at, plan, pieces, after):
    n = tok.shape[0]
    N = n * ROWS
    blocks = SD((4, 4, OWN, CH), BF)

    def chunk(j, spot):
        return 2 * jnp.bitwise_xor(spot[0], j % 4) + jnp.bitwise_xor(spot[1], 1 - j // 4)

    def early(j, spot):
        return jnp.bitwise_xor(spot[0], jnp.minimum(j, 3))

    def late(j, spot):
        return jnp.bitwise_xor(spot[0], jnp.maximum(j, 4) - 4)

    rows = full((n, ROWS, D), **ONE)
    third = full((n, ROWS, LP), **ONE)
    cut = full((n, TOK, D), **ONE)
    outer = full((4, 1, OWN, CH), **ONE)
    args = (spot, tok, *atts, g, pmt, vecs, eb, at, *pieces)

    def body(*refs):
        middle_kernel(plan, len(pieces), *refs[: len(args)], *refs[len(args) + len(after) :])

    grid_spec = pltpu.PrefetchScalarGridSpec(
        num_scalar_prefetch=1,
        grid=(8,),
        in_specs=[rows, third, third, third, rows, full((ROWS, ROWS)), full((8, D)),
                  pl.BlockSpec((1, 1, CH), lambda j, spot: (chunk(j, spot), 0, 0)), smem()]
        + [any_space()] * (len(pieces) + len(after)),
        out_specs=[cut, cut, rows, rows, outer, outer,
                   pl.BlockSpec((4, 1, OWN, CH), lambda j, spot: (0, early(j, spot), 0, 0)),
                   pl.BlockSpec((4, 1, OWN, CH), lambda j, spot: (0, late(j, spot), 0, 0)),
                   pl.BlockSpec((1, 4, OWN, CH), lambda j, spot: (crossed(jnp.minimum(j, 3)), 0, 0, 0)),
                   pl.BlockSpec((1, 4, OWN, CH), lambda j, spot: (crossed(jnp.maximum(j, 4) - 4), 0, 0, 0)),
                   pl.BlockSpec((1, 1, CH), lambda j, spot: (chunk(j, spot), 0, 0)), full((8, D))],
        scratch_shapes=[pltpu.VMEM((D, D), BF), pltpu.VMEM((D, FF), BF), pltpu.VMEM((FF, D), BF),
                        pltpu.VMEM((N, D), F32), pltpu.VMEM((N, D), BF), pltpu.VMEM((N, D), BF), pltpu.VMEM((D, N), BF),
                        pltpu.VMEM((N, D), F32), pltpu.VMEM((N, D), F32), pltpu.VMEM((N, CH), BF), pltpu.VMEM((N, CH), BF),
                        pltpu.SemaphoreType.DMA((len(plan),))],
    )
    return pl.pallas_call(
        body,
        grid_spec=grid_spec,
        out_shape=[SD((n, TOK, D), BF), SD((n, TOK, D), BF), SD((n, ROWS, D), F32), SD((n, ROWS, D), BF),
                   SD((4, 1, OWN, CH), BF), SD((4, 1, OWN, CH), BF), blocks, blocks, blocks, blocks,
                   SD((8, 1, CH), F32), SD((8, D), F32)],
        compiler_params=params(62),
        cost_estimate=cost(6e10, 40 * MB, 7e6),
        name="middle",
    )(*args, *after)


def back_kernel(proj_ref, pt_ref, da_ref, gp_ref, db_ref):
    @pl.when(pl.program_id(0) == 0)
    def _():
        db_ref[...] = jnp.zeros_like(db_ref)

    hid = lane_head((TOK, LB))
    scale = HD**-0.5
    for w in range(2):
        r = slice(w * TOK, (w + 1) * TOK)
        for blk in range(LP // LB):
            l = blk * LB
            q = proj_ref[0, r, l : l + LB]
            k = proj_ref[0, r, LP + l : LP + l + LB]
            v = proj_ref[0, r, 2 * LP + l : 2 * LP + l + LB]
            do = da_ref[0, r, l : l + LB]
            qt, kt, dt = q.T, k.T, do.T
            dq, dk, dv = [], [], []
            for h in range(HB):
                hh = blk * HB + h
                s = slice(HD * h, HD * h + HD)
                dp = nt(jnp.where(hid == h, v, jnp.zeros_like(v)), do)
                pb = pt_ref[0, w, hh]
                p = pb.astype(F32)
                pd = p * dp
                ds = pd - p * colsum(pd)
                db_ref[hh] += ds
                dsb = ds.astype(BF)
                dq.append(nn(kt[s, :], dsb))
                dk.append(nt(qt[s, :], dsb))
                dv.append(nt(dt[s, :], pb))
            gp_ref[0, r, l : l + LB] = (jnp.concatenate(dq, axis=0) * scale).astype(BF).T
            gp_ref[0, r, LP + l : LP + l + LB] = (jnp.concatenate(dk, axis=0) * scale).astype(BF).T
            gp_ref[0, r, 2 * LP + l : 2 * LP + l + LB] = jnp.concatenate(dv, axis=0).astype(BF).T


def back_call(group, proj, pt, da, after):
    n = proj.shape[0]

    def blk(*s):
        return pl.BlockSpec((1,) + s, lambda i: (i,) + (0,) * len(s))

    return run(
        back_kernel, 3, (proj, pt, da), after,
        grid=(n,),
        in_specs=[blk(ROWS, 3 * LP), blk(2, HP, TOK, TOK), pl.BlockSpec((1, ROWS, LP), lambda i: (i, 0, group))],
        out_specs=[blk(ROWS, 3 * LP), full((HP, TOK, TOK))],
        out_shape=[SD((n, ROWS, 3 * LP), BF), SD((HP, TOK, TOK), F32)],
        compiler_params=params(),
        cost_estimate=cost(1.8e10, 10 * MB),
        name="attend_back",
    )


def inner_kernel(spot_ref, n1t_ref, *rest):
    me = spot_ref[0]
    core = spot_ref[1]
    gp_refs, outs, sum_ref = rest[: len(rest) // 3], rest[len(rest) // 3 : -1], rest[-1]
    for k, gp_ref in enumerate(gp_refs):
        n = gp_ref.shape[0]
        gp = gp_ref[...].reshape(n * ROWS, 3 * LP)
        sum_ref[k] = colsum(gp.astype(F32))
        gi = nn(n1t_ref[...], gp).astype(BF)
        send, keep = outs[2 * k], outs[2 * k + 1]

        for c in range(2):
            @pl.when(core == c)
            def _():
                for b in range(4):
                    r = slice(b * OWN, (b + 1) * OWN)
                    rel = jnp.bitwise_xor(me, b)
                    rel = crossed(rel) if k == 0 else rel
                    keep[rel, 0] = gi[r, c * CH : (c + 1) * CH]
                    send[rel, 0] = gi[r, (1 - c) * CH : (2 - c) * CH]


def inner_call(spot, n1t, gps, after):
    block = SD((4, 1, OWN, CH), BF)
    return single(
        inner_kernel, (spot, n1t, *gps), [block] * (2 * len(gps)) + [SD((len(gps), 1, 3 * LP), F32)], after,
        cost_estimate=cost(4e9 * len(gps), 6 * MB), name="inner_grad",
    )


def last_kernel(tok_ref, gmid_ref, vec_ref, pmt_ref, gp0_ref, gp1_ref, gp2_ref, w0_ref, w1_ref, w2_ref,
                small_ref, stay_ref, send_ref):
    @pl.when(pl.program_id(0) == 0)
    def _():
        small_ref[...] = jnp.zeros_like(small_ref)

    d = nt(gp0_ref[0], w0_ref[...]) + nt(gp1_ref[0], w1_ref[...]) + nt(gp2_ref[0], w2_ref[...])
    xh, r = norm_parts(tok_ref[0].astype(F32))
    small_ref[0:1, :] += colsum(d * xh)
    small_ref[1:2, :] += colsum(d)
    d = d * vec_ref[2:3, :]
    gm = gmid_ref[0] + r * (d - jnp.mean(d, axis=-1, keepdims=True) - xh * jnp.mean(d * xh, axis=-1, keepdims=True))
    o = nn(pmt_ref[...], gm.astype(BF)).astype(BF)
    stay_ref[0] = o[:TOK]
    send_ref[0] = o[TOK:]


def last_call(tok, gmid, gain, pmt, gps, ws, after):
    n = tok.shape[0]

    def blk(*s):
        return pl.BlockSpec((1,) + s, lambda i: (i,) + (0,) * len(s))

    return run(
        last_kernel, 10, (tok, gmid, gain, pmt, *gps, *ws), after,
        grid=(n,),
        in_specs=[blk(ROWS, D), blk(ROWS, D), full((8, D)), full((ROWS, ROWS))] + [blk(ROWS, 3 * LP)] * 3
        + [full((D, 3 * LP), **ONE)] * 3,
        out_specs=[full((8, D)), blk(TOK, D), blk(TOK, D)],
        out_shape=[SD((8, D), F32), SD((n, TOK, D), BF), SD((n, TOK, D), BF)],
        compiler_params=params(),
        cost_estimate=cost(2e10, 20 * MB),
        name="last",
    )


def vector_finish_kernel(count, spot_ref, sums_ref, thr_ref, inner_ref, inb_ref, outb_ref, upb_ref, downb_ref, g1_ref, s1_ref,
                         g2_ref, s2_ref, table_ref, clip_ref, factor_ref, max_ref):
    shard = spot_ref[2]

    def part(ref, rows, step=1):
        size = ref.shape[0]
        start = shard * size
        row = sums_ref[pl.ds(rows + step * (start // D), 1), :]
        row = jnp.broadcast_to(row, (8, D))
        ref[...] = pltpu.roll(row, D - start % D, 1)[0:1, :size].reshape(size)

    part(inb_ref, V_IN, 2)
    part(upb_ref, V_UP)
    for i, ref in enumerate((downb_ref, g2_ref, s2_ref, outb_ref)):
        part(ref, V_SMALL + i)
    part(g1_ref, V_ONE)
    part(s1_ref, V_ONE + 1)
    table_ref[...] = sums_ref[V_TABLE : V_TABLE + HEADS, :WIDE].T[: SPAN * SPAN, :]
    top = sums_ref[V_PEAK : V_PEAK + 1, :HEADS]
    factor = thr_ref[...].reshape(1, HEADS)
    factor = factor / jnp.maximum(top, factor)
    max_ref[...] = top.reshape(HEADS)
    factor_ref[...] = factor.reshape(HEADS)
    root = jnp.broadcast_to(jnp.sqrt(factor), (8, HEADS))
    head = lax.broadcasted_iota(jnp.int32, (HEADS, D), 0)
    col = lax.broadcasted_iota(jnp.int32, (HEADS, D), 1) // HD
    scale = lax.dot_general(root, (head == col).astype(F32), (((1,), (0,)), ((), ())), preferred_element_type=F32,
                            precision=lax.Precision.HIGHEST)[0:1, :]
    for k in range(2):
        clip_ref[:, k * D : (k + 1) * D] = (inner_ref[:, k * D : (k + 1) * D].astype(F32) * scale).astype(BF)
    clip_ref[:, 2 * D :] = inner_ref[:, 2 * D :]


def vector_finish(place, sums, threshold, inner, count):
    line = SD((D // count,), F32)
    return single(
        functools.partial(vector_finish_kernel, count), (place, sums, threshold, inner),
        [SD((2 * D // count,), F32), line, SD((FF // count,), F32), line, line, line, line, line,
         SD((SPAN * SPAN, HEADS), F32), SD(inner.shape, BF), SD((HEADS,), F32), SD((HEADS,), F32)],
        cost_estimate=cost(1e7, 3 * MB), name="vector_finish",
    )


def feed_finish_kernel(spot_ref, em_ref, eo_ref, rm_ref, ro_ref, ge_ref, gr_ref):
    for core in range(2):
        @pl.when(spot_ref[1] == core)
        def _():
            for c, e_ref, r_ref in ((core, em_ref, rm_ref), (1 - core, eo_ref, ro_ref)):
                for b in range(4):
                    ge_ref[:, (2 * b + c) * CH : (2 * b + c + 1) * CH] = e_ref[b].astype(F32)
                    r = c * CH + (b // 2) * OWN
                    gr_ref[r : r + OWN, (b % 2) * CH : (b % 2 + 1) * CH] = r_ref[b].astype(F32)


def feed_finish(spot, em, eo, rm, ro):
    return single(
        feed_finish_kernel, (spot, em, eo, rm, ro), [SD((OWN, FF), F32), SD((2 * CH, D), F32)],
        cost_estimate=cost(1e7, 8 * MB), name="feed_finish",
    )


def inner_columns(p, c):
    if c == 0:
        return [(0, LP, p * LP), (LP, LP // 2, D + p * LP)]
    return [(0, LP // 2, D + p * LP + LP // 2), (LP // 2, LP, 2 * D + p * LP)]


def inner_finish_kernel(spot_ref, *refs):
    mine, other, (gi_ref, go_ref) = refs[:4], refs[4:8], refs[8:]
    for core in range(2):
        @pl.when(spot_ref[1] == core)
        def _():
            for c, blocks in ((core, mine), (1 - core, other)):
                for p in range(3):
                    for at, size, put in inner_columns(p, c):
                        gi_ref[:, put : put + size] = blocks[p][0, :, at : at + size].astype(F32)
                go_ref[:, c * CH : (c + 1) * CH] = blocks[3][0].astype(F32)


def inner_finish(spot, mine, other):
    return single(
        inner_finish_kernel, (spot, *mine, *other), [SD((OWN, 3 * D), F32), SD((OWN, D), F32)],
        cost_estimate=cost(1e7, 4 * MB), name="inner_finish",
    )


def swap(block, axis, bit):
    count = lax.axis_size(axis)
    return lax.ppermute(block, axis, [(i, i ^ bit) for i in range(count) if i ^ bit < count])


def everywhere_hops():
    for axis in ("half", "shard", "replica"):
        bit = 1
        while bit < lax.axis_size(axis):
            yield axis, bit
            bit *= 2


def join_vectors(a, b):
    row = lax.broadcasted_iota(jnp.int32, a.shape, 0)
    return jnp.where(row == V_PEAK, jnp.maximum(a, b), a + b)


class Everywhere:
    def __init__(self, value):
        self.value = value
        self.hops = list(everywhere_hops())
        self.flying = None
        self.step()

    def step(self):
        if self.flying is not None:
            self.value = join_vectors(self.value, self.flying)
            self.flying = None
        if self.hops:
            self.flying = swap(self.value, *self.hops.pop(0))
        return [self.value]

    @property
    def done(self):
        return self.flying is None


def near(block):
    return [swap(block, "shard", 1), swap(block, "shard", 2)]


def fence(*values):
    return lax.optimization_barrier(values)


def add(a, b):
    return (a.astype(F32) + b.astype(F32)).astype(BF)


class Reduction:
    def __init__(self, sends, keeps, replica, short):
        self.short = short
        self.low = (replica & 1) == 0
        self.low2 = (replica & 2) == 0
        self.keep = keeps
        self.sent = sends
        self.stage = 0
        self.flying = [swap(v, "half", 1) for v in sends]

    def step(self):
        hlf = OWN // 2
        got, low, low2 = self.flying, self.low, self.low2
        if self.stage == 0:
            self.sent = [add(k[2:], g[2:]) for k, g in zip(self.keep, got)]
            self.keep = [add(k[:2], g[:2]) for k, g in zip(self.keep, got)]
            self.flying = [swap(self.sent[0], "shard", 1), swap(self.sent[1], "shard", 2)]
        elif self.stage == 1:
            self.sent = [add(k[1], g[1]) for k, g in zip(self.keep, got)]
            self.keep = [add(k[0], g[0]) for k, g in zip(self.keep, got)]
            self.flying = [swap(self.sent[0], "shard", 2), swap(self.sent[1], "shard", 1)]
        elif self.stage == 2:
            a, b = (add(k, g) for k, g in zip(self.keep, got))
            self.keep = jnp.where(low, a, b)
            self.sent = [jnp.where(low, b, a)]
            self.flying = swap(self.sent[0], "replica", 1)
        elif self.stage == 3 and self.short:
            self.keep = add(self.keep, got)
            self.sent = [self.keep]
            self.flying = swap(self.keep, "replica", 2)
            self.stage = 4
        elif self.stage == 3:
            u = add(self.keep, got)
            self.keep = jnp.where(low2, u[:, :hlf], u[:, hlf:])
            self.sent = [jnp.where(low2, u[:, hlf:], u[:, :hlf])]
            self.flying = swap(self.sent[0], "replica", 2)
        elif self.stage == 4:
            self.keep = add(self.keep, got)
            self.sent = [self.keep]
            self.flying = swap(self.keep, "replica", 2)
        elif self.stage == 5:
            v = self.keep
            if self.short:
                self.keep = add(v, got)
            else:
                self.keep = jnp.concatenate([jnp.where(low2, v, got), jnp.where(low2, got, v)], axis=1)
            self.sent = [self.keep]
            self.flying = swap(self.keep, "replica", 1)
        elif self.stage == 6:
            v = self.keep
            self.keep = [jnp.where(low, v, got), jnp.where(low, got, v)]
            self.sent = self.keep
            self.flying = [swap(v, "half", 1) for v in self.keep]
        self.stage += 1
        return list(self.sent)

    @property
    def done(self):
        return self.stage == 7


def together(chains, *others):
    left = [c for c in chains if not c.done]
    flying, others = fence([c.flying for c in left], others)
    for c, v in zip(left, flying):
        c.flying = v
        c.step()
    return others


def shards(images, cotangent, present, threshold, inner_weight, inner_bias, outer_weight, outer_bias, expand_weight,
           expand_bias, reduce_weight, reduce_bias, first_gain, first_shift, second_gain, second_shift, bias_table):
    n = images.shape[0]
    core = lax.axis_index("half")
    shard = lax.axis_index("shard")
    replica = lax.axis_index("replica")
    shard_count = lax.axis_size("shard")
    quick = shard_count == 4 and lax.axis_size("replica") == 4
    me = shard if quick else jnp.int32(0)
    spot = jnp.stack([me, core]).astype(jnp.int32)
    own_images = images.reshape(n, ROWS, D)
    own_grad = cotangent.reshape(n, ROWS, D)
    vectors = (inner_bias, outer_bias, expand_bias, reduce_bias, first_gain, first_shift, second_gain, second_shift)
    order = jnp.asarray(row_order(), BF)
    back_order = jnp.asarray(row_order().T, BF)
    alive = present.astype(F32).reshape(1, n)
    table_rows = jnp.pad(bias_table.astype(F32).T, ((0, 0), (0, WIDE - bias_table.shape[0])))
    if quick:
        first, others, others_half = first_call(spot, vectors, inner_weight)
        get_first, get_others = near(first), near(others_half)
        expand_weight, first = fence(expand_weight, first)
        big, up = cut_call(spot, outer_weight, expand_weight, reduce_weight, own_images, own_grad)
        spot, up, big = fence(spot, up, big)
        upper = swap(up, "half", 1)
        masks_0 = bias_call(0, spot, table_rows)
        get_first, upper, masks_0 = fence(get_first, upper, masks_0)
        get_first.append(swap(get_first[0], "shard", 2))
        tok, g, grad_down = prep_call(own_images, own_grad, upper, alive, order)
        get_first, get_others, tok = fence(get_first, get_others, tok)
        first_pieces = [first] + get_first
        get_others.append(swap(get_others[1], "shard", 1))
        others_back = [swap(v, "half", 1) for v in get_others[:2]]
        in_bias, up_bias, vecs, n1, n1t = vector_call(spot, first_pieces, tok)
        n1, big = fence(n1, big)
        get_big = near(big)
    else:
        masks_0 = bias_call(0, spot, table_rows)
        upper = jnp.concatenate([swap(own_images[:, :TOK], "half", 1), swap(own_grad[:, :TOK], "half", 1)])
        whole_vectors = [lax.all_gather(v, "shard", axis=0, tiled=True).reshape(4, -1) for v in vectors]
        parts = jnp.stack([jnp.pad(v, ((0, 0), (0, D - v.shape[1]))) for v in whole_vectors], axis=1)
        parts = [jnp.pad(parts[r], ((0, 8), (0, 0))) for r in range(4)]
        thirds = inner_weight.reshape(-1, 3, 3, LP).transpose(0, 2, 1, 3).reshape(-1, 3, 3 * LP)
        first = thirds[:, 0]
        others = thirds[:, 1:].reshape(-1, 6 * LP)

        tok, g, grad_down = prep_call(own_images, own_grad, upper, alive, order)
        in_bias, up_bias, vecs, n1, n1t = vector_call(spot, parts, tok)

    if quick:
        def places(rows):
            at = [me * rows]
            for c in (core, 1 - core):
                at += [(me ^ 1) * rows + c * (rows // 2), (me ^ 2) * rows + c * (rows // 2), (me ^ 3) * rows + c * (rows // 2)]
            return at

        first_at = jnp.stack([(me ^ r) * OWN for r in range(4)]).astype(jnp.int32)
        in_at = jnp.stack(places(OWN)).astype(jnp.int32)

        def in_plan(columns):
            return [(k, 0, OWN if k == 0 else OWN // 2, columns, 3 * LP, 0, 0) for k in range(7)]

        in_plans = [[(k, 0, OWN, 0, 3 * LP, 0, 0) for k in range(4)], in_plan(0), in_plan(3 * LP)]
    else:
        first_at = in_at = jnp.zeros((1,), jnp.int32)
        first_pieces = [lax.all_gather(first, "shard", axis=0, tiled=True)]
        others_pieces = [lax.all_gather(others, "shard", axis=0, tiled=True)]
        in_plans = [[(0, 0, D, k, 3 * LP, 0, 0)] for k in (0, 0, 3 * LP)]

    results = [attend_call(0, n1, in_bias, masks_0, first_at, in_plans[0], first_pieces, [])]
    if quick:
        get_others, others_back, results, spot = fence(get_others, others_back, results, spot)
        others_back.append(swap(get_others[2], "half", 1))
    masks_1 = bias_call(1, spot, table_rows)
    masks_2 = bias_call(2, spot, table_rows)
    if quick:
        others_back, masks_1, masks_2 = fence(others_back, masks_1, masks_2)
        others_pieces = [others] + get_others + others_back
    results.append(attend_call(1, n1, in_bias, masks_1, in_at, in_plans[1], others_pieces, [masks_2]))
    if quick:
        get_big, results, masks_2 = fence(get_big, results, masks_2)
        far = [swap(get_big[0][: BIG // 2], "shard", 2), swap(get_big[1][BIG // 2 :], "shard", 1)]
        big_back = [swap(v, "half", 1) for v in get_big]
    results.append(attend_call(2, n1, in_bias, masks_2, in_at, in_plans[2], others_pieces, []))
    if quick:
        far, big_back, results = fence(far, big_back, results)
        far_back = [swap(v, "half", 1) for v in far]
        far_back, results = fence(far_back, results)
        pieces = [outer_weight, expand_weight, reduce_weight] + get_big + far + big_back + far_back
        hlf = OWN // 2
        plan = [(0, 0, OWN, 0, D, 0, 0), (1, 0, OWN, 0, FF, 1, 0), (2, 0, 4 * OWN, 0, D, 2, 0)]
        short, long = places(OWN), places(4 * OWN)
        at = [short[0], short[0], long[0]]
        parts = [(b * hlf, hlf, 1, b * D) for b in range(4)] + [(4 * hlf, hlf, 0, 0), (5 * hlf, 4 * hlf, 2, 0)]

        def add_piece(source, lo, hi, place):
            for row, rows, target, column in parts:
                a, b = max(row, lo), min(row + rows, hi)
                if a < b:
                    plan.append((source, a - lo, b - a, 0, D, target, column))
                    at.append((long if target == 2 else short)[place] + (a - row))

        for side in range(2):
            for k in range(2):
                add_piece(3 + 4 * side + k, 0, BIG, 1 + 3 * side + k)
            add_piece(5 + 4 * side, 0, BIG // 2, 3 + 3 * side)
            add_piece(6 + 4 * side, BIG // 2, BIG, 3 + 3 * side)
        at = jnp.stack(at).astype(jnp.int32)
    else:
        pieces = [lax.all_gather(v, "shard", axis=0, tiled=True) for v in (outer_weight, expand_weight, reduce_weight)]
        plan = [(0, 0, D, 0, D, 0, 0), (1, 0, D, 0, FF, 1, 0), (2, 0, FF, 0, D, 2, 0)]
        at = jnp.zeros((3,), jnp.int32)
    projs, pts, atts, peak, ws = zip(*results)
    (stay, send, gmid, datt, out_send, out_keep, e_send, e_keep, r_send, r_keep, grad_up, small) = middle_call(
        spot, tok, atts, g, back_order, vecs, up_bias, at, plan, pieces, []
    )
    if quick:
        feed = Reduction([r_send, e_send], [r_keep, e_keep], replica, False)
    lower_out = swap(send, "half", 1)
    gp0, db0 = back_call(0, projs[0], pts[0], datt, [])
    if quick:
        (gp0, lower_out, projs) = together([feed], gp0, lower_out, projs)
    gp1, db1 = back_call(1, projs[1], pts[1], datt, feed.sent if quick else [])
    i0_send, i0_keep, i1_send, i1_keep, in01 = inner_call(spot, n1t, (gp0, gp1), [])
    chains = []
    if quick:
        i0_send, i1_send, projs = together([feed], i0_send, i1_send, projs)
        ahead = Reduction([i0_send, i1_send], [i0_keep, i1_keep], replica, True)
        chains = [feed, ahead]
    gp2, db2 = back_call(2, projs[2], pts[2], datt, feed.sent if quick else [])
    if quick:
        gp2, db2 = together(chains, gp2, db2)
    i2_send, i2_keep, in2 = inner_call(spot, n1t, (gp2,), feed.sent + ahead.sent if quick else [])
    if quick:
        rest = Reduction([i2_send, out_send], [i2_keep, out_keep], replica, True)
        chains = [feed, ahead, rest]
    one, gstay, gsend = last_call(tok, gmid, vecs, back_order, (gp0, gp1, gp2), ws, [i2_send])
    after = []
    if quick:
        gsend, one = together(chains, gsend, one)
        after = feed.sent + ahead.sent + rest.sent
    lower_grad = swap(gsend, "half", 1)
    peak = jnp.concatenate(peak, axis=2)
    peaks = jnp.max(jnp.where((present > 0)[:, None, None, None], peak, NEGATIVE), axis=(0, 1, 3)).reshape(1, HEADS)
    sums = table_call((db0, db1, db2), grad_up, grad_down, small, in01, in2, one, peaks, after)
    if quick:
        sums, lower_grad = together(chains, sums, lower_grad)
    every = Everywhere(sums)
    chains.append(every)
    while not all(c.done for c in chains):
        together(chains)
    sums = every.value

    place = jnp.stack([me, core, shard]).astype(jnp.int32)
    (grad_inbias, grad_outbias, grad_upbias, grad_downbias, grad_gain_1, grad_shift_1, grad_gain_2, grad_shift_2, grad_table,
     clipped, factors, maxima) = vector_finish(place, sums, threshold, inner_weight, shard_count)

    if quick:
        (rm, em), (ro, eo) = feed.keep, feed.flying
        grad_expand, grad_reduce = feed_finish(spot, em, eo, rm, ro)
        grad_inner, grad_outer = inner_finish(spot, ahead.keep + rest.keep, ahead.flying + rest.flying)
    else:
        def halves(keep, send, axis):
            lo = jnp.where(core == 0, keep, send)
            hi = jnp.where(core == 0, send, keep)
            return jnp.concatenate([lo, hi], axis=axis)

        def whole(keep, send):
            both = halves(keep[:, :, :, None], send[:, :, :, None], 3)
            return both.transpose(0, 2, 1, 3, 4).reshape(D, -1)

        def settle(v):
            v = lax.psum_scatter(v.astype(BF), "shard", scatter_dimension=0, tiled=True)
            return lax.psum(v, ("replica", "half")).astype(F32)

        def rows_of(v):
            return straight(v).reshape(4, 1, 2, 2, OWN, CH).transpose(0, 1, 2, 4, 3, 5).reshape(4, 1, CH, D)

        def straight(v):
            return jnp.stack([v[0], v[2], v[1], v[3]])

        grad_reduce = settle(halves(rows_of(r_keep), rows_of(r_send), 1).reshape(FF, D))
        grad_expand = settle(whole(e_keep, e_send))
        grad_outer = settle(whole(out_keep, out_send))
        by_third = [
            whole(straight(i0_keep), straight(i0_send)), whole(i1_keep, i1_send), whole(straight(i2_keep), straight(i2_send))
        ]
        by_third = jnp.stack(by_third, axis=1).reshape(D, 3, 3, LP).transpose(0, 2, 1, 3).reshape(D, 3 * D)
        grad_inner = settle(by_third)

    block_out = jnp.concatenate([lower_out, stay], axis=1).reshape(images.shape)
    grad_images = jnp.concatenate([lower_grad, gstay], axis=1).reshape(images.shape)
    return (
        block_out,
        grad_images,
        grad_inner,
        grad_inbias,
        grad_outer,
        grad_outbias,
        grad_expand,
        grad_upbias,
        grad_reduce,
        grad_downbias,
        grad_gain_1,
        grad_shift_1,
        grad_gain_2,
        grad_shift_2,
        grad_table,
        clipped,
        factors,
        maxima,
    )


def solution(mesh):
    rows = P(("replica", "shard"), "half", None, None)
    cut = P("shard", None)
    line = P("shard")
    return jax.shard_map(
        shards,
        mesh=mesh,
        in_specs=(rows, rows, P(("replica", "shard")), P(), cut, line, cut, line, cut, line, cut, line, line, line, line,
                  line, P()),
        out_specs=(rows, rows, cut, line, cut, line, cut, line, cut, line, line, line, line, line, P(), cut, P(), P()),
        check_vma=False,
    )
```

```python
import functools
import math

import numpy as np
import jax
import jax.numpy as jnp
from jax import lax
from jax.experimental import pallas as pl
from jax.experimental.pallas import tpu as pltpu
from jax.sharding import PartitionSpec as P

D = 768
HEADS = 24
HD = 32
WIN = 12
GRID = 24
SHIFT = 6
FF = 3072
TOK = WIN * WIN
ROWS = WIN * GRID
SPAN = 2 * WIN - 1
EPS = 1e-5
MASKED = -100.0
NEGATIVE = -1e30
LOG2E = math.log2(math.e)
BF = jnp.bfloat16
F32 = jnp.float32
MB = 1 << 20
OWN = 192
CH = 384
WIDE = 640
NARROW = 384
TALL = WIN * 16
HB = 8
LB = HB * HD
HP = 8
LP = HP * HD
NB = 576
SCALE = 1e-3
ONE = dict(pipeline_mode=pl.Buffered(1))
SD = jax.ShapeDtypeStruct


def nn(a, b):
    return lax.dot_general(a, b, (((1,), (0,)), ((), ())), preferred_element_type=F32)


def nt(a, b):
    return lax.dot_general(a, b, (((1,), (1,)), ((), ())), preferred_element_type=F32)


def tn(a, b):
    return lax.dot_general(a, b, (((0,), (0,)), ((), ())), preferred_element_type=F32)


def full(shape, **kw):
    return pl.BlockSpec(shape, lambda *_: (0,) * len(shape), **kw)


def any_space():
    return pl.BlockSpec(memory_space=pl.ANY)


def smem():
    return pl.BlockSpec(memory_space=pltpu.SMEM)


def run(kernel, count, args, after, in_specs, **kw):
    def body(*refs):
        kernel(*refs[:count], *refs[count + len(after) :])

    return pl.pallas_call(body, in_specs=list(in_specs) + [any_space()] * len(after), **kw)(*args, *after)


def params(limit=60):
    return pltpu.CompilerParams(vmem_limit_bytes=limit * MB)


def cost(flops, moved, exps=0):
    return pl.CostEstimate(flops=int(flops * SCALE), bytes_accessed=int(moved * SCALE), transcendentals=0)


def whole(array):
    return full(array.shape, **ONE)


def single(kernel, args, out_shape, after=(), scratch=(), **kw):
    specs = [smem() if v.dtype == jnp.int32 else whole(v) for v in args]
    shapes = out_shape if isinstance(out_shape, (list, tuple)) else [out_shape]
    out = run(
        kernel, len(args), args, after, grid=(1,), in_specs=specs, out_specs=[whole(v) for v in shapes], out_shape=list(shapes),
        scratch_shapes=list(scratch), compiler_params=params(), **kw
    )
    return out if isinstance(out_shape, (list, tuple)) else out[0]


def colsum(v):
    return jnp.sum(v, axis=0, keepdims=True)


def norm_parts(x):
    c = x - jnp.mean(x, axis=-1, keepdims=True)
    r = lax.rsqrt(jnp.mean(c * c, axis=-1, keepdims=True) + EPS)
    return c * r, r


def row_order():
    cells = np.arange(ROWS)
    win, rest = cells // TOK, cells % TOK
    a, b = rest // WIN, rest % WIN
    m = np.zeros((ROWS, ROWS), np.float32)
    m[cells, a * GRID + (win * WIN + b + SHIFT) % GRID] = 1
    return m


def spread_q():
    q = np.arange(TOK)
    m = np.zeros((TOK, NARROW), np.float32)
    m[q, SPAN * (q // WIN) + q % WIN] = 1
    return m


def spread_k(reverse):
    k = np.arange(TOK)
    b = k % WIN
    m = np.zeros((TALL, TOK), np.float32)
    m[16 * (k // WIN) + (WIN - 1 - b if reverse else b), k] = 1
    return m


def copies(plan, refs, at, targets, sems):
    for i, (src, row, rows, col, cols, dst, put) in enumerate(plan):
        place = pl.ds(pl.multiple_of(at[i], 16), rows)
        yield pltpu.make_async_copy(
            refs[src].at[pl.ds(row, rows), pl.ds(col, cols)], targets[dst].at[place, pl.ds(put, cols)], sems.at[i]
        )


def hidden_block(k):
    return 2 * (k % 4) + k // 4


def region_masks():
    line = np.arange(GRID)
    region = (line >= GRID - WIN).astype(np.int32) + (line >= GRID - SHIFT).astype(np.int32)
    lab = 3 * region[:, None] + region[None, :]
    lab = lab.reshape(2, WIN, 2, WIN).transpose(0, 2, 1, 3).reshape(2, 2, TOK)
    return np.where(lab[:, :, :, None] != lab[:, :, None, :], MASKED, 0.0).astype(np.float32)


def bias_kernel(spot_ref, table_ref, mask_ref, sq_ref, sk_ref, out_ref, tall):
    masks = [mask_ref[spot_ref[1], w].astype(F32) for w in range(2)]
    for h in range(HP):
        row = pltpu.roll(jnp.broadcast_to(table_ref[h : h + 1, :], (16, WIDE)), 0, 1, stride=1, stride_axis=0)
        for a in range(WIN):
            off = (SPAN * a - SPAN * (WIN - 1) - (WIN - 1)) % WIDE
            tall[16 * a : 16 * a + 16, :] = pltpu.roll(row, off, 1)[:, :NARROW].astype(BF)
        wide = nn(tall[...], sq_ref[...]).astype(BF)
        bias = nn(sk_ref[...], wide)
        for w in range(2):
            out_ref[w, h] = (bias + masks[w]) * LOG2E


def bias_call(group, spot, table):
    args = (spot, table, jnp.asarray(region_masks(), BF), jnp.asarray(spread_q().T, BF), jnp.asarray(spread_k(False).T, BF))
    out = SD((2, HP, TOK, TOK), F32)
    return pl.pallas_call(
        bias_kernel,
        grid=(1,),
        in_specs=[smem(), pl.BlockSpec((HP, WIDE), lambda i: (group, 0))] + [whole(v) for v in args[2:]],
        out_specs=whole(out),
        out_shape=out,
        scratch_shapes=[pltpu.VMEM((TALL, NARROW), BF)],
        compiler_params=params(),
        cost_estimate=cost(2e9, 3 * MB),
        name="bias",
    )(*args)


V_UP, V_SMALL, V_IN, V_ONE, V_PEAK, V_TABLE, V_ROWS = 0, 4, 8, 11, 13, 16, 40


def table_kernel(db0_ref, db1_ref, db2_ref, up_ref, down_ref, small_ref, in01_ref, in2_ref, one_ref, peak_ref, sq_ref, sk_ref, out_ref):
    def split(v):
        hi = v.astype(BF)
        return hi, (v - hi.astype(F32)).astype(BF)

    out_ref[...] = jnp.zeros_like(out_ref)
    for k in range(8):
        b = hidden_block(k)
        out_ref[V_UP + b // 2 : V_UP + b // 2 + 1, (b % 2) * CH : (b % 2 + 1) * CH] = up_ref[
            k // 2, :, (k % 2) * CH : (k % 2 + 1) * CH
        ]
    out_ref[V_SMALL : V_SMALL + 1, :] = down_ref[...]
    out_ref[V_SMALL + 1 : V_SMALL + 4, :] = small_ref[1:4, :]
    for p in range(3):
        row = in01_ref[p] if p < 2 else in2_ref[0]
        for k in range(3):
            out_ref[V_IN + k : V_IN + k + 1, p * LP : (p + 1) * LP] = row[:, k * LP : (k + 1) * LP]
    out_ref[V_ONE : V_ONE + 2, :] = one_ref[0:2, :]
    out_ref[V_PEAK : V_PEAK + 1, :HEADS] = peak_ref[...]
    for h in range(HEADS):
        hi, lo = split((db0_ref, db1_ref, db2_ref)[h // HP][h % HP])
        tall = nn(sk_ref[...], hi) + nn(sk_ref[...], lo)
        hi, lo = split(tall)
        wide = nn(hi, sq_ref[...]) + nn(lo, sq_ref[...])
        wide = jnp.concatenate([wide, jnp.zeros((TALL, WIDE - NARROW), F32)], axis=1)
        tot = jnp.zeros((16, WIDE), F32)
        for a in range(WIN):
            tot = tot + pltpu.roll(wide[16 * a : 16 * a + 16, :], SPAN * (WIN - 1 - a), 1)
        tot = pltpu.roll(tot, 0, 1, stride=1, stride_axis=0)
        out_ref[V_TABLE + h : V_TABLE + h + 1, :WIDE] = colsum(tot)


def table_call(dbs, up, down, small, in01, in2, one, peaks, after):
    args = (*dbs, up, down, small, in01, in2, one, peaks, jnp.asarray(spread_q(), BF), jnp.asarray(spread_k(True), BF))
    return single(table_kernel, args, SD((V_ROWS, D), F32), after, cost_estimate=cost(6e9, 4 * MB), name="table")


def lane_head(shape):
    return lax.broadcasted_iota(jnp.int32, shape, len(shape) - 1) // HD


VECTORS = (2 * D, D, FF, D, D, D, D, D)


def first_kernel(spot_ref, *refs):
    vecs, (inner_ref, own_ref, gown_ref, first_ref, others_ref, half_ref, up_ref) = refs[:8], refs[8:]
    n = own_ref.shape[0]
    up_ref[:n] = own_ref[...]
    up_ref[n:] = gown_ref[...]
    mine = pl.ds(pl.multiple_of(spot_ref[1] * (OWN // 2), 16), OWN // 2)
    for k in range(3):
        first_ref[:OWN, k * LP : (k + 1) * LP] = inner_ref[:, k * D : k * D + LP]
        for p in (1, 2):
            src = slice(k * D + p * LP, k * D + (p + 1) * LP)
            dst = slice(((p - 1) * 3 + k) * LP, ((p - 1) * 3 + k + 1) * LP)
            others_ref[:, dst] = inner_ref[:, src]
            half_ref[:, dst] = inner_ref[mine, src]
    rows = [jnp.zeros((8, D), F32)]
    for v in vecs:
        row = v[...].astype(F32).reshape(1, v.shape[0])
        if v.shape[0] < D:
            row = jnp.concatenate([row, jnp.zeros((1, D - v.shape[0]), F32)], axis=1)
        rows.insert(-1, row)
    first_ref[OWN:, :] = jnp.concatenate(rows, axis=0).astype(BF)


def first_call(spot, vectors, inner, own, gown):
    n = own.shape[0]
    top = full((n, TOK, D))
    shapes = [SD((OWN + 16, D), BF), SD((OWN, 6 * LP), BF), SD((OWN // 2, 6 * LP), BF), SD((2 * n, TOK, D), BF)]
    return pl.pallas_call(
        first_kernel,
        grid=(1,),
        in_specs=[smem()] + [whole(v) for v in vectors] + [whole(inner), top, top],
        out_specs=[whole(v) for v in shapes],
        out_shape=shapes,
        compiler_params=params(),
        cost_estimate=cost(1e6, 6 * MB),
        name="first",
    )(spot, *vectors, inner, own, gown)


BIG = 4 * (OWN // 2) + OWN // 2 + 2 * OWN


def cut_kernel(spot_ref, outer_ref, expand_ref, reduce_ref, big_ref):
    core = spot_ref[1]
    hlf = OWN // 2
    mine = pl.ds(pl.multiple_of(core * hlf, 16), hlf)
    for k in range(4):
        big_ref[k * hlf : (k + 1) * hlf, :] = expand_ref[mine, k * D : (k + 1) * D]
    big_ref[4 * hlf : 5 * hlf, :] = outer_ref[mine, :]
    big_ref[5 * hlf :, :] = reduce_ref[pl.ds(pl.multiple_of(core * 2 * OWN, 16), 2 * OWN), :]


def cut_call(spot, outer, expand, reduce):
    return single(
        cut_kernel, (spot, outer, expand, reduce), [SD((BIG, D), BF)], cost_estimate=cost(1e6, 3 * MB), name="cut"
    )[0]


def prep_kernel(own_ref, gown_ref, recv_ref, alive_ref, pm_ref, tok_ref, g_ref, sum_ref):
    n = own_ref.shape[0]
    tot = jnp.zeros((1, D), F32)
    for i in range(n):
        tok_ref[i] = nn(pm_ref[...], jnp.concatenate([own_ref[i, TOK:, :], recv_ref[i]], axis=0)).astype(BF)
        g = nn(pm_ref[...], jnp.concatenate([gown_ref[i, TOK:, :], recv_ref[n + i]], axis=0)) * alive_ref[0:1, i : i + 1]
        g_ref[i] = g.astype(BF)
        tot = tot + colsum(g)
    sum_ref[...] = tot


def prep_call(own, gown, recv, alive, pm):
    rows = SD(own.shape, BF)
    return single(
        prep_kernel, (own, gown, recv, alive, pm), [rows, rows, SD((1, D), F32)], cost_estimate=cost(3e9, 16 * MB), name="prep"
    )


def vector_kernel(spot_ref, pa_ref, pb_ref, pc_ref, pd_ref, tok_ref, inb_ref, up_ref, vec_ref, n1_ref, n1t_ref, parts):
    n = tok_ref.shape[0]
    for r, ref in enumerate((pa_ref, pb_ref, pc_ref, pd_ref)):
        parts[jnp.bitwise_xor(spot_ref[0], r)] = ref[:8, :].astype(F32)

    def vector(i):
        size = VECTORS[i] // 4
        return jnp.concatenate([parts[s][i : i + 1, :size] for s in range(4)], axis=1)

    vin = vector(0)
    for p in range(3):
        inb_ref[p] = jnp.concatenate(
            [vin[:, p * LP : (p + 1) * LP], jnp.zeros((1, LP), F32), vin[:, D + p * LP : D + (p + 1) * LP]], axis=1
        )
    vup = vector(2)
    for k in range(8):
        up_ref[k // 2, :, (k % 2) * CH : (k % 2 + 1) * CH] = vup[:, hidden_block(k) * CH : (hidden_block(k) + 1) * CH]
    gain, shift = vector(4), vector(5)
    vec_ref[...] = jnp.zeros_like(vec_ref)
    for r, v in enumerate((vector(1), vector(3), gain, vector(6), vector(7))):
        vec_ref[r : r + 1, :] = v
    for i in range(n):
        xh, _ = norm_parts(tok_ref[i].astype(F32))
        n1 = (xh * gain + shift).astype(BF)
        n1_ref[i] = n1
        n1t_ref[:, i * ROWS : (i + 1) * ROWS] = n1.T


def vector_call(spot, parts, tok):
    n = tok.shape[0]
    last = parts[0].shape[0] // 16 - 1
    shapes = [SD((3, 1, 3 * LP), F32), SD((4, 1, 2 * CH), F32), SD((8, D), F32), SD(tok.shape, BF), SD((D, n * ROWS), BF)]
    return pl.pallas_call(
        vector_kernel,
        grid=(1,),
        in_specs=[smem()] + [pl.BlockSpec((16, D), lambda i: (last, 0))] * 4 + [whole(tok)],
        out_specs=[whole(v) for v in shapes],
        out_shape=shapes,
        scratch_shapes=[pltpu.VMEM((4, 8, D), F32)],
        compiler_params=params(),
        cost_estimate=cost(5e9, 8 * MB),
        name="vectors",
    )(spot, *parts, tok)


def attend_kernel(plan, count, n1_ref, b_ref, bm_ref, at_ref, *rest):
    pieces = rest[:count]
    proj_ref, pt_ref, att_ref, peak_ref, w_ref, sems = rest[count:]

    @pl.when(pl.program_id(0) == 0)
    def _():
        for c in copies(plan, pieces, at_ref, (w_ref,), sems):
            c.start()
        for c in copies(plan, pieces, at_ref, (w_ref,), sems):
            c.wait()

    proj_ref[0] = (nn(n1_ref[0], w_ref[...]) + b_ref[0]).astype(BF)
    hid = lane_head((TOK, LB))
    scale = HD**-0.5
    for w in range(2):
        r = slice(w * TOK, (w + 1) * TOK)
        for blk in range(LP // LB):
            l = blk * LB
            q = proj_ref[0, r, l : l + LB]
            k = proj_ref[0, r, LP + l : LP + l + LB]
            v = proj_ref[0, r, 2 * LP + l : 2 * LP + l + LB]
            vt = v.T
            apart = jnp.concatenate([jnp.where(hid == h, k, jnp.zeros_like(k)) for h in range(HB)], axis=0)
            sts = nn(apart, q.T)
            outs = []
            for h in range(HB):
                hh = blk * HB + h
                st = sts[h * TOK : (h + 1) * TOK]
                peak_ref[0, w, hh : hh + 1, :] = jnp.max(st, axis=0, keepdims=True) * scale
                t = st * (scale * LOG2E) + bm_ref[w, hh]
                e = jnp.exp2(t - jnp.max(t, axis=0, keepdims=True))
                p = (e * (1.0 / colsum(e))).astype(BF)
                pt_ref[0, w, hh] = p
                outs.append(nn(vt[HD * h : HD * h + HD, :], p))
            att_ref[0, r, l : l + LB] = jnp.concatenate(outs, axis=0).astype(BF).T


def attend_call(group, n1, b, bm, at, plan, pieces, after):
    n = n1.shape[0]

    def blk(*s):
        return pl.BlockSpec((1,) + s, lambda i: (i,) + (0,) * len(s))

    return run(
        functools.partial(attend_kernel, plan, len(pieces)), 4 + len(pieces), (n1, b, bm, at, *pieces), after,
        grid=(n,),
        in_specs=[blk(ROWS, D), pl.BlockSpec((1, 1, 3 * LP), lambda i: (group, 0, 0)), full((2, HP, TOK, TOK), **ONE), smem()]
        + [any_space()] * len(pieces),
        out_specs=[blk(ROWS, 3 * LP), blk(2, HP, TOK, TOK), blk(ROWS, LP), blk(2, HP, TOK), full((D, 3 * LP), **ONE)],
        out_shape=[SD((n, ROWS, 3 * LP), BF), SD((n, 2, HP, TOK, TOK), BF), SD((n, ROWS, LP), BF), SD((n, 2, HP, TOK), F32),
                   SD((D, 3 * LP), BF)],
        scratch_shapes=[pltpu.SemaphoreType.DMA((len(plan),))],
        compiler_params=params(),
        cost_estimate=cost(1.3e10, 12 * MB, 1.4e6),
        name="attend",
    )


def gelu_parts(h):
    d = 1.0 + (0.3275911 * 0.5**0.5) * jnp.abs(h)
    t = pl.reciprocal(d, approx=True)
    t = t * (2.0 - d * t)
    e = jnp.exp2(h * h * (-0.5 * LOG2E))
    p = (((0.5 * 1.061405429) * t - 0.5 * 1.453152027) * t + 0.5 * 1.421413741) * t - 0.5 * 0.284496736
    p = (p * t + 0.5 * 0.254829592) * t * e
    cdf = jnp.where(h >= 0, 1.0 - p, p)
    return cdf, cdf + h * (e * ((2 * math.pi) ** -0.5))


def middle_kernel(plan, count, spot_ref, tok_ref, att0_ref, att1_ref, att2_ref, gin_ref, pmt_ref, vec_ref, eb_ref,
                  at_ref, *rest):
    pieces = rest[:count]
    (stay_ref, send_ref, gmid_ref, datt_ref, os_ref, ok_ref, es_ref, ek_ref, rs_ref, rk_ref, geb_ref, small_ref,
     wo, we, wr, mid, n2, g, n2t, acc, e2, act, gh, sems) = rest[count:]
    j = pl.program_id(0)
    n = tok_ref.shape[0]
    N = n * ROWS
    me = spot_ref[0]
    core = spot_ref[1]
    early = [k for k, entry in enumerate(plan) if entry[5] == 0]
    out_b, red_b, gain, shift = vec_ref[0:1, :], vec_ref[1:2, :], vec_ref[3:4, :], vec_ref[4:5, :]

    def attended(i):
        return jnp.concatenate([att0_ref[i], att1_ref[i], att2_ref[i]], axis=-1)

    @pl.when(j == 0)
    def _():
        moves = list(copies(plan, pieces, at_ref, (wo, we, wr), sems))
        for c in moves:
            c.start()
        for k in early:
            moves[k].wait()
        for i in range(n):
            s = slice(i * ROWS, (i + 1) * ROWS)
            g[s, :] = gin_ref[i]
            m = tok_ref[i].astype(F32) + nn(attended(i), wo[...]) + out_b
            mid[s, :] = m
            xh, _ = norm_parts(m)
            x2 = (xh * gain + shift).astype(BF)
            n2[s, :] = x2
            n2t[:, s] = x2.T
            acc[s, :] = m + red_b
            e2[s, :] = jnp.zeros((ROWS, D), F32)
        for k, c in enumerate(moves):
            if k not in early:
                c.wait()

    at = pl.multiple_of((2 * jnp.bitwise_xor(core, 1 - j // 2) + j % 2) * 2 * CH, 2 * CH)
    cols = pl.ds(at, 2 * CH)
    tot = jnp.zeros((1, 2 * CH), F32)
    for s0 in range(0, N, NB):
        s = slice(s0, s0 + NB)
        h = nn(n2[s, :], we[:, cols]) + eb_ref[0]
        cdf, dg = gelu_parts(h)
        act[s, :] = (h * cdf).astype(BF)
        x = (nt(g[s, :], wr[cols, :]) * dg).astype(BF)
        gh[s, :] = x
        tot = tot + colsum(x.astype(F32))
    geb_ref[0] = tot
    ge = nn(n2t[...], gh[...]).astype(BF)
    gr = tn(act[...], g[...]).astype(BF)

    def put(e_ref, r_ref):
        for t in range(2):
            for b in range(4):
                e_ref[crossed(jnp.bitwise_xor(me, b)), t] = ge[b * OWN : (b + 1) * OWN, t * CH : (t + 1) * CH]
                r_ref[jnp.bitwise_xor(me % 2, t), b] = gr[
                    t * CH + (b // 2) * OWN : t * CH + (b // 2 + 1) * OWN, (b % 2) * CH : (b % 2 + 1) * CH
                ]

    @pl.when(j < 2)
    def _():
        put(es_ref, rs_ref)

    @pl.when(j >= 2)
    def _():
        put(ek_ref, rk_ref)

    for s0 in range(0, N, NB):
        s = slice(s0, s0 + NB)
        acc[s, :] += nn(act[s, :], wr[cols, :])
        e2[s, :] += nt(gh[s, :], we[:, cols])

    @pl.when(j == 3)
    def _():
        gn = jnp.zeros((1, D), F32)
        shf = gn
        ob = gn
        for i in range(n):
            s = slice(i * ROWS, (i + 1) * ROWS)
            o = nn(pmt_ref[...], acc[s, :].astype(BF)).astype(BF)
            stay_ref[i] = o[:TOK]
            send_ref[i] = o[TOK:]
            xh, r = norm_parts(mid[s, :])
            d = e2[s, :]
            gn = gn + colsum(d * xh)
            shf = shf + colsum(d)
            d = d * gain
            gm = g[s, :].astype(F32) + r * (
                d - jnp.mean(d, axis=-1, keepdims=True) - xh * jnp.mean(d * xh, axis=-1, keepdims=True)
            )
            gmid_ref[i] = gm
            gb = gm.astype(BF)
            ob = ob + colsum(gb.astype(F32))
            g[s, :] = gb
            datt_ref[i] = nt(gb, wo[...]).astype(BF)
            n2[s, :] = attended(i)
        for c, ref in ((1 - core, os_ref), (core, ok_ref)):
            go = tn(n2[...], g[:, pl.ds(pl.multiple_of(c * CH, 128), CH)]).astype(BF)
            for b in range(4):
                ref[jnp.bitwise_xor(me, b), 0] = go[b * OWN : (b + 1) * OWN, :]
        small_ref[1:2, :] = gn
        small_ref[2:3, :] = shf
        small_ref[3:4, :] = ob


def crossed(r):
    return 2 * (r % 2) + r // 2


def middle_call(spot, tok, atts, g, pmt, vecs, eb, at, plan, pieces, after):
    n = tok.shape[0]
    N = n * ROWS
    blocks = SD((4, 4, OWN, CH), BF)

    def chunk(j, spot):
        return 2 * jnp.bitwise_xor(spot[1], 1 - j // 2) + j % 2

    def early(j):
        return jnp.minimum(j, 1)

    def late(j):
        return jnp.maximum(j, 2) - 2

    rows = full((n, ROWS, D), **ONE)
    third = full((n, ROWS, LP), **ONE)
    cut = full((n, TOK, D), **ONE)
    outer = full((4, 1, OWN, CH), **ONE)
    args = (spot, tok, *atts, g, pmt, vecs, eb, at, *pieces)

    def body(*refs):
        middle_kernel(plan, len(pieces), *refs[: len(args)], *refs[len(args) + len(after) :])

    grid_spec = pltpu.PrefetchScalarGridSpec(
        num_scalar_prefetch=1,
        grid=(4,),
        in_specs=[rows, third, third, third, rows, full((ROWS, ROWS)), full((8, D)),
                  pl.BlockSpec((1, 1, 2 * CH), lambda j, spot: (chunk(j, spot), 0, 0)), smem()]
        + [any_space()] * (len(pieces) + len(after)),
        out_specs=[cut, cut, rows, rows, outer, outer,
                   pl.BlockSpec((4, 2, OWN, CH), lambda j, spot: (0, early(j), 0, 0)),
                   pl.BlockSpec((4, 2, OWN, CH), lambda j, spot: (0, late(j), 0, 0)),
                   pl.BlockSpec((2, 4, OWN, CH), lambda j, spot: (jnp.bitwise_xor(early(j), spot[0] // 2), 0, 0, 0)),
                   pl.BlockSpec((2, 4, OWN, CH), lambda j, spot: (jnp.bitwise_xor(late(j), spot[0] // 2), 0, 0, 0)),
                   pl.BlockSpec((1, 1, 2 * CH), lambda j, spot: (chunk(j, spot), 0, 0)), full((8, D))],
        scratch_shapes=[pltpu.VMEM((D, D), BF), pltpu.VMEM((D, FF), BF), pltpu.VMEM((FF, D), BF),
                        pltpu.VMEM((N, D), F32), pltpu.VMEM((N, D), BF), pltpu.VMEM((N, D), BF), pltpu.VMEM((D, N), BF),
                        pltpu.VMEM((N, D), F32), pltpu.VMEM((N, D), F32), pltpu.VMEM((N, 2 * CH), BF), pltpu.VMEM((N, 2 * CH), BF),
                        pltpu.SemaphoreType.DMA((len(plan),))],
    )
    return pl.pallas_call(
        body,
        grid_spec=grid_spec,
        out_shape=[SD((n, TOK, D), BF), SD((n, TOK, D), BF), SD((n, ROWS, D), F32), SD((n, ROWS, D), BF),
                   SD((4, 1, OWN, CH), BF), SD((4, 1, OWN, CH), BF), blocks, blocks, blocks, blocks,
                   SD((4, 1, 2 * CH), F32), SD((8, D), F32)],
        compiler_params=params(62),
        cost_estimate=cost(6e10, 40 * MB, 7e6),
        name="middle",
    )(*args, *after)


def back_kernel(proj_ref, pt_ref, da_ref, gp_ref, db_ref):
    @pl.when(pl.program_id(0) == 0)
    def _():
        db_ref[...] = jnp.zeros_like(db_ref)

    hid = lane_head((TOK, LB))
    scale = HD**-0.5
    for w in range(2):
        r = slice(w * TOK, (w + 1) * TOK)
        for blk in range(LP // LB):
            l = blk * LB
            q = proj_ref[0, r, l : l + LB]
            k = proj_ref[0, r, LP + l : LP + l + LB]
            v = proj_ref[0, r, 2 * LP + l : 2 * LP + l + LB]
            do = da_ref[0, r, l : l + LB]
            qt, kt, dt = q.T, k.T, do.T
            dq, dk, dv = [], [], []
            dps = nn(jnp.concatenate([jnp.where(hid == h, v, jnp.zeros_like(v)) for h in range(HB)], axis=0), dt)
            for h in range(HB):
                hh = blk * HB + h
                s = slice(HD * h, HD * h + HD)
                dp = dps[h * TOK : (h + 1) * TOK]
                pb = pt_ref[0, w, hh]
                p = pb.astype(F32)
                pd = p * dp
                ds = pd - p * colsum(pd)
                db_ref[hh] += ds
                dsb = ds.astype(BF)
                dq.append(nn(kt[s, :], dsb))
                dk.append(nt(qt[s, :], dsb))
                dv.append(nt(dt[s, :], pb))
            gp_ref[0, r, l : l + LB] = (jnp.concatenate(dq, axis=0) * scale).astype(BF).T
            gp_ref[0, r, LP + l : LP + l + LB] = (jnp.concatenate(dk, axis=0) * scale).astype(BF).T
            gp_ref[0, r, 2 * LP + l : 2 * LP + l + LB] = jnp.concatenate(dv, axis=0).astype(BF).T


def back_call(group, proj, pt, da, after):
    n = proj.shape[0]

    def blk(*s):
        return pl.BlockSpec((1,) + s, lambda i: (i,) + (0,) * len(s))

    return run(
        back_kernel, 3, (proj, pt, da), after,
        grid=(n,),
        in_specs=[blk(ROWS, 3 * LP), blk(2, HP, TOK, TOK), pl.BlockSpec((1, ROWS, LP), lambda i: (i, 0, group))],
        out_specs=[blk(ROWS, 3 * LP), full((HP, TOK, TOK))],
        out_shape=[SD((n, ROWS, 3 * LP), BF), SD((HP, TOK, TOK), F32)],
        compiler_params=params(),
        cost_estimate=cost(1.8e10, 10 * MB),
        name="attend_back",
    )


def inner_kernel(spot_ref, n1t_ref, *rest):
    me = spot_ref[0]
    core = spot_ref[1]
    gp_refs, outs, sum_ref = rest[: len(rest) // 3], rest[len(rest) // 3 : -1], rest[-1]
    for k, gp_ref in enumerate(gp_refs):
        n = gp_ref.shape[0]
        gp = gp_ref[...].reshape(n * ROWS, 3 * LP)
        sum_ref[k] = colsum(gp.astype(F32))
        gi = nn(n1t_ref[...], gp).astype(BF)
        send, keep = outs[2 * k], outs[2 * k + 1]

        for c in range(2):
            @pl.when(core == c)
            def _():
                for b in range(4):
                    r = slice(b * OWN, (b + 1) * OWN)
                    rel = jnp.bitwise_xor(me, b)
                    rel = crossed(rel) if k == 0 else rel
                    keep[rel, 0] = gi[r, c * CH : (c + 1) * CH]
                    send[rel, 0] = gi[r, (1 - c) * CH : (2 - c) * CH]


def inner_call(spot, n1t, gps, after):
    block = SD((4, 1, OWN, CH), BF)
    return single(
        inner_kernel, (spot, n1t, *gps), [block] * (2 * len(gps)) + [SD((len(gps), 1, 3 * LP), F32)], after,
        cost_estimate=cost(4e9 * len(gps), 6 * MB), name="inner_grad",
    )


def last_kernel(tok_ref, gmid_ref, vec_ref, pmt_ref, gp0_ref, gp1_ref, gp2_ref, w0_ref, w1_ref, w2_ref,
                small_ref, stay_ref, send_ref):
    @pl.when(pl.program_id(0) == 0)
    def _():
        small_ref[...] = jnp.zeros_like(small_ref)

    d = nt(gp0_ref[0], w0_ref[...]) + nt(gp1_ref[0], w1_ref[...]) + nt(gp2_ref[0], w2_ref[...])
    xh, r = norm_parts(tok_ref[0].astype(F32))
    small_ref[0:1, :] += colsum(d * xh)
    small_ref[1:2, :] += colsum(d)
    d = d * vec_ref[2:3, :]
    gm = gmid_ref[0] + r * (d - jnp.mean(d, axis=-1, keepdims=True) - xh * jnp.mean(d * xh, axis=-1, keepdims=True))
    o = nn(pmt_ref[...], gm.astype(BF)).astype(BF)
    stay_ref[0] = o[:TOK]
    send_ref[0] = o[TOK:]


def last_call(tok, gmid, gain, pmt, gps, ws, after):
    n = tok.shape[0]

    def blk(*s):
        return pl.BlockSpec((1,) + s, lambda i: (i,) + (0,) * len(s))

    return run(
        last_kernel, 10, (tok, gmid, gain, pmt, *gps, *ws), after,
        grid=(n,),
        in_specs=[blk(ROWS, D), blk(ROWS, D), full((8, D)), full((ROWS, ROWS))] + [blk(ROWS, 3 * LP)] * 3
        + [full((D, 3 * LP), **ONE)] * 3,
        out_specs=[full((8, D)), blk(TOK, D), blk(TOK, D)],
        out_shape=[SD((8, D), F32), SD((n, TOK, D), BF), SD((n, TOK, D), BF)],
        compiler_params=params(),
        cost_estimate=cost(2e10, 20 * MB),
        name="last",
    )


def vector_finish_kernel(count, spot_ref, sums_ref, thr_ref, inner_ref, inb_ref, outb_ref, upb_ref, downb_ref, g1_ref, s1_ref,
                         g2_ref, s2_ref, table_ref, clip_ref, factor_ref, max_ref):
    shard = spot_ref[2]

    def part(ref, rows, step=1):
        size = ref.shape[0]
        start = shard * size
        row = sums_ref[pl.ds(rows + step * (start // D), 1), :]
        row = jnp.broadcast_to(row, (8, D))
        ref[...] = pltpu.roll(row, D - start % D, 1)[0:1, :size].reshape(size)

    part(inb_ref, V_IN, 2)
    part(upb_ref, V_UP)
    for i, ref in enumerate((downb_ref, g2_ref, s2_ref, outb_ref)):
        part(ref, V_SMALL + i)
    part(g1_ref, V_ONE)
    part(s1_ref, V_ONE + 1)
    table_ref[...] = sums_ref[V_TABLE : V_TABLE + HEADS, :WIDE].T[: SPAN * SPAN, :]
    top = sums_ref[V_PEAK : V_PEAK + 1, :HEADS]
    factor = thr_ref[...].reshape(1, HEADS)
    factor = factor / jnp.maximum(top, factor)
    max_ref[...] = top.reshape(HEADS)
    factor_ref[...] = factor.reshape(HEADS)
    root = jnp.broadcast_to(jnp.sqrt(factor), (8, HEADS))
    head = lax.broadcasted_iota(jnp.int32, (HEADS, D), 0)
    col = lax.broadcasted_iota(jnp.int32, (HEADS, D), 1) // HD
    scale = lax.dot_general(root, (head == col).astype(F32), (((1,), (0,)), ((), ())), preferred_element_type=F32,
                            precision=lax.Precision.HIGHEST)[0:1, :]
    for k in range(2):
        clip_ref[:, k * D : (k + 1) * D] = (inner_ref[:, k * D : (k + 1) * D].astype(F32) * scale).astype(BF)
    clip_ref[:, 2 * D :] = inner_ref[:, 2 * D :]


def vector_finish(place, sums, threshold, inner, count):
    line = SD((D // count,), F32)
    return single(
        functools.partial(vector_finish_kernel, count), (place, sums, threshold, inner),
        [SD((2 * D // count,), F32), line, SD((FF // count,), F32), line, line, line, line, line,
         SD((SPAN * SPAN, HEADS), F32), SD(inner.shape, BF), SD((HEADS,), F32), SD((HEADS,), F32)],
        cost_estimate=cost(1e7, 3 * MB), name="vector_finish",
    )


def feed_finish_kernel(spot_ref, em_ref, eo_ref, rm_ref, ro_ref, ge_ref, gr_ref):
    for core in range(2):
        @pl.when(spot_ref[1] == core)
        def _():
            for c, e_ref, r_ref in ((core, em_ref, rm_ref), (1 - core, eo_ref, ro_ref)):
                for b in range(4):
                    ge_ref[:, (2 * b + c) * CH : (2 * b + c + 1) * CH] = e_ref[b].astype(F32)
                    r = c * CH + (b // 2) * OWN
                    gr_ref[r : r + OWN, (b % 2) * CH : (b % 2 + 1) * CH] = r_ref[b].astype(F32)


def feed_finish(spot, em, eo, rm, ro):
    return single(
        feed_finish_kernel, (spot, em, eo, rm, ro), [SD((OWN, FF), F32), SD((2 * CH, D), F32)],
        cost_estimate=cost(1e7, 8 * MB), name="feed_finish",
    )


def inner_columns(p, c):
    if c == 0:
        return [(0, LP, p * LP), (LP, LP // 2, D + p * LP)]
    return [(0, LP // 2, D + p * LP + LP // 2), (LP // 2, LP, 2 * D + p * LP)]


def inner_finish_kernel(spot_ref, *refs):
    mine, other, (gi_ref, go_ref) = refs[:4], refs[4:8], refs[8:]
    for core in range(2):
        @pl.when(spot_ref[1] == core)
        def _():
            for c, blocks in ((core, mine), (1 - core, other)):
                for p in range(3):
                    for at, size, put in inner_columns(p, c):
                        gi_ref[:, put : put + size] = blocks[p][0, :, at : at + size].astype(F32)
                go_ref[:, c * CH : (c + 1) * CH] = blocks[3][0].astype(F32)


def inner_finish(spot, mine, other):
    return single(
        inner_finish_kernel, (spot, *mine, *other), [SD((OWN, 3 * D), F32), SD((OWN, D), F32)],
        cost_estimate=cost(1e7, 4 * MB), name="inner_finish",
    )


def swap(block, axis, bit):
    count = lax.axis_size(axis)
    return lax.ppermute(block, axis, [(i, i ^ bit) for i in range(count) if i ^ bit < count])


def everywhere_hops():
    for axis in ("half", "shard", "replica"):
        bit = 1
        while bit < lax.axis_size(axis):
            yield axis, bit
            bit *= 2


def join_vectors(a, b):
    row = lax.broadcasted_iota(jnp.int32, a.shape, 0)
    return jnp.where(row == V_PEAK, jnp.maximum(a, b), a + b)


class Everywhere:
    def __init__(self, value):
        self.value = value
        self.hops = list(everywhere_hops())
        self.flying = None
        self.step()

    def step(self):
        if self.flying is not None:
            self.value = join_vectors(self.value, self.flying)
            self.flying = None
        if self.hops:
            self.flying = swap(self.value, *self.hops.pop(0))
        return [self.value]

    @property
    def done(self):
        return self.flying is None


def near(block):
    return [swap(block, "shard", 1), swap(block, "shard", 2)]


def fence(*values):
    return lax.optimization_barrier(values)


def add(a, b):
    return (a.astype(F32) + b.astype(F32)).astype(BF)


class Reduction:
    def __init__(self, sends, keeps, replica, short):
        self.short = short
        self.low = (replica & 1) == 0
        self.low2 = (replica & 2) == 0
        self.keep = keeps
        self.sent = sends
        self.stage = 0
        self.flying = [swap(v, "half", 1) for v in sends]

    def step(self):
        hlf = OWN // 2
        got, low, low2 = self.flying, self.low, self.low2
        if self.stage == 0:
            self.sent = [add(k[2:], g[2:]) for k, g in zip(self.keep, got)]
            self.keep = [add(k[:2], g[:2]) for k, g in zip(self.keep, got)]
            self.flying = [swap(self.sent[0], "shard", 1), swap(self.sent[1], "shard", 2)]
        elif self.stage == 1:
            self.sent = [add(k[1], g[1]) for k, g in zip(self.keep, got)]
            self.keep = [add(k[0], g[0]) for k, g in zip(self.keep, got)]
            self.flying = [swap(self.sent[0], "shard", 2), swap(self.sent[1], "shard", 1)]
        elif self.stage == 2:
            a, b = (add(k, g) for k, g in zip(self.keep, got))
            self.keep = jnp.where(low, a, b)
            self.sent = [jnp.where(low, b, a)]
            self.flying = swap(self.sent[0], "replica", 1)
        elif self.stage == 3 and self.short:
            self.keep = add(self.keep, got)
            self.sent = [self.keep]
            self.flying = swap(self.keep, "replica", 2)
            self.stage = 4
        elif self.stage == 3:
            u = add(self.keep, got)
            self.keep = jnp.where(low2, u[:, :hlf], u[:, hlf:])
            self.sent = [jnp.where(low2, u[:, hlf:], u[:, :hlf])]
            self.flying = swap(self.sent[0], "replica", 2)
        elif self.stage == 4:
            self.keep = add(self.keep, got)
            self.sent = [self.keep]
            self.flying = swap(self.keep, "replica", 2)
        elif self.stage == 5:
            v = self.keep
            if self.short:
                self.keep = add(v, got)
            else:
                self.keep = jnp.concatenate([jnp.where(low2, v, got), jnp.where(low2, got, v)], axis=1)
            self.sent = [self.keep]
            self.flying = swap(self.keep, "replica", 1)
        elif self.stage == 6:
            v = self.keep
            self.keep = [jnp.where(low, v, got), jnp.where(low, got, v)]
            self.sent = self.keep
            self.flying = [swap(v, "half", 1) for v in self.keep]
        self.stage += 1
        return list(self.sent)

    @property
    def done(self):
        return self.stage == 7


def together(chains, *others):
    left = [c for c in chains if not c.done]
    flying, others = fence([c.flying for c in left], others)
    for c, v in zip(left, flying):
        c.flying = v
        c.step()
    return others


def shards(images, cotangent, present, threshold, inner_weight, inner_bias, outer_weight, outer_bias, expand_weight,
           expand_bias, reduce_weight, reduce_bias, first_gain, first_shift, second_gain, second_shift, bias_table):
    n = images.shape[0]
    core = lax.axis_index("half")
    shard = lax.axis_index("shard")
    replica = lax.axis_index("replica")
    shard_count = lax.axis_size("shard")
    quick = shard_count == 4 and lax.axis_size("replica") == 4
    me = shard if quick else jnp.int32(0)
    spot = jnp.stack([me, core]).astype(jnp.int32)
    own_images = images.reshape(n, ROWS, D)
    own_grad = cotangent.reshape(n, ROWS, D)
    vectors = (inner_bias, outer_bias, expand_bias, reduce_bias, first_gain, first_shift, second_gain, second_shift)
    order = jnp.asarray(row_order(), BF)
    back_order = jnp.asarray(row_order().T, BF)
    alive = present.astype(F32).reshape(1, n)
    table_rows = jnp.pad(bias_table.astype(F32).T, ((0, 0), (0, WIDE - bias_table.shape[0])))
    if quick:
        first, others, others_half, up = first_call(spot, vectors, inner_weight, own_images, own_grad)
        first, up, spot, others_half = fence(first, up, spot, others_half)
        get_first = near(first)
        upper = swap(up, "half", 1)
        masks_0 = bias_call(0, spot, table_rows)
        get_first, upper, masks_0, others_half = fence(get_first, upper, masks_0, others_half)
        get_first.append(swap(get_first[0], "shard", 2))
        get_others = near(others_half)
        tok, g, grad_down = prep_call(own_images, own_grad, upper, alive, order)
        big = cut_call(spot, outer_weight, expand_weight, reduce_weight)
        get_first, get_others, tok, spot, big = fence(get_first, get_others, tok, spot, big)
        first_pieces = [first] + get_first
        get_others.append(swap(get_others[1], "shard", 1))
        in_bias, up_bias, vecs, n1, n1t = vector_call(spot, first_pieces, tok)
        get_others, n1, big = fence(get_others, n1, big)
        others_back = [swap(v, "half", 1) for v in get_others]
        get_big = near(big)
    else:
        masks_0 = bias_call(0, spot, table_rows)
        upper = jnp.concatenate([swap(own_images[:, :TOK], "half", 1), swap(own_grad[:, :TOK], "half", 1)])
        whole_vectors = [lax.all_gather(v, "shard", axis=0, tiled=True).reshape(4, -1) for v in vectors]
        parts = jnp.stack([jnp.pad(v, ((0, 0), (0, D - v.shape[1]))) for v in whole_vectors], axis=1)
        parts = [jnp.pad(parts[r], ((0, 8), (0, 0))) for r in range(4)]
        thirds = inner_weight.reshape(-1, 3, 3, LP).transpose(0, 2, 1, 3).reshape(-1, 3, 3 * LP)
        first = thirds[:, 0]
        others = thirds[:, 1:].reshape(-1, 6 * LP)

        tok, g, grad_down = prep_call(own_images, own_grad, upper, alive, order)
        in_bias, up_bias, vecs, n1, n1t = vector_call(spot, parts, tok)

    if quick:
        def places(rows):
            at = [me * rows]
            for c in (core, 1 - core):
                at += [(me ^ 1) * rows + c * (rows // 2), (me ^ 2) * rows + c * (rows // 2), (me ^ 3) * rows + c * (rows // 2)]
            return at

        first_at = jnp.stack([(me ^ r) * OWN for r in range(4)]).astype(jnp.int32)
        in_at = jnp.stack(places(OWN)).astype(jnp.int32)

        def in_plan(columns):
            return [(k, 0, OWN if k == 0 else OWN // 2, columns, 3 * LP, 0, 0) for k in range(7)]

        in_plans = [[(k, 0, OWN, 0, 3 * LP, 0, 0) for k in range(4)], in_plan(0), in_plan(3 * LP)]
    else:
        first_at = in_at = jnp.zeros((1,), jnp.int32)
        first_pieces = [lax.all_gather(first, "shard", axis=0, tiled=True)]
        others_pieces = [lax.all_gather(others, "shard", axis=0, tiled=True)]
        in_plans = [[(0, 0, D, k, 3 * LP, 0, 0)] for k in (0, 0, 3 * LP)]

    results = [attend_call(0, n1, in_bias, masks_0, first_at, in_plans[0], first_pieces, [])]
    if quick:
        others_back, results, spot = fence(others_back, results, spot)
    masks_1 = bias_call(1, spot, table_rows)
    masks_2 = bias_call(2, spot, table_rows)
    if quick:
        masks_1, masks_2 = fence(masks_1, masks_2)
        others_pieces = [others] + get_others + others_back
    results.append(attend_call(1, n1, in_bias, masks_1, in_at, in_plans[1], others_pieces, [masks_2]))
    if quick:
        get_big, results, masks_2 = fence(get_big, results, masks_2)
        far = [swap(get_big[0][: BIG // 2], "shard", 2), swap(get_big[1][BIG // 2 :], "shard", 1)]
        big_back = [swap(v, "half", 1) for v in get_big]
    results.append(attend_call(2, n1, in_bias, masks_2, in_at, in_plans[2], others_pieces, []))
    if quick:
        far, big_back, results = fence(far, big_back, results)
        far_back = [swap(v, "half", 1) for v in far]
        far_back, results = fence(far_back, results)
        pieces = [outer_weight, expand_weight, reduce_weight] + get_big + far + big_back + far_back
        hlf = OWN // 2
        plan = [(0, 0, OWN, 0, D, 0, 0)]
        short = places(OWN)
        long = [None] + [c * 4 * CH + (me ^ r) * CH for c in (core, 1 - core) for r in (1, 2, 3)]
        at = [short[0]]
        for k in range(8):
            plan.append((1, 0, OWN, hidden_block(k) * CH, CH, 1, k * CH))
            at.append(short[0])
        for c in range(2):
            plan.append((2, c * CH, CH, 0, D, 2, 0))
            at.append(c * 4 * CH + me * CH)
        parts = [(b * hlf, hlf, 1, b * D) for b in range(4)] + [(4 * hlf, hlf, 0, 0), (5 * hlf, 4 * hlf, 2, 0)]

        def add_piece(source, lo, hi, place):
            for row, rows, target, column in parts:
                a, b = max(row, lo), min(row + rows, hi)
                if a < b and target == 1:
                    for c in range(2):
                        plan.append((source, a - lo, b - a, c * CH, CH, 1, c * 4 * CH + column // 2))
                        at.append(short[place] + (a - row))
                elif a < b:
                    plan.append((source, a - lo, b - a, 0, D, target, column))
                    at.append((long if target == 2 else short)[place] + (a - row))

        for side in range(2):
            for k in range(2):
                add_piece(3 + 4 * side + k, 0, BIG, 1 + 3 * side + k)
            add_piece(5 + 4 * side, 0, BIG // 2, 3 + 3 * side)
            add_piece(6 + 4 * side, BIG // 2, BIG, 3 + 3 * side)
        at = jnp.stack(at).astype(jnp.int32)
    else:
        pieces = [lax.all_gather(v, "shard", axis=0, tiled=True) for v in (outer_weight, expand_weight, reduce_weight)]
        plan, at = [(0, 0, D, 0, D, 0, 0)], [0]
        for k in range(8):
            plan += [(1, 0, D, hidden_block(k) * CH, CH, 1, k * CH), (2, hidden_block(k) * CH, CH, 0, D, 2, 0)]
            at += [0, k * CH]
        at = jnp.asarray(at, jnp.int32)
    projs, pts, atts, peak, ws = zip(*results)
    (stay, send, gmid, datt, out_send, out_keep, e_send, e_keep, r_send, r_keep, grad_up, small) = middle_call(
        spot, tok, atts, g, back_order, vecs, up_bias, at, plan, pieces, []
    )
    if quick:
        feed = Reduction([e_send, r_send], [e_keep, r_keep], replica, False)
    lower_out = swap(send, "half", 1)
    gp0, db0 = back_call(0, projs[0], pts[0], datt, [])
    if quick:
        (gp0, lower_out, projs) = together([feed], gp0, lower_out, projs)
    gp1, db1 = back_call(1, projs[1], pts[1], datt, feed.sent if quick else [])
    i0_send, i0_keep, i1_send, i1_keep, in01 = inner_call(spot, n1t, (gp0, gp1), [])
    chains = []
    if quick:
        i0_send, i1_send, projs = together([feed], i0_send, i1_send, projs)
        ahead = Reduction([i0_send, i1_send], [i0_keep, i1_keep], replica, True)
        chains = [feed, ahead]
    gp2, db2 = back_call(2, projs[2], pts[2], datt, feed.sent if quick else [])
    if quick:
        gp2, db2 = together(chains, gp2, db2)
    i2_send, i2_keep, in2 = inner_call(spot, n1t, (gp2,), feed.sent + ahead.sent if quick else [])
    if quick:
        rest = Reduction([i2_send, out_send], [i2_keep, out_keep], replica, True)
        chains = [feed, ahead, rest]
    one, gstay, gsend = last_call(tok, gmid, vecs, back_order, (gp0, gp1, gp2), ws, [i2_send])
    after = []
    if quick:
        gsend, one = together(chains, gsend, one)
        after = feed.sent + ahead.sent + rest.sent
    lower_grad = swap(gsend, "half", 1)
    peak = jnp.concatenate(peak, axis=2)
    peaks = jnp.max(jnp.where((present > 0)[:, None, None, None], peak, NEGATIVE), axis=(0, 1, 3)).reshape(1, HEADS)
    sums = table_call((db0, db1, db2), grad_up, grad_down, small, in01, in2, one, peaks, after)
    if quick:
        sums, lower_grad = together(chains, sums, lower_grad)
    every = Everywhere(sums)
    chains.append(every)
    done = None
    while not all(c.done for c in chains):
        if quick and done is None and feed.done:
            swapped = fence(feed.flying)[0]
            (em, rm), (eo, ro) = feed.keep, swapped
            done = feed_finish(spot, em, eo, rm, ro)
            chains = [c for c in chains if c is not feed]
            done = together(chains, *done)
        else:
            together(chains)
    sums = every.value

    place = jnp.stack([me, core, shard]).astype(jnp.int32)
    (grad_inbias, grad_outbias, grad_upbias, grad_downbias, grad_gain_1, grad_shift_1, grad_gain_2, grad_shift_2, grad_table,
     clipped, factors, maxima) = vector_finish(place, sums, threshold, inner_weight, shard_count)

    if quick:
        grad_expand, grad_reduce = done
        grad_inner, grad_outer = inner_finish(spot, ahead.keep + rest.keep, ahead.flying + rest.flying)
    else:
        def halves(keep, send, axis):
            lo = jnp.where(core == 0, keep, send)
            hi = jnp.where(core == 0, send, keep)
            return jnp.concatenate([lo, hi], axis=axis)

        def whole(keep, send):
            both = halves(keep[:, :, :, None], send[:, :, :, None], 3)
            return both.transpose(0, 2, 1, 3, 4).reshape(D, -1)

        def settle(v):
            v = lax.psum_scatter(v.astype(BF), "shard", scatter_dimension=0, tiled=True)
            return lax.psum(v, ("replica", "half")).astype(F32)

        def rows_of(v):
            return v.reshape(4, 1, 2, 2, OWN, CH).transpose(0, 1, 2, 4, 3, 5).reshape(4, 1, CH, D)

        def straight(v):
            return jnp.stack([v[0], v[2], v[1], v[3]])

        grad_reduce = settle(halves(rows_of(r_keep), rows_of(r_send), 1).reshape(FF, D))
        grad_expand = settle(whole(straight(e_keep), straight(e_send)))
        grad_outer = settle(whole(out_keep, out_send))
        by_third = [
            whole(straight(i0_keep), straight(i0_send)), whole(i1_keep, i1_send), whole(straight(i2_keep), straight(i2_send))
        ]
        by_third = jnp.stack(by_third, axis=1).reshape(D, 3, 3, LP).transpose(0, 2, 1, 3).reshape(D, 3 * D)
        grad_inner = settle(by_third)

    block_out = jnp.concatenate([lower_out, stay], axis=1).reshape(images.shape)
    grad_images = jnp.concatenate([lower_grad, gstay], axis=1).reshape(images.shape)
    return (
        block_out,
        grad_images,
        grad_inner,
        grad_inbias,
        grad_outer,
        grad_outbias,
        grad_expand,
        grad_upbias,
        grad_reduce,
        grad_downbias,
        grad_gain_1,
        grad_shift_1,
        grad_gain_2,
        grad_shift_2,
        grad_table,
        clipped,
        factors,
        maxima,
    )


def solution(mesh):
    rows = P(("replica", "shard"), "half", None, None)
    cut = P("shard", None)
    line = P("shard")
    return jax.shard_map(
        shards,
        mesh=mesh,
        in_specs=(rows, rows, P(("replica", "shard")), P(), cut, line, cut, line, cut, line, cut, line, line, line, line,
                  line, P()),
        out_specs=(rows, rows, cut, line, cut, line, cut, line, cut, line, line, line, line, line, P(), cut, P(), P()),
        check_vma=False,
    )
```

```python
import functools
import math

import numpy as np
import jax
import jax.numpy as jnp
from jax import lax
from jax.experimental import pallas as pl
from jax.experimental.pallas import tpu as pltpu
from jax.sharding import PartitionSpec as P

D = 768
HEADS = 24
HD = 32
WIN = 12
GRID = 24
SHIFT = 6
FF = 3072
TOK = WIN * WIN
ROWS = WIN * GRID
SPAN = 2 * WIN - 1
EPS = 1e-5
MASKED = -100.0
NEGATIVE = -1e30
LOG2E = math.log2(math.e)
BF = jnp.bfloat16
F32 = jnp.float32
MB = 1 << 20
OWN = 192
CH = 384
WIDE = 640
NARROW = 384
TALL = WIN * 16
HB = 8
LB = HB * HD
HP = 8
LP = HP * HD
NB = 576
SCALE = 1e-3
ONE = dict(pipeline_mode=pl.Buffered(1))
SD = jax.ShapeDtypeStruct


def nn(a, b):
    return lax.dot_general(a, b, (((1,), (0,)), ((), ())), preferred_element_type=F32)


def nt(a, b):
    return lax.dot_general(a, b, (((1,), (1,)), ((), ())), preferred_element_type=F32)


def tn(a, b):
    return lax.dot_general(a, b, (((0,), (0,)), ((), ())), preferred_element_type=F32)


def full(shape, **kw):
    return pl.BlockSpec(shape, lambda *_: (0,) * len(shape), **kw)


def any_space():
    return pl.BlockSpec(memory_space=pl.ANY)


def smem():
    return pl.BlockSpec(memory_space=pltpu.SMEM)


def run(kernel, count, args, after, in_specs, **kw):
    def body(*refs):
        kernel(*refs[:count], *refs[count + len(after) :])

    return pl.pallas_call(body, in_specs=list(in_specs) + [any_space()] * len(after), **kw)(*args, *after)


def params(limit=60):
    return pltpu.CompilerParams(vmem_limit_bytes=limit * MB)


def cost(flops, moved, exps=0):
    return pl.CostEstimate(flops=int(flops * SCALE), bytes_accessed=int(moved * SCALE), transcendentals=0)


def whole(array):
    return full(array.shape, **ONE)


def single(kernel, args, out_shape, after=(), scratch=(), **kw):
    specs = [smem() if v.dtype == jnp.int32 else whole(v) for v in args]
    shapes = out_shape if isinstance(out_shape, (list, tuple)) else [out_shape]
    out = run(
        kernel, len(args), args, after, grid=(1,), in_specs=specs, out_specs=[whole(v) for v in shapes], out_shape=list(shapes),
        scratch_shapes=list(scratch), compiler_params=params(), **kw
    )
    return out if isinstance(out_shape, (list, tuple)) else out[0]


def colsum(v):
    return jnp.sum(v, axis=0, keepdims=True)


def norm_parts(x):
    c = x - jnp.mean(x, axis=-1, keepdims=True)
    r = lax.rsqrt(jnp.mean(c * c, axis=-1, keepdims=True) + EPS)
    return c * r, r


def row_order():
    cells = np.arange(ROWS)
    win, rest = cells // TOK, cells % TOK
    a, b = rest // WIN, rest % WIN
    m = np.zeros((ROWS, ROWS), np.float32)
    m[cells, a * GRID + (win * WIN + b + SHIFT) % GRID] = 1
    return m


def spread_q():
    q = np.arange(TOK)
    m = np.zeros((TOK, NARROW), np.float32)
    m[q, SPAN * (q // WIN) + q % WIN] = 1
    return m


def spread_k(reverse):
    k = np.arange(TOK)
    b = k % WIN
    m = np.zeros((TALL, TOK), np.float32)
    m[16 * (k // WIN) + (WIN - 1 - b if reverse else b), k] = 1
    return m


def copies(plan, refs, at, targets, sems):
    for i, (src, row, rows, col, cols, dst, put) in enumerate(plan):
        place = pl.ds(pl.multiple_of(at[i], 16), rows)
        yield pltpu.make_async_copy(
            refs[src].at[pl.ds(row, rows), pl.ds(col, cols)], targets[dst].at[place, pl.ds(put, cols)], sems.at[i]
        )


def hidden_block(k):
    return 2 * (k % 4) + k // 4


def region_masks():
    line = np.arange(GRID)
    region = (line >= GRID - WIN).astype(np.int32) + (line >= GRID - SHIFT).astype(np.int32)
    lab = 3 * region[:, None] + region[None, :]
    lab = lab.reshape(2, WIN, 2, WIN).transpose(0, 2, 1, 3).reshape(2, 2, TOK)
    return np.where(lab[:, :, :, None] != lab[:, :, None, :], MASKED, 0.0).astype(np.float32)


def bias_kernel(spot_ref, table_ref, mask_ref, sq_ref, sk_ref, out_ref, tall):
    masks = [mask_ref[spot_ref[1], w].astype(F32) for w in range(2)]
    for h in range(HP):
        row = pltpu.roll(jnp.broadcast_to(table_ref[h : h + 1, :], (16, WIDE)), 0, 1, stride=1, stride_axis=0)
        for a in range(WIN):
            off = (SPAN * a - SPAN * (WIN - 1) - (WIN - 1)) % WIDE
            tall[16 * a : 16 * a + 16, :] = pltpu.roll(row, off, 1)[:, :NARROW].astype(BF)
        wide = nn(tall[...], sq_ref[...]).astype(BF)
        bias = nn(sk_ref[...], wide)
        for w in range(2):
            out_ref[w, h] = (bias + masks[w]) * LOG2E


def bias_call(group, spot, table):
    args = (spot, table, jnp.asarray(region_masks(), BF), jnp.asarray(spread_q().T, BF), jnp.asarray(spread_k(False).T, BF))
    out = SD((2, HP, TOK, TOK), F32)
    return pl.pallas_call(
        bias_kernel,
        grid=(1,),
        in_specs=[smem(), pl.BlockSpec((HP, WIDE), lambda i: (group, 0))] + [whole(v) for v in args[2:]],
        out_specs=whole(out),
        out_shape=out,
        scratch_shapes=[pltpu.VMEM((TALL, NARROW), BF)],
        compiler_params=params(),
        cost_estimate=cost(2e9, 3 * MB),
        name="bias",
    )(*args)


V_UP, V_SMALL, V_IN, V_ONE, V_PEAK, V_TABLE, V_ROWS = 0, 4, 8, 11, 13, 16, 40


def table_kernel(db0_ref, db1_ref, db2_ref, up_ref, down_ref, small_ref, in_ref, peak_ref, sq_ref, sk_ref, out_ref):
    def split(v):
        hi = v.astype(BF)
        return hi, (v - hi.astype(F32)).astype(BF)

    out_ref[...] = jnp.zeros_like(out_ref)
    for k in range(8):
        b = hidden_block(k)
        out_ref[V_UP + b // 2 : V_UP + b // 2 + 1, (b % 2) * CH : (b % 2 + 1) * CH] = up_ref[
            k // 2, :, (k % 2) * CH : (k % 2 + 1) * CH
        ]
    out_ref[V_SMALL : V_SMALL + 1, :] = down_ref[...]
    out_ref[V_SMALL + 1 : V_SMALL + 4, :] = small_ref[1:4, :]
    for p in range(3):
        row = in_ref[p]
        for k in range(3):
            out_ref[V_IN + k : V_IN + k + 1, p * LP : (p + 1) * LP] = row[:, k * LP : (k + 1) * LP]
    out_ref[V_PEAK : V_PEAK + 1, :HEADS] = peak_ref[...]
    for h in range(HEADS):
        hi, lo = split((db0_ref, db1_ref, db2_ref)[h // HP][h % HP])
        tall = nn(sk_ref[...], hi) + nn(sk_ref[...], lo)
        hi, lo = split(tall)
        wide = nn(hi, sq_ref[...]) + nn(lo, sq_ref[...])
        wide = jnp.concatenate([wide, jnp.zeros((TALL, WIDE - NARROW), F32)], axis=1)
        tot = jnp.zeros((16, WIDE), F32)
        for a in range(WIN):
            tot = tot + pltpu.roll(wide[16 * a : 16 * a + 16, :], SPAN * (WIN - 1 - a), 1)
        tot = pltpu.roll(tot, 0, 1, stride=1, stride_axis=0)
        out_ref[V_TABLE + h : V_TABLE + h + 1, :WIDE] = colsum(tot)


def table_call(dbs, up, down, small, sums_in, peaks, after):
    args = (*dbs, up, down, small, sums_in, peaks, jnp.asarray(spread_q(), BF), jnp.asarray(spread_k(True), BF))
    return single(table_kernel, args, SD((V_ROWS, D), F32), after, cost_estimate=cost(6e9, 4 * MB), name="table")


def lane_head(shape):
    return lax.broadcasted_iota(jnp.int32, shape, len(shape) - 1) // HD


VECTORS = (2 * D, D, FF, D, D, D, D, D)


def first_kernel(spot_ref, *refs):
    vecs, (inner_ref, own_ref, gown_ref, first_ref, others_ref, half_ref, up_ref) = refs[:8], refs[8:]
    n = own_ref.shape[0]
    up_ref[:n] = own_ref[...]
    up_ref[n:] = gown_ref[...]
    mine = pl.ds(pl.multiple_of(spot_ref[1] * (OWN // 2), 16), OWN // 2)
    for k in range(3):
        first_ref[:OWN, k * LP : (k + 1) * LP] = inner_ref[:, k * D : k * D + LP]
        for p in (1, 2):
            src = slice(k * D + p * LP, k * D + (p + 1) * LP)
            dst = slice(((p - 1) * 3 + k) * LP, ((p - 1) * 3 + k + 1) * LP)
            others_ref[:, dst] = inner_ref[:, src]
            half_ref[:, dst] = inner_ref[mine, src]
    rows = [jnp.zeros((8, D), F32)]
    for v in vecs:
        row = v[...].astype(F32).reshape(1, v.shape[0])
        if v.shape[0] < D:
            row = jnp.concatenate([row, jnp.zeros((1, D - v.shape[0]), F32)], axis=1)
        rows.insert(-1, row)
    first_ref[OWN:, :] = jnp.concatenate(rows, axis=0).astype(BF)


def first_call(spot, vectors, inner, own, gown):
    n = own.shape[0]
    top = full((n, TOK, D))
    shapes = [SD((OWN + 16, D), BF), SD((OWN, 6 * LP), BF), SD((OWN // 2, 6 * LP), BF), SD((2 * n, TOK, D), BF)]
    return pl.pallas_call(
        first_kernel,
        grid=(1,),
        in_specs=[smem()] + [whole(v) for v in vectors] + [whole(inner), top, top],
        out_specs=[whole(v) for v in shapes],
        out_shape=shapes,
        compiler_params=params(),
        cost_estimate=cost(1e6, 6 * MB),
        name="first",
    )(spot, *vectors, inner, own, gown)


BIG = 4 * (OWN // 2) + OWN // 2 + 2 * OWN


def cut_kernel(spot_ref, outer_ref, expand_ref, reduce_ref, big_ref):
    core = spot_ref[1]
    hlf = OWN // 2
    mine = pl.ds(pl.multiple_of(core * hlf, 16), hlf)
    for k in range(4):
        big_ref[k * hlf : (k + 1) * hlf, :] = expand_ref[mine, k * D : (k + 1) * D]
    big_ref[4 * hlf : 5 * hlf, :] = outer_ref[mine, :]
    big_ref[5 * hlf :, :] = reduce_ref[pl.ds(pl.multiple_of(core * 2 * OWN, 16), 2 * OWN), :]


def cut_call(spot, outer, expand, reduce):
    return single(
        cut_kernel, (spot, outer, expand, reduce), [SD((BIG, D), BF)], cost_estimate=cost(1e6, 3 * MB), name="cut"
    )[0]


def prep_kernel(own_ref, gown_ref, recv_ref, alive_ref, pm_ref, tok_ref, g_ref, sum_ref):
    n = own_ref.shape[0]
    tot = jnp.zeros((1, D), F32)
    for i in range(n):
        tok_ref[i] = nn(pm_ref[...], jnp.concatenate([own_ref[i, TOK:, :], recv_ref[i]], axis=0)).astype(BF)
        g = nn(pm_ref[...], jnp.concatenate([gown_ref[i, TOK:, :], recv_ref[n + i]], axis=0)) * alive_ref[0:1, i : i + 1]
        g_ref[i] = g.astype(BF)
        tot = tot + colsum(g)
    sum_ref[...] = tot


def prep_call(own, gown, recv, alive, pm):
    rows = SD(own.shape, BF)
    return single(
        prep_kernel, (own, gown, recv, alive, pm), [rows, rows, SD((1, D), F32)], cost_estimate=cost(3e9, 16 * MB), name="prep"
    )


def vector_kernel(spot_ref, pa_ref, pb_ref, pc_ref, pd_ref, tok_ref, inb_ref, up_ref, vec_ref, n1_ref, n1t_ref, parts):
    n = tok_ref.shape[0]
    for r, ref in enumerate((pa_ref, pb_ref, pc_ref, pd_ref)):
        parts[jnp.bitwise_xor(spot_ref[0], r)] = ref[:8, :].astype(F32)

    def vector(i):
        size = VECTORS[i] // 4
        return jnp.concatenate([parts[s][i : i + 1, :size] for s in range(4)], axis=1)

    vin = vector(0)
    for p in range(3):
        inb_ref[p] = jnp.concatenate(
            [vin[:, p * LP : (p + 1) * LP], jnp.zeros((1, LP), F32), vin[:, D + p * LP : D + (p + 1) * LP]], axis=1
        )
    vup = vector(2)
    for k in range(8):
        up_ref[k // 2, :, (k % 2) * CH : (k % 2 + 1) * CH] = vup[:, hidden_block(k) * CH : (hidden_block(k) + 1) * CH]
    gain, shift = vector(4), vector(5)
    vec_ref[...] = jnp.zeros_like(vec_ref)
    for r, v in enumerate((vector(1), vector(3), gain, vector(6), vector(7))):
        vec_ref[r : r + 1, :] = v
    for i in range(n):
        xh, _ = norm_parts(tok_ref[i].astype(F32))
        n1 = (xh * gain + shift).astype(BF)
        n1_ref[i] = n1
        n1t_ref[:, i * ROWS : (i + 1) * ROWS] = n1.T


def vector_call(spot, parts, tok):
    n = tok.shape[0]
    last = parts[0].shape[0] // 16 - 1
    shapes = [SD((3, 1, 3 * LP), F32), SD((4, 1, 2 * CH), F32), SD((8, D), F32), SD(tok.shape, BF), SD((D, n * ROWS), BF)]
    return pl.pallas_call(
        vector_kernel,
        grid=(1,),
        in_specs=[smem()] + [pl.BlockSpec((16, D), lambda i: (last, 0))] * 4 + [whole(tok)],
        out_specs=[whole(v) for v in shapes],
        out_shape=shapes,
        scratch_shapes=[pltpu.VMEM((4, 8, D), F32)],
        compiler_params=params(),
        cost_estimate=cost(5e9, 8 * MB),
        name="vectors",
    )(spot, *parts, tok)


def attend_kernel(plan, count, n1_ref, b_ref, bm_ref, at_ref, *rest):
    pieces = rest[:count]
    proj_ref, pt_ref, att_ref, peak_ref, w_ref, sems = rest[count:]

    @pl.when(pl.program_id(0) == 0)
    def _():
        for c in copies(plan, pieces, at_ref, (w_ref,), sems):
            c.start()
        for c in copies(plan, pieces, at_ref, (w_ref,), sems):
            c.wait()

    proj_ref[0] = (nn(n1_ref[0], w_ref[...]) + b_ref[0]).astype(BF)
    hid = lane_head((TOK, LB))
    scale = HD**-0.5
    for w in range(2):
        r = slice(w * TOK, (w + 1) * TOK)
        for blk in range(LP // LB):
            l = blk * LB
            q = proj_ref[0, r, l : l + LB]
            k = proj_ref[0, r, LP + l : LP + l + LB]
            v = proj_ref[0, r, 2 * LP + l : 2 * LP + l + LB]
            vt = v.T
            apart = jnp.concatenate([jnp.where(hid == h, k, jnp.zeros_like(k)) for h in range(HB)], axis=0)
            sts = nn(apart, q.T)
            outs = []
            for h in range(HB):
                hh = blk * HB + h
                st = sts[h * TOK : (h + 1) * TOK]
                peak_ref[0, w, hh : hh + 1, :] = jnp.max(st, axis=0, keepdims=True) * scale
                t = st * (scale * LOG2E) + bm_ref[w, hh]
                e = jnp.exp2(t - jnp.max(t, axis=0, keepdims=True))
                p = (e * (1.0 / colsum(e))).astype(BF)
                pt_ref[0, w, hh] = p
                outs.append(nn(vt[HD * h : HD * h + HD, :], p))
            att_ref[0, r, l : l + LB] = jnp.concatenate(outs, axis=0).astype(BF).T


def attend_call(group, n1, b, bm, at, plan, pieces, after):
    n = n1.shape[0]

    def blk(*s):
        return pl.BlockSpec((1,) + s, lambda i: (i,) + (0,) * len(s))

    return run(
        functools.partial(attend_kernel, plan, len(pieces)), 4 + len(pieces), (n1, b, bm, at, *pieces), after,
        grid=(n,),
        in_specs=[blk(ROWS, D), pl.BlockSpec((1, 1, 3 * LP), lambda i: (group, 0, 0)), full((2, HP, TOK, TOK), **ONE), smem()]
        + [any_space()] * len(pieces),
        out_specs=[blk(ROWS, 3 * LP), blk(2, HP, TOK, TOK), blk(ROWS, LP), blk(2, HP, TOK), full((D, 3 * LP), **ONE)],
        out_shape=[SD((n, ROWS, 3 * LP), BF), SD((n, 2, HP, TOK, TOK), BF), SD((n, ROWS, LP), BF), SD((n, 2, HP, TOK), F32),
                   SD((D, 3 * LP), BF)],
        scratch_shapes=[pltpu.SemaphoreType.DMA((len(plan),))],
        compiler_params=params(),
        cost_estimate=cost(1.3e10, 12 * MB, 1.4e6),
        name="attend",
    )


def gelu_parts(h):
    d = 1.0 + (0.3275911 * 0.5**0.5) * jnp.abs(h)
    t = pl.reciprocal(d, approx=True)
    t = t * (2.0 - d * t)
    e = jnp.exp2(h * h * (-0.5 * LOG2E))
    p = (((0.5 * 1.061405429) * t - 0.5 * 1.453152027) * t + 0.5 * 1.421413741) * t - 0.5 * 0.284496736
    p = (p * t + 0.5 * 0.254829592) * t * e
    cdf = jnp.where(h >= 0, 1.0 - p, p)
    return cdf, cdf + h * (e * ((2 * math.pi) ** -0.5))


def middle_kernel(plan, count, spot_ref, tok_ref, att0_ref, att1_ref, att2_ref, gin_ref, pmt_ref, vec_ref, eb_ref,
                  at_ref, *rest):
    pieces = rest[:count]
    (stay_ref, send_ref, gmid_ref, datt_ref, os_ref, ok_ref, es_ref, ek_ref, rs_ref, rk_ref, geb_ref, small_ref,
     wo, we, wr, mid, n2, g, n2t, acc, e2, act, gh, sems) = rest[count:]
    j = pl.program_id(0)
    n = tok_ref.shape[0]
    N = n * ROWS
    me = spot_ref[0]
    core = spot_ref[1]
    early = [k for k, entry in enumerate(plan) if entry[5] == 0]
    out_b, red_b, gain, shift = vec_ref[0:1, :], vec_ref[1:2, :], vec_ref[3:4, :], vec_ref[4:5, :]

    def attended(i):
        return jnp.concatenate([att0_ref[i], att1_ref[i], att2_ref[i]], axis=-1)

    @pl.when(j == 0)
    def _():
        moves = list(copies(plan, pieces, at_ref, (wo, we, wr), sems))
        for c in moves:
            c.start()
        for k in early:
            moves[k].wait()
        for i in range(n):
            s = slice(i * ROWS, (i + 1) * ROWS)
            g[s, :] = gin_ref[i]
            m = tok_ref[i].astype(F32) + nn(attended(i), wo[...]) + out_b
            mid[s, :] = m
            xh, _ = norm_parts(m)
            x2 = (xh * gain + shift).astype(BF)
            n2[s, :] = x2
            n2t[:, s] = x2.T
            acc[s, :] = m + red_b
            e2[s, :] = jnp.zeros((ROWS, D), F32)
        for k, c in enumerate(moves):
            if k not in early:
                c.wait()

    at = pl.multiple_of((2 * jnp.bitwise_xor(core, 1 - j // 2) + j % 2) * 2 * CH, 2 * CH)
    cols = pl.ds(at, 2 * CH)
    tot = jnp.zeros((1, 2 * CH), F32)
    for s0 in range(0, N, NB):
        s = slice(s0, s0 + NB)
        h = nn(n2[s, :], we[:, cols]) + eb_ref[0]
        cdf, dg = gelu_parts(h)
        act[s, :] = (h * cdf).astype(BF)
        x = (nt(g[s, :], wr[cols, :]) * dg).astype(BF)
        gh[s, :] = x
        tot = tot + colsum(x.astype(F32))
    geb_ref[0] = tot
    ge = nn(n2t[...], gh[...]).astype(BF)
    gr = tn(act[...], g[...]).astype(BF)

    def put(e_ref, r_ref):
        for t in range(2):
            for b in range(4):
                e_ref[crossed(jnp.bitwise_xor(me, b)), t] = ge[b * OWN : (b + 1) * OWN, t * CH : (t + 1) * CH]
                r_ref[jnp.bitwise_xor(me % 2, t), b] = gr[
                    t * CH + (b // 2) * OWN : t * CH + (b // 2 + 1) * OWN, (b % 2) * CH : (b % 2 + 1) * CH
                ]

    @pl.when(j < 2)
    def _():
        put(es_ref, rs_ref)

    @pl.when(j >= 2)
    def _():
        put(ek_ref, rk_ref)

    for s0 in range(0, N, NB):
        s = slice(s0, s0 + NB)
        acc[s, :] += nn(act[s, :], wr[cols, :])
        e2[s, :] += nt(gh[s, :], we[:, cols])

    @pl.when(j == 3)
    def _():
        gn = jnp.zeros((1, D), F32)
        shf = gn
        ob = gn
        for i in range(n):
            s = slice(i * ROWS, (i + 1) * ROWS)
            o = nn(pmt_ref[...], acc[s, :].astype(BF)).astype(BF)
            stay_ref[i] = o[:TOK]
            send_ref[i] = o[TOK:]
            xh, r = norm_parts(mid[s, :])
            d = e2[s, :]
            gn = gn + colsum(d * xh)
            shf = shf + colsum(d)
            d = d * gain
            gm = g[s, :].astype(F32) + r * (
                d - jnp.mean(d, axis=-1, keepdims=True) - xh * jnp.mean(d * xh, axis=-1, keepdims=True)
            )
            gmid_ref[i] = gm
            gb = gm.astype(BF)
            ob = ob + colsum(gb.astype(F32))
            g[s, :] = gb
            datt_ref[i] = nt(gb, wo[...]).astype(BF)
            n2[s, :] = attended(i)
        for c, ref in ((1 - core, os_ref), (core, ok_ref)):
            go = tn(n2[...], g[:, pl.ds(pl.multiple_of(c * CH, 128), CH)]).astype(BF)
            for b in range(4):
                ref[jnp.bitwise_xor(me, b), 0] = go[b * OWN : (b + 1) * OWN, :]
        small_ref[1:2, :] = gn
        small_ref[2:3, :] = shf
        small_ref[3:4, :] = ob


def crossed(r):
    return 2 * (r % 2) + r // 2


def middle_call(spot, tok, atts, g, pmt, vecs, eb, at, plan, pieces, after):
    n = tok.shape[0]
    N = n * ROWS
    blocks = SD((4, 4, OWN, CH), BF)

    def chunk(j, spot):
        return 2 * jnp.bitwise_xor(spot[1], 1 - j // 2) + j % 2

    def early(j):
        return jnp.minimum(j, 1)

    def late(j):
        return jnp.maximum(j, 2) - 2

    rows = full((n, ROWS, D), **ONE)
    third = full((n, ROWS, LP), **ONE)
    cut = full((n, TOK, D), **ONE)
    outer = full((4, 1, OWN, CH), **ONE)
    args = (spot, tok, *atts, g, pmt, vecs, eb, at, *pieces)

    def body(*refs):
        middle_kernel(plan, len(pieces), *refs[: len(args)], *refs[len(args) + len(after) :])

    grid_spec = pltpu.PrefetchScalarGridSpec(
        num_scalar_prefetch=1,
        grid=(4,),
        in_specs=[rows, third, third, third, rows, full((ROWS, ROWS)), full((8, D)),
                  pl.BlockSpec((1, 1, 2 * CH), lambda j, spot: (chunk(j, spot), 0, 0)), smem()]
        + [any_space()] * (len(pieces) + len(after)),
        out_specs=[cut, cut, rows, rows, outer, outer,
                   pl.BlockSpec((4, 2, OWN, CH), lambda j, spot: (0, early(j), 0, 0)),
                   pl.BlockSpec((4, 2, OWN, CH), lambda j, spot: (0, late(j), 0, 0)),
                   pl.BlockSpec((2, 4, OWN, CH), lambda j, spot: (jnp.bitwise_xor(early(j), spot[0] // 2), 0, 0, 0)),
                   pl.BlockSpec((2, 4, OWN, CH), lambda j, spot: (jnp.bitwise_xor(late(j), spot[0] // 2), 0, 0, 0)),
                   pl.BlockSpec((1, 1, 2 * CH), lambda j, spot: (chunk(j, spot), 0, 0)), full((8, D))],
        scratch_shapes=[pltpu.VMEM((D, D), BF), pltpu.VMEM((D, FF), BF), pltpu.VMEM((FF, D), BF),
                        pltpu.VMEM((N, D), F32), pltpu.VMEM((N, D), BF), pltpu.VMEM((N, D), BF), pltpu.VMEM((D, N), BF),
                        pltpu.VMEM((N, D), F32), pltpu.VMEM((N, D), F32), pltpu.VMEM((N, 2 * CH), BF), pltpu.VMEM((N, 2 * CH), BF),
                        pltpu.SemaphoreType.DMA((len(plan),))],
    )
    return pl.pallas_call(
        body,
        grid_spec=grid_spec,
        out_shape=[SD((n, TOK, D), BF), SD((n, TOK, D), BF), SD((n, ROWS, D), F32), SD((n, ROWS, D), BF),
                   SD((4, 1, OWN, CH), BF), SD((4, 1, OWN, CH), BF), blocks, blocks, blocks, blocks,
                   SD((4, 1, 2 * CH), F32), SD((8, D), F32)],
        compiler_params=params(62),
        cost_estimate=cost(6e10, 40 * MB, 7e6),
        name="middle",
    )(*args, *after)


def back_kernel(proj_ref, pt_ref, da_ref, gp_ref, db_ref):
    @pl.when(pl.program_id(0) == 0)
    def _():
        db_ref[...] = jnp.zeros_like(db_ref)

    hid = lane_head((TOK, LB))
    scale = HD**-0.5
    for w in range(2):
        r = slice(w * TOK, (w + 1) * TOK)
        for blk in range(LP // LB):
            l = blk * LB
            q = proj_ref[0, r, l : l + LB]
            k = proj_ref[0, r, LP + l : LP + l + LB]
            v = proj_ref[0, r, 2 * LP + l : 2 * LP + l + LB]
            do = da_ref[0, r, l : l + LB]
            qt, kt, dt = q.T, k.T, do.T
            dq, dk, dv = [], [], []
            dps = nn(jnp.concatenate([jnp.where(hid == h, v, jnp.zeros_like(v)) for h in range(HB)], axis=0), dt)
            for h in range(HB):
                hh = blk * HB + h
                s = slice(HD * h, HD * h + HD)
                dp = dps[h * TOK : (h + 1) * TOK]
                pb = pt_ref[0, w, hh]
                p = pb.astype(F32)
                pd = p * dp
                ds = pd - p * colsum(pd)
                db_ref[hh] += ds
                dsb = ds.astype(BF)
                dq.append(nn(kt[s, :], dsb))
                dk.append(nt(qt[s, :], dsb))
                dv.append(nt(dt[s, :], pb))
            gp_ref[0, r, l : l + LB] = (jnp.concatenate(dq, axis=0) * scale).astype(BF).T
            gp_ref[0, r, LP + l : LP + l + LB] = (jnp.concatenate(dk, axis=0) * scale).astype(BF).T
            gp_ref[0, r, 2 * LP + l : 2 * LP + l + LB] = jnp.concatenate(dv, axis=0).astype(BF).T


def back_call(group, proj, pt, da, after):
    n = proj.shape[0]

    def blk(*s):
        return pl.BlockSpec((1,) + s, lambda i: (i,) + (0,) * len(s))

    return run(
        back_kernel, 3, (proj, pt, da), after,
        grid=(n,),
        in_specs=[blk(ROWS, 3 * LP), blk(2, HP, TOK, TOK), pl.BlockSpec((1, ROWS, LP), lambda i: (i, 0, group))],
        out_specs=[blk(ROWS, 3 * LP), full((HP, TOK, TOK))],
        out_shape=[SD((n, ROWS, 3 * LP), BF), SD((HP, TOK, TOK), F32)],
        compiler_params=params(),
        cost_estimate=cost(1.8e10, 10 * MB),
        name="attend_back",
    )


def inner_kernel(spot_ref, n1t_ref, gp0_ref, gp1_ref, gp2_ref, os_ref, ok_ref, xs_ref, xk_ref, ys_ref, yk_ref, sum_ref):
    me = spot_ref[0]
    core = spot_ref[1]
    n = gp0_ref.shape[0]
    ys_ref[:, 1:2] = os_ref[...]
    yk_ref[:, 1:2] = ok_ref[...]
    for p, gp_ref, send, keep, m in ((0, gp0_ref, xs_ref, xk_ref, 0), (1, gp1_ref, ys_ref, yk_ref, 0), (2, gp2_ref, xs_ref, xk_ref, 1)):
        gp = gp_ref[...].reshape(n * ROWS, 3 * LP)
        sum_ref[p] = colsum(gp.astype(F32))
        gi = nn(n1t_ref[...], gp).astype(BF)

        for c in range(2):
            @pl.when(core == c)
            def _():
                for b in range(4):
                    r = slice(b * OWN, (b + 1) * OWN)
                    rel = jnp.bitwise_xor(me, b)
                    rel = rel if p == 1 else crossed(rel)
                    keep[rel, m] = gi[r, c * CH : (c + 1) * CH]
                    send[rel, m] = gi[r, (1 - c) * CH : (2 - c) * CH]


def inner_call(spot, n1t, gps, outer, after):
    block = SD((4, 2, OWN, CH), BF)
    return single(
        inner_kernel, (spot, n1t, *gps, *outer), [block] * 4 + [SD((3, 1, 3 * LP), F32)], after,
        cost_estimate=cost(1.2e10, 12 * MB), name="inner_grad",
    )


def last_kernel(tok_ref, gmid_ref, vec_ref, pmt_ref, gp0_ref, gp1_ref, gp2_ref, w0_ref, w1_ref, w2_ref,
                small_ref, stay_ref, send_ref):
    @pl.when(pl.program_id(0) == 0)
    def _():
        small_ref[...] = jnp.zeros_like(small_ref)

    d = nt(gp0_ref[0], w0_ref[...]) + nt(gp1_ref[0], w1_ref[...]) + nt(gp2_ref[0], w2_ref[...])
    xh, r = norm_parts(tok_ref[0].astype(F32))
    small_ref[0:1, :] += colsum(d * xh)
    small_ref[1:2, :] += colsum(d)
    d = d * vec_ref[2:3, :]
    gm = gmid_ref[0] + r * (d - jnp.mean(d, axis=-1, keepdims=True) - xh * jnp.mean(d * xh, axis=-1, keepdims=True))
    o = nn(pmt_ref[...], gm.astype(BF)).astype(BF)
    stay_ref[0] = o[:TOK]
    send_ref[0] = o[TOK:]


def last_call(first, n, tok, gmid, gain, pmt, gps, ws, after):
    def blk(*s):
        return pl.BlockSpec((1,) + s, lambda i: (first + i,) + (0,) * len(s))

    cut = pl.BlockSpec((1, TOK, D), lambda i: (i, 0, 0))

    return run(
        last_kernel, 10, (tok, gmid, gain, pmt, *gps, *ws), after,
        grid=(n,),
        in_specs=[blk(ROWS, D), blk(ROWS, D), full((8, D)), full((ROWS, ROWS))] + [blk(ROWS, 3 * LP)] * 3
        + [full((D, 3 * LP), **ONE)] * 3,
        out_specs=[full((8, D)), cut, cut],
        out_shape=[SD((8, D), F32), SD((n, TOK, D), BF), SD((n, TOK, D), BF)],
        compiler_params=params(),
        cost_estimate=cost(2e10, 20 * MB),
        name="last",
    )


def vector_finish_kernel(count, spot_ref, sums_ref, thr_ref, inner_ref, inb_ref, outb_ref, upb_ref, downb_ref, g1_ref, s1_ref,
                         g2_ref, s2_ref, table_ref, clip_ref, factor_ref, max_ref):
    shard = spot_ref[2]

    def part(ref, rows, step=1):
        size = ref.shape[0]
        start = shard * size
        row = sums_ref[pl.ds(rows + step * (start // D), 1), :]
        row = jnp.broadcast_to(row, (8, D))
        ref[...] = pltpu.roll(row, D - start % D, 1)[0:1, :size].reshape(size)

    part(inb_ref, V_IN, 2)
    part(upb_ref, V_UP)
    for i, ref in enumerate((downb_ref, g2_ref, s2_ref, outb_ref)):
        part(ref, V_SMALL + i)
    part(g1_ref, V_ONE)
    part(s1_ref, V_ONE + 1)
    table_ref[...] = sums_ref[V_TABLE : V_TABLE + HEADS, :WIDE].T[: SPAN * SPAN, :]
    top = sums_ref[V_PEAK : V_PEAK + 1, :HEADS]
    factor = thr_ref[...].reshape(1, HEADS)
    factor = factor / jnp.maximum(top, factor)
    max_ref[...] = top.reshape(HEADS)
    factor_ref[...] = factor.reshape(HEADS)
    root = jnp.broadcast_to(jnp.sqrt(factor), (8, HEADS))
    head = lax.broadcasted_iota(jnp.int32, (HEADS, D), 0)
    col = lax.broadcasted_iota(jnp.int32, (HEADS, D), 1) // HD
    scale = lax.dot_general(root, (head == col).astype(F32), (((1,), (0,)), ((), ())), preferred_element_type=F32,
                            precision=lax.Precision.HIGHEST)[0:1, :]
    for k in range(2):
        clip_ref[:, k * D : (k + 1) * D] = (inner_ref[:, k * D : (k + 1) * D].astype(F32) * scale).astype(BF)
    clip_ref[:, 2 * D :] = inner_ref[:, 2 * D :]


def vector_finish(place, sums, threshold, inner, count):
    line = SD((D // count,), F32)
    return single(
        functools.partial(vector_finish_kernel, count), (place, sums, threshold, inner),
        [SD((2 * D // count,), F32), line, SD((FF // count,), F32), line, line, line, line, line,
         SD((SPAN * SPAN, HEADS), F32), SD(inner.shape, BF), SD((HEADS,), F32), SD((HEADS,), F32)],
        cost_estimate=cost(1e7, 3 * MB), name="vector_finish",
    )


def feed_finish_kernel(spot_ref, mine_ref, other_ref, ge_ref, gr_ref):
    for core in range(2):
        @pl.when(spot_ref[1] == core)
        def _():
            for c, ref in ((core, mine_ref), (1 - core, other_ref)):
                for b in range(4):
                    ge_ref[:, (2 * b + c) * CH : (2 * b + c + 1) * CH] = ref[b].astype(F32)
                    r = c * CH + (b // 2) * OWN
                    gr_ref[r : r + OWN, (b % 2) * CH : (b % 2 + 1) * CH] = ref[4 + b].astype(F32)


def feed_finish(spot, mine, other):
    return single(
        feed_finish_kernel, (spot, mine, other), [SD((OWN, FF), F32), SD((2 * CH, D), F32)],
        cost_estimate=cost(1e7, 8 * MB), name="feed_finish",
    )


def inner_columns(p, c):
    if c == 0:
        return [(0, LP, p * LP), (LP, LP // 2, D + p * LP)]
    return [(0, LP // 2, D + p * LP + LP // 2), (LP // 2, LP, 2 * D + p * LP)]


def inner_finish_kernel(spot_ref, mine_ref, other_ref, gi_ref, go_ref):
    for core in range(2):
        @pl.when(spot_ref[1] == core)
        def _():
            for c, ref in ((core, mine_ref), (1 - core, other_ref)):
                for k, p in enumerate((0, 2, 1)):
                    for at, size, put in inner_columns(p, c):
                        gi_ref[:, put : put + size] = ref[k, :, at : at + size].astype(F32)
                go_ref[:, c * CH : (c + 1) * CH] = ref[3].astype(F32)


def inner_finish(spot, mine, other):
    return single(
        inner_finish_kernel, (spot, mine, other), [SD((OWN, 3 * D), F32), SD((OWN, D), F32)],
        cost_estimate=cost(1e7, 4 * MB), name="inner_finish",
    )


def swap(block, axis, bit):
    count = lax.axis_size(axis)
    return lax.ppermute(block, axis, [(i, i ^ bit) for i in range(count) if i ^ bit < count])


def join_vectors(a, b):
    row = lax.broadcasted_iota(jnp.int32, a.shape, 0)
    return jnp.where(row == V_PEAK, jnp.maximum(a, b), a + b)


class Everywhere:
    def __init__(self, sums, ones, direct):
        self.value = [sums, *ones]
        self.flying = []
        self.hops = [("shard", (1, 2, 3)), ("replica", (1,)), ("replica", (2,)), ("half", (1,))]
        if not direct:
            self.hops = [
                (axis, (1 << k,))
                for axis in ("shard", "replica", "half") for k in range((lax.axis_size(axis) - 1).bit_length())
            ]
        self.done = False

    def inputs(self):
        return self.value + self.flying

    def compute(self, values, low, low2):
        v, *others = values
        if not self.flying:
            ones = others[0] + others[1]
            return [jnp.concatenate([v[:V_ONE], ones[:2], v[V_ONE + 2 :]], axis=0)]
        if len(others) == 3:
            return [join_vectors(join_vectors(v, others[0]), join_vectors(others[1], others[2]))]
        return [join_vectors(v, others[0])]

    def launch(self, outs):
        self.value = outs
        self.done = not self.hops
        if self.hops:
            axis, bits = self.hops.pop(0)
            self.flying = [swap(outs[0], axis, bit) for bit in bits]


def near(block):
    return [swap(block, "shard", 1), swap(block, "shard", 2)]


def fence(*values):
    return lax.optimization_barrier(values)


def add(a, b):
    return (a.astype(F32) + b.astype(F32)).astype(BF)


class Reduction:
    def __init__(self, sends, keeps, quarters):
        self.quarters = quarters
        self.keep = keeps
        self.stage = 0
        self.sent = sends
        self.flying = [swap(v, "half", 1) for v in sends]

    def inputs(self):
        return list(self.keep) + list(self.flying)

    def compute(self, values, low, low2):
        hlf = OWN // 2
        kept, got = values[: len(self.keep)], values[len(self.keep) :]
        if self.stage == 0:
            return [add(k[:2], g[:2]) for k, g in zip(kept, got)] + [add(k[2:], g[2:]) for k, g in zip(kept, got)]
        if self.stage == 1:
            return [add(k[0], g[0]) for k, g in zip(kept, got)] + [add(k[1], g[1]) for k, g in zip(kept, got)]
        if self.stage == 2:
            if self.quarters:
                u, v = (add(k, g) for k, g in zip(kept, got))
                return [jnp.where(low, u, v), jnp.where(low, v, u)]
            v = jnp.concatenate([add(k, g) for k, g in zip(kept, got)], axis=0)
            return [jnp.where(low, v[:, :hlf], v[:, hlf:]), jnp.where(low, v[:, hlf:], v[:, :hlf])]
        v = kept[0]
        if self.quarters and self.stage == 3:
            v = add(v, got[0])
            return [jnp.where(low2, v[:, :hlf], v[:, hlf:]), jnp.where(low2, v[:, hlf:], v[:, :hlf])]
        if self.quarters and self.stage == 5:
            return [jnp.concatenate([jnp.where(low2, v, got[0]), jnp.where(low2, got[0], v)], axis=1)]
        if self.quarters and self.stage == 6:
            return [jnp.concatenate([jnp.where(low, v, got[0]), jnp.where(low, got[0], v)], axis=0)]
        if self.stage in (3, 4):
            return [add(v, got[0])]
        return [jnp.concatenate([jnp.where(low, v, got[0]), jnp.where(low, got[0], v)], axis=1)]

    def launch(self, outs):
        if self.stage < 2:
            half = len(outs) // 2
            self.keep, self.sent = outs[:half], outs[half:]
            bits = (1, 2) if self.stage == 0 else (2, 1)
            self.flying = [swap(v, "shard", bit) for v, bit in zip(self.sent, bits)]
        else:
            self.keep, self.sent = outs[:1], outs[-1:]
            if self.stage == (6 if self.quarters else 5):
                self.flying = [swap(self.keep[0], "half", 1)]
            else:
                far = (3, 4) if self.quarters else (3,)
                self.flying = [swap(self.sent[0], "replica", 2 if self.stage in far else 1)]
        self.stage += 1


def hop_kernel(chains, counts, place_ref, *refs):
    replica = place_ref[3]
    low, low2 = (replica & 1) == 0, (replica & 2) == 0
    refs = list(refs)
    inputs = [[refs.pop(0)[...] for _ in range(count)] for count in counts]
    for chain, values in zip(chains, inputs):
        for out in chain.compute(values, low, low2):
            refs.pop(0)[...] = out


def together(place, chains, *others, plain=False):
    flying, others = fence([c.flying for c in chains], others)
    for c, v in zip(chains, flying):
        c.flying = v
    inputs = [c.inputs() for c in chains]
    low, low2 = (place[3] & 1) == 0, (place[3] & 2) == 0
    shapes = [jax.eval_shape(c.compute, v, low, low2) for c, v in zip(chains, inputs)]
    if plain:
        outs = [c.compute(v, low, low2) for c, v in zip(chains, inputs)]
    else:
        flat = [x for v in inputs for x in v]
        results = list(single(
            functools.partial(hop_kernel, chains, [len(v) for v in inputs]), (place, *flat),
            [SD(x.shape, x.dtype) for v in shapes for x in v], cost_estimate=cost(1e7, 4 * MB), name="hop",
        ))
        outs = [[results.pop(0) for _ in v] for v in shapes]
    for c, v in zip(chains, outs):
        c.launch(v)
    return others


def shards(images, cotangent, present, threshold, inner_weight, inner_bias, outer_weight, outer_bias, expand_weight,
           expand_bias, reduce_weight, reduce_bias, first_gain, first_shift, second_gain, second_shift, bias_table):
    n = images.shape[0]
    core = lax.axis_index("half")
    shard = lax.axis_index("shard")
    replica = lax.axis_index("replica")
    shard_count = lax.axis_size("shard")
    quick = shard_count == 4 and lax.axis_size("replica") == 4
    me = shard if quick else jnp.int32(0)
    spot = jnp.stack([me, core]).astype(jnp.int32)
    place = jnp.stack([me, core, shard, replica]).astype(jnp.int32)
    own_images = images.reshape(n, ROWS, D)
    own_grad = cotangent.reshape(n, ROWS, D)
    vectors = (inner_bias, outer_bias, expand_bias, reduce_bias, first_gain, first_shift, second_gain, second_shift)
    order = jnp.asarray(row_order(), BF)
    back_order = jnp.asarray(row_order().T, BF)
    alive = present.astype(F32).reshape(1, n)
    table_rows = jnp.pad(bias_table.astype(F32).T, ((0, 0), (0, WIDE - bias_table.shape[0])))
    if quick:
        first, others, others_half, up = first_call(spot, vectors, inner_weight, own_images, own_grad)
        first, up, spot, others_half = fence(first, up, spot, others_half)
        get_first = near(first)
        upper = swap(up, "half", 1)
        masks_0 = bias_call(0, spot, table_rows)
        get_first, upper, masks_0, others_half = fence(get_first, upper, masks_0, others_half)
        get_first.append(swap(get_first[0], "shard", 2))
        get_others = near(others_half)
        tok, g, grad_down = prep_call(own_images, own_grad, upper, alive, order)
        big = cut_call(spot, outer_weight, expand_weight, reduce_weight)
        get_first, get_others, tok, spot, big = fence(get_first, get_others, tok, spot, big)
        first_pieces = [first] + get_first
        get_others.append(swap(get_others[1], "shard", 1))
        in_bias, up_bias, vecs, n1, n1t = vector_call(spot, first_pieces, tok)
        get_others, n1, big = fence(get_others, n1, big)
        others_back = [swap(v, "half", 1) for v in get_others]
        get_big = near(big)
    else:
        masks_0 = bias_call(0, spot, table_rows)
        upper = jnp.concatenate([swap(own_images[:, :TOK], "half", 1), swap(own_grad[:, :TOK], "half", 1)])
        whole_vectors = [lax.all_gather(v, "shard", axis=0, tiled=True).reshape(4, -1) for v in vectors]
        parts = jnp.stack([jnp.pad(v, ((0, 0), (0, D - v.shape[1]))) for v in whole_vectors], axis=1)
        parts = [jnp.pad(parts[r], ((0, 8), (0, 0))) for r in range(4)]
        thirds = inner_weight.reshape(-1, 3, 3, LP).transpose(0, 2, 1, 3).reshape(-1, 3, 3 * LP)
        first = thirds[:, 0]
        others = thirds[:, 1:].reshape(-1, 6 * LP)

        tok, g, grad_down = prep_call(own_images, own_grad, upper, alive, order)
        in_bias, up_bias, vecs, n1, n1t = vector_call(spot, parts, tok)

    if quick:
        def places(rows):
            at = [me * rows]
            for c in (core, 1 - core):
                at += [(me ^ 1) * rows + c * (rows // 2), (me ^ 2) * rows + c * (rows // 2), (me ^ 3) * rows + c * (rows // 2)]
            return at

        first_at = jnp.stack([(me ^ r) * OWN for r in range(4)]).astype(jnp.int32)
        in_at = jnp.stack(places(OWN)).astype(jnp.int32)

        def in_plan(columns):
            return [(k, 0, OWN if k == 0 else OWN // 2, columns, 3 * LP, 0, 0) for k in range(7)]

        in_plans = [[(k, 0, OWN, 0, 3 * LP, 0, 0) for k in range(4)], in_plan(0), in_plan(3 * LP)]
    else:
        first_at = in_at = jnp.zeros((1,), jnp.int32)
        first_pieces = [lax.all_gather(first, "shard", axis=0, tiled=True)]
        others_pieces = [lax.all_gather(others, "shard", axis=0, tiled=True)]
        in_plans = [[(0, 0, D, k, 3 * LP, 0, 0)] for k in (0, 0, 3 * LP)]

    results = [attend_call(0, n1, in_bias, masks_0, first_at, in_plans[0], first_pieces, [])]
    if quick:
        others_back, results, spot = fence(others_back, results, spot)
    masks_1 = bias_call(1, spot, table_rows)
    masks_2 = bias_call(2, spot, table_rows)
    if quick:
        masks_1, masks_2 = fence(masks_1, masks_2)
        others_pieces = [others] + get_others + others_back
    results.append(attend_call(1, n1, in_bias, masks_1, in_at, in_plans[1], others_pieces, [masks_2]))
    if quick:
        get_big, results, masks_2 = fence(get_big, results, masks_2)
        far = [swap(get_big[0][: BIG // 2], "shard", 2), swap(get_big[1][BIG // 2 :], "shard", 1)]
        big_back = [swap(v, "half", 1) for v in get_big]
    results.append(attend_call(2, n1, in_bias, masks_2, in_at, in_plans[2], others_pieces, []))
    if quick:
        far, big_back, results = fence(far, big_back, results)
        far_back = [swap(v, "half", 1) for v in far]
        far_back, results = fence(far_back, results)
        pieces = [outer_weight, expand_weight, reduce_weight] + get_big + far + big_back + far_back
        hlf = OWN // 2
        plan = [(0, 0, OWN, 0, D, 0, 0)]
        short = places(OWN)
        long = [None] + [c * 4 * CH + (me ^ r) * CH for c in (core, 1 - core) for r in (1, 2, 3)]
        at = [short[0]]
        for k in range(8):
            plan.append((1, 0, OWN, hidden_block(k) * CH, CH, 1, k * CH))
            at.append(short[0])
        for c in range(2):
            plan.append((2, c * CH, CH, 0, D, 2, 0))
            at.append(c * 4 * CH + me * CH)
        parts = [(b * hlf, hlf, 1, b * D) for b in range(4)] + [(4 * hlf, hlf, 0, 0), (5 * hlf, 4 * hlf, 2, 0)]

        def add_piece(source, lo, hi, place):
            for row, rows, target, column in parts:
                a, b = max(row, lo), min(row + rows, hi)
                if a < b and target == 1:
                    for c in range(2):
                        plan.append((source, a - lo, b - a, c * CH, CH, 1, c * 4 * CH + column // 2))
                        at.append(short[place] + (a - row))
                elif a < b:
                    plan.append((source, a - lo, b - a, 0, D, target, column))
                    at.append((long if target == 2 else short)[place] + (a - row))

        for side in range(2):
            for k in range(2):
                add_piece(3 + 4 * side + k, 0, BIG, 1 + 3 * side + k)
            add_piece(5 + 4 * side, 0, BIG // 2, 3 + 3 * side)
            add_piece(6 + 4 * side, BIG // 2, BIG, 3 + 3 * side)
        at = jnp.stack(at).astype(jnp.int32)
    else:
        pieces = [lax.all_gather(v, "shard", axis=0, tiled=True) for v in (outer_weight, expand_weight, reduce_weight)]
        plan, at = [(0, 0, D, 0, D, 0, 0)], [0]
        for k in range(8):
            plan += [(1, 0, D, hidden_block(k) * CH, CH, 1, k * CH), (2, hidden_block(k) * CH, CH, 0, D, 2, 0)]
            at += [0, k * CH]
        at = jnp.asarray(at, jnp.int32)
    projs, pts, atts, peak, ws = zip(*results)
    (stay, send, gmid, datt, out_send, out_keep, e_send, e_keep, r_send, r_keep, grad_up, small) = middle_call(
        spot, tok, atts, g, back_order, vecs, up_bias, at, plan, pieces, []
    )
    def wait_for(chains):
        return [v for c in chains for v in c.sent]

    after = []
    if quick:
        feed = Reduction([e_send, r_send], [e_keep, r_keep], True)
    lower_out = swap(send, "half", 1)
    gp0, db0 = back_call(0, projs[0], pts[0], datt, [])
    if quick:
        gp0, lower_out, projs = together(place, [feed], gp0, lower_out, projs, plain=True)
        after = wait_for([feed])
    gp1, db1 = back_call(1, projs[1], pts[1], datt, after)
    gp2, db2 = back_call(2, projs[2], pts[2], datt, [gp1])
    x_send, x_keep, y_send, y_keep, sums_in = inner_call(spot, n1t, (gp0, gp1, gp2), (out_send, out_keep), [])
    peak = jnp.concatenate(peak, axis=2)
    peaks = jnp.max(jnp.where((present > 0)[:, None, None, None], peak, NEGATIVE), axis=(0, 1, 3)).reshape(1, HEADS)
    after = [x_send]
    if quick:
        x_send, y_send, gp2 = together(place, [feed], x_send, y_send, gp2)
        rest = Reduction([x_send, y_send], [x_keep, y_keep], False)
        after = wait_for([feed])
    half = n // 2
    one_a, gstay_a, gsend_a = last_call(0, half, tok, gmid, vecs, back_order, (gp0, gp1, gp2), ws, after)
    after = [gsend_a]
    if quick:
        gsend_a, one_a = together(place, [rest, feed], gsend_a, one_a)
        after = wait_for([rest, feed])
    lower_a = swap(gsend_a, "half", 1)
    one_b, gstay_b, gsend_b = last_call(half, n - half, tok, gmid, vecs, back_order, (gp0, gp1, gp2), ws, after)
    after = [gsend_b]
    if quick:
        gsend_b, lower_a = together(place, [rest, feed], gsend_b, lower_a)
        after = wait_for([rest, feed])
    lower_b = swap(gsend_b, "half", 1)
    sums = table_call((db0, db1, db2), grad_up, grad_down, small, sums_in, peaks, after)
    every = Everywhere(sums, (one_a, one_b), quick)
    if quick:
        rest.flying, feed.flying, lower_b = fence(rest.flying, feed.flying, lower_b)
        together(place, [rest, every, feed])
        together(place, [rest, every, feed])
        together(place, [rest, every])
        rest.flying, every.flying, feed.flying = fence(rest.flying, every.flying, feed.flying)
        together(place, [rest, every, feed])
        every.flying, feed.flying = fence(every.flying, feed.flying)
        grad_expand, grad_reduce = feed_finish(spot, *feed.keep, *feed.flying)
        together(place, [every])
    else:
        while not every.done:
            together(place, [every])
    sums = every.value[0]

    (grad_inbias, grad_outbias, grad_upbias, grad_downbias, grad_gain_1, grad_shift_1, grad_gain_2, grad_shift_2, grad_table,
     clipped, factors, maxima) = vector_finish(place, sums, threshold, inner_weight, shard_count)

    if quick:
        grad_inner, grad_outer = inner_finish(spot, *rest.keep, *rest.flying)
    else:
        def halves(keep, send, axis):
            lo = jnp.where(core == 0, keep, send)
            hi = jnp.where(core == 0, send, keep)
            return jnp.concatenate([lo, hi], axis=axis)

        def whole(keep, send):
            both = halves(keep[:, :, :, None], send[:, :, :, None], 3)
            return both.transpose(0, 2, 1, 3, 4).reshape(D, -1)

        def settle(v):
            v = lax.psum_scatter(v.astype(BF), "shard", scatter_dimension=0, tiled=True)
            return lax.psum(v, ("replica", "half")).astype(F32)

        def rows_of(v):
            return v.reshape(4, 1, 2, 2, OWN, CH).transpose(0, 1, 2, 4, 3, 5).reshape(4, 1, CH, D)

        def straight(v):
            return jnp.stack([v[0], v[2], v[1], v[3]])

        grad_reduce = settle(halves(rows_of(r_keep), rows_of(r_send), 1).reshape(FF, D))
        grad_expand = settle(whole(straight(e_keep), straight(e_send)))
        grad_outer = settle(whole(out_keep, out_send))
        x_keep, x_send = straight(x_keep), straight(x_send)
        by_third = [
            whole(x_keep[:, :1], x_send[:, :1]), whole(y_keep[:, :1], y_send[:, :1]), whole(x_keep[:, 1:], x_send[:, 1:])
        ]
        by_third = jnp.stack(by_third, axis=1).reshape(D, 3, 3, LP).transpose(0, 2, 1, 3).reshape(D, 3 * D)
        grad_inner = settle(by_third)

    block_out = jnp.concatenate([lower_out, stay], axis=1).reshape(images.shape)
    lower_grad = jnp.concatenate([lower_a, lower_b])
    gstay = jnp.concatenate([gstay_a, gstay_b])
    grad_images = jnp.concatenate([lower_grad, gstay], axis=1).reshape(images.shape)
    return (
        block_out,
        grad_images,
        grad_inner,
        grad_inbias,
        grad_outer,
        grad_outbias,
        grad_expand,
        grad_upbias,
        grad_reduce,
        grad_downbias,
        grad_gain_1,
        grad_shift_1,
        grad_gain_2,
        grad_shift_2,
        grad_table,
        clipped,
        factors,
        maxima,
    )


def solution(mesh):
    rows = P(("replica", "shard"), "half", None, None)
    cut = P("shard", None)
    line = P("shard")
    return jax.shard_map(
        shards,
        mesh=mesh,
        in_specs=(rows, rows, P(("replica", "shard")), P(), cut, line, cut, line, cut, line, cut, line, line, line, line,
                  line, P()),
        out_specs=(rows, rows, cut, line, cut, line, cut, line, cut, line, line, line, line, line, P(), cut, P(), P()),
        check_vma=False,
    )
```

```python
import functools
import math

import numpy as np
import jax
import jax.numpy as jnp
from jax import lax
from jax.experimental import pallas as pl
from jax.experimental.pallas import tpu as pltpu
from jax.sharding import PartitionSpec as P

D = 768
HEADS = 24
HD = 32
WIN = 12
GRID = 24
SHIFT = 6
FF = 3072
TOK = WIN * WIN
ROWS = WIN * GRID
SPAN = 2 * WIN - 1
EPS = 1e-5
MASKED = -100.0
NEGATIVE = -1e30
LOG2E = math.log2(math.e)
BF = jnp.bfloat16
F32 = jnp.float32
MB = 1 << 20
OWN = 192
CH = 384
WIDE = 640
NARROW = 384
TALL = WIN * 16
HB = 8
LB = HB * HD
HP = 8
LP = HP * HD
NB = 576
SCALE = 1e-3
ONE = dict(pipeline_mode=pl.Buffered(1))
SD = jax.ShapeDtypeStruct


def nn(a, b):
    return lax.dot_general(a, b, (((1,), (0,)), ((), ())), preferred_element_type=F32)


def nt(a, b):
    return lax.dot_general(a, b, (((1,), (1,)), ((), ())), preferred_element_type=F32)


def tn(a, b):
    return lax.dot_general(a, b, (((0,), (0,)), ((), ())), preferred_element_type=F32)


def full(shape, **kw):
    return pl.BlockSpec(shape, lambda *_: (0,) * len(shape), **kw)


def any_space():
    return pl.BlockSpec(memory_space=pl.ANY)


def smem():
    return pl.BlockSpec(memory_space=pltpu.SMEM)


def run(kernel, count, args, after, in_specs, **kw):
    def body(*refs):
        kernel(*refs[:count], *refs[count + len(after) :])

    return pl.pallas_call(body, in_specs=list(in_specs) + [any_space()] * len(after), **kw)(*args, *after)


def params(limit=63):
    return pltpu.CompilerParams(vmem_limit_bytes=limit * MB)


def cost(flops, moved, exps=0):
    return pl.CostEstimate(flops=int(flops * SCALE), bytes_accessed=int(moved * SCALE), transcendentals=0)


def whole(array):
    return full(array.shape, **ONE)


def single(kernel, args, out_shape, after=(), scratch=(), **kw):
    specs = [smem() if v.dtype == jnp.int32 else whole(v) for v in args]
    shapes = out_shape if isinstance(out_shape, (list, tuple)) else [out_shape]
    out = run(
        kernel, len(args), args, after, grid=(1,), in_specs=specs, out_specs=[whole(v) for v in shapes], out_shape=list(shapes),
        scratch_shapes=list(scratch), compiler_params=params(), **kw
    )
    return out if isinstance(out_shape, (list, tuple)) else out[0]


def colsum(v):
    return jnp.sum(v, axis=0, keepdims=True)


def norm_parts(x):
    c = x - jnp.mean(x, axis=-1, keepdims=True)
    r = lax.rsqrt(jnp.mean(c * c, axis=-1, keepdims=True) + EPS)
    return c * r, r


def row_order():
    cells = np.arange(ROWS)
    win, rest = cells // TOK, cells % TOK
    a, b = rest // WIN, rest % WIN
    m = np.zeros((ROWS, ROWS), np.float32)
    m[cells, a * GRID + (win * WIN + b + SHIFT) % GRID] = 1
    return m


def spread_q():
    q = np.arange(TOK)
    m = np.zeros((TOK, NARROW), np.float32)
    m[q, SPAN * (q // WIN) + q % WIN] = 1
    return m


def spread_k(reverse):
    k = np.arange(TOK)
    b = k % WIN
    m = np.zeros((TALL, TOK), np.float32)
    m[16 * (k // WIN) + (WIN - 1 - b if reverse else b), k] = 1
    return m


def copies(plan, refs, at, targets, sems):
    for i, (src, row, rows, col, cols, dst, put) in enumerate(plan):
        place = pl.ds(pl.multiple_of(at[i], 16), rows)
        yield pltpu.make_async_copy(
            refs[src].at[pl.ds(row, rows), pl.ds(col, cols)], targets[dst].at[place, pl.ds(put, cols)], sems.at[i]
        )


def hidden_block(k):
    return 2 * (k % 4) + k // 4


def region_masks():
    line = np.arange(GRID)
    region = (line >= GRID - WIN).astype(np.int32) + (line >= GRID - SHIFT).astype(np.int32)
    lab = 3 * region[:, None] + region[None, :]
    lab = lab.reshape(2, WIN, 2, WIN).transpose(0, 2, 1, 3).reshape(2, 2, TOK)
    return np.where(lab[:, :, :, None] != lab[:, :, None, :], MASKED, 0.0).astype(np.float32)


def bias_kernel(spot_ref, table_ref, mask_ref, sq_ref, sk_ref, out_ref, tall):
    masks = [mask_ref[spot_ref[1], w].astype(F32) for w in range(2)]
    for h in range(HP):
        row = pltpu.roll(jnp.broadcast_to(table_ref[h : h + 1, :], (16, WIDE)), 0, 1, stride=1, stride_axis=0)
        for a in range(WIN):
            off = (SPAN * a - SPAN * (WIN - 1) - (WIN - 1)) % WIDE
            tall[16 * a : 16 * a + 16, :] = pltpu.roll(row, off, 1)[:, :NARROW].astype(BF)
        wide = nn(tall[...], sq_ref[...]).astype(BF)
        bias = nn(sk_ref[...], wide)
        for w in range(2):
            out_ref[w, h] = (bias + masks[w]) * LOG2E


def bias_call(group, spot, table):
    args = (spot, table, jnp.asarray(region_masks(), BF), jnp.asarray(spread_q().T, BF), jnp.asarray(spread_k(False).T, BF))
    out = SD((2, HP, TOK, TOK), F32)
    return pl.pallas_call(
        bias_kernel,
        grid=(1,),
        in_specs=[smem(), pl.BlockSpec((HP, WIDE), lambda i: (group, 0))] + [whole(v) for v in args[2:]],
        out_specs=whole(out),
        out_shape=out,
        scratch_shapes=[pltpu.VMEM((TALL, NARROW), BF)],
        compiler_params=params(),
        cost_estimate=cost(2e9, 3 * MB),
        name="bias",
    )(*args)


V_UP, V_SMALL, V_IN, V_ONE, V_PEAK, V_TABLE, V_ROWS = 0, 4, 8, 11, 13, 16, 40


def table_kernel(db0_ref, db1_ref, db2_ref, up_ref, down_ref, small_ref, in_ref, peak_ref, sq_ref, sk_ref, out_ref):
    def split(v):
        hi = v.astype(BF)
        return hi, (v - hi.astype(F32)).astype(BF)

    out_ref[...] = jnp.zeros_like(out_ref)
    for k in range(8):
        b = hidden_block(k)
        out_ref[V_UP + b // 2 : V_UP + b // 2 + 1, (b % 2) * CH : (b % 2 + 1) * CH] = up_ref[
            k // 2, :, (k % 2) * CH : (k % 2 + 1) * CH
        ]
    out_ref[V_SMALL : V_SMALL + 1, :] = down_ref[...]
    out_ref[V_SMALL + 1 : V_SMALL + 4, :] = small_ref[1:4, :]
    for p in range(3):
        row = in_ref[p]
        for k in range(3):
            out_ref[V_IN + k : V_IN + k + 1, p * LP : (p + 1) * LP] = row[:, k * LP : (k + 1) * LP]
    out_ref[V_PEAK : V_PEAK + 1, :HEADS] = peak_ref[...]
    for h in range(HEADS):
        hi, lo = split((db0_ref, db1_ref, db2_ref)[h // HP][h % HP])
        tall = nn(sk_ref[...], hi) + nn(sk_ref[...], lo)
        hi, lo = split(tall)
        wide = nn(hi, sq_ref[...]) + nn(lo, sq_ref[...])
        wide = jnp.concatenate([wide, jnp.zeros((TALL, WIDE - NARROW), F32)], axis=1)
        tot = jnp.zeros((16, WIDE), F32)
        for a in range(WIN):
            tot = tot + pltpu.roll(wide[16 * a : 16 * a + 16, :], SPAN * (WIN - 1 - a), 1)
        tot = pltpu.roll(tot, 0, 1, stride=1, stride_axis=0)
        out_ref[V_TABLE + h : V_TABLE + h + 1, :WIDE] = colsum(tot)


def table_call(dbs, up, down, small, sums_in, peaks, after):
    args = (*dbs, up, down, small, sums_in, peaks, jnp.asarray(spread_q(), BF), jnp.asarray(spread_k(True), BF))
    return single(table_kernel, args, SD((V_ROWS, D), F32), after, cost_estimate=cost(6e9, 4 * MB), name="table")


def lane_head(shape):
    return lax.broadcasted_iota(jnp.int32, shape, len(shape) - 1) // HD


VECTORS = (2 * D, D, FF, D, D, D, D, D)


def first_kernel(spot_ref, *refs):
    vecs, (inner_ref, own_ref, gown_ref, first_ref, others_ref, half_ref, up_ref) = refs[:8], refs[8:]
    n = own_ref.shape[0]
    up_ref[:n] = own_ref[...]
    up_ref[n:] = gown_ref[...]
    mine = pl.ds(pl.multiple_of(spot_ref[1] * (OWN // 2), 16), OWN // 2)
    for k in range(3):
        first_ref[:OWN, k * LP : (k + 1) * LP] = inner_ref[:, k * D : k * D + LP]
        for p in (1, 2):
            src = slice(k * D + p * LP, k * D + (p + 1) * LP)
            dst = slice(((p - 1) * 3 + k) * LP, ((p - 1) * 3 + k + 1) * LP)
            others_ref[:, dst] = inner_ref[:, src]
            half_ref[:, dst] = inner_ref[mine, src]
    rows = [jnp.zeros((8, D), F32)]
    for v in vecs:
        row = v[...].astype(F32).reshape(1, v.shape[0])
        if v.shape[0] < D:
            row = jnp.concatenate([row, jnp.zeros((1, D - v.shape[0]), F32)], axis=1)
        rows.insert(-1, row)
    first_ref[OWN:, :] = jnp.concatenate(rows, axis=0).astype(BF)


def first_call(spot, vectors, inner, own, gown):
    n = own.shape[0]
    top = full((n, TOK, D))
    shapes = [SD((OWN + 16, D), BF), SD((OWN, 6 * LP), BF), SD((OWN // 2, 6 * LP), BF), SD((2 * n, TOK, D), BF)]
    return pl.pallas_call(
        first_kernel,
        grid=(1,),
        in_specs=[smem()] + [whole(v) for v in vectors] + [whole(inner), top, top],
        out_specs=[whole(v) for v in shapes],
        out_shape=shapes,
        compiler_params=params(),
        cost_estimate=cost(1e6, 6 * MB),
        name="first",
    )(spot, *vectors, inner, own, gown)


BIG = 4 * (OWN // 2) + OWN // 2 + 2 * OWN


def cut_kernel(spot_ref, outer_ref, expand_ref, reduce_ref, big_ref):
    core = spot_ref[1]
    hlf = OWN // 2
    mine = pl.ds(pl.multiple_of(core * hlf, 16), hlf)
    for k in range(4):
        big_ref[k * hlf : (k + 1) * hlf, :] = expand_ref[mine, k * D : (k + 1) * D]
    big_ref[4 * hlf : 5 * hlf, :] = outer_ref[mine, :]
    big_ref[5 * hlf :, :] = reduce_ref[pl.ds(pl.multiple_of(core * 2 * OWN, 16), 2 * OWN), :]


def cut_call(spot, outer, expand, reduce):
    return single(
        cut_kernel, (spot, outer, expand, reduce), [SD((BIG, D), BF)], cost_estimate=cost(1e6, 3 * MB), name="cut"
    )[0]


def prep_kernel(own_ref, gown_ref, recv_ref, alive_ref, pm_ref, tok_ref, g_ref, sum_ref):
    n = own_ref.shape[0]
    tot = jnp.zeros((1, D), F32)
    for i in range(n):
        tok_ref[i] = nn(pm_ref[...], jnp.concatenate([own_ref[i, TOK:, :], recv_ref[i]], axis=0)).astype(BF)
        g = nn(pm_ref[...], jnp.concatenate([gown_ref[i, TOK:, :], recv_ref[n + i]], axis=0)) * alive_ref[0:1, i : i + 1]
        g_ref[i] = g.astype(BF)
        tot = tot + colsum(g)
    sum_ref[...] = tot


def prep_call(own, gown, recv, alive, pm):
    rows = SD(own.shape, BF)
    return single(
        prep_kernel, (own, gown, recv, alive, pm), [rows, rows, SD((1, D), F32)], cost_estimate=cost(3e9, 16 * MB), name="prep"
    )


def vector_kernel(spot_ref, pa_ref, pb_ref, pc_ref, pd_ref, tok_ref, inb_ref, up_ref, vec_ref, n1_ref, n1t_ref, parts):
    n = tok_ref.shape[0]
    for r, ref in enumerate((pa_ref, pb_ref, pc_ref, pd_ref)):
        parts[jnp.bitwise_xor(spot_ref[0], r)] = ref[:8, :].astype(F32)

    def vector(i):
        size = VECTORS[i] // 4
        return jnp.concatenate([parts[s][i : i + 1, :size] for s in range(4)], axis=1)

    vin = vector(0)
    for p in range(3):
        inb_ref[p] = jnp.concatenate(
            [vin[:, p * LP : (p + 1) * LP], jnp.zeros((1, LP), F32), vin[:, D + p * LP : D + (p + 1) * LP]], axis=1
        )
    vup = vector(2)
    for k in range(8):
        up_ref[k // 2, :, (k % 2) * CH : (k % 2 + 1) * CH] = vup[:, hidden_block(k) * CH : (hidden_block(k) + 1) * CH]
    gain, shift = vector(4), vector(5)
    vec_ref[...] = jnp.zeros_like(vec_ref)
    for r, v in enumerate((vector(1), vector(3), gain, vector(6), vector(7))):
        vec_ref[r : r + 1, :] = v
    for i in range(n):
        xh, _ = norm_parts(tok_ref[i].astype(F32))
        n1 = (xh * gain + shift).astype(BF)
        n1_ref[i] = n1
        n1t_ref[:, i * ROWS : (i + 1) * ROWS] = n1.T


def vector_call(spot, parts, tok):
    n = tok.shape[0]
    last = parts[0].shape[0] // 16 - 1
    shapes = [SD((3, 1, 3 * LP), F32), SD((4, 1, 2 * CH), F32), SD((8, D), F32), SD(tok.shape, BF), SD((D, n * ROWS), BF)]
    return pl.pallas_call(
        vector_kernel,
        grid=(1,),
        in_specs=[smem()] + [pl.BlockSpec((16, D), lambda i: (last, 0))] * 4 + [whole(tok)],
        out_specs=[whole(v) for v in shapes],
        out_shape=shapes,
        scratch_shapes=[pltpu.VMEM((4, 8, D), F32)],
        compiler_params=params(),
        cost_estimate=cost(5e9, 8 * MB),
        name="vectors",
    )(spot, *parts, tok)


def attend_kernel(plan, count, n1_ref, b_ref, bm_ref, at_ref, *rest):
    pieces = rest[:count]
    proj_ref, pt_ref, att_ref, peak_ref, w_ref, sems = rest[count:]

    @pl.when(pl.program_id(0) == 0)
    def _():
        for c in copies(plan, pieces, at_ref, (w_ref,), sems):
            c.start()
        for c in copies(plan, pieces, at_ref, (w_ref,), sems):
            c.wait()

    proj_ref[0] = (nn(n1_ref[0], w_ref[...]) + b_ref[0]).astype(BF)
    hid = lane_head((TOK, LB))
    scale = HD**-0.5
    for w in range(2):
        r = slice(w * TOK, (w + 1) * TOK)
        for blk in range(LP // LB):
            l = blk * LB
            q = proj_ref[0, r, l : l + LB]
            k = proj_ref[0, r, LP + l : LP + l + LB]
            v = proj_ref[0, r, 2 * LP + l : 2 * LP + l + LB]
            vt = v.T
            apart = jnp.concatenate([jnp.where(hid == h, k, jnp.zeros_like(k)) for h in range(HB)], axis=0)
            sts = nn(apart, q.T)
            outs = []
            for h in range(HB):
                hh = blk * HB + h
                st = sts[h * TOK : (h + 1) * TOK]
                peak_ref[0, w, hh : hh + 1, :] = jnp.max(st, axis=0, keepdims=True) * scale
                t = st * (scale * LOG2E) + bm_ref[w, hh]
                e = jnp.exp2(t - jnp.max(t, axis=0, keepdims=True))
                p = (e * (1.0 / colsum(e))).astype(BF)
                pt_ref[0, w, hh] = p
                outs.append(nn(vt[HD * h : HD * h + HD, :], p))
            att_ref[0, r, l : l + LB] = jnp.concatenate(outs, axis=0).astype(BF).T


def attend_call(group, n1, b, bm, at, plan, pieces, after):
    n = n1.shape[0]

    def blk(*s):
        return pl.BlockSpec((1,) + s, lambda i: (i,) + (0,) * len(s))

    return run(
        functools.partial(attend_kernel, plan, len(pieces)), 4 + len(pieces), (n1, b, bm, at, *pieces), after,
        grid=(n,),
        in_specs=[blk(ROWS, D), pl.BlockSpec((1, 1, 3 * LP), lambda i: (group, 0, 0)), full((2, HP, TOK, TOK), **ONE), smem()]
        + [any_space()] * len(pieces),
        out_specs=[blk(ROWS, 3 * LP), blk(2, HP, TOK, TOK), blk(ROWS, LP), blk(2, HP, TOK), full((D, 3 * LP), **ONE)],
        out_shape=[SD((n, ROWS, 3 * LP), BF), SD((n, 2, HP, TOK, TOK), BF), SD((n, ROWS, LP), BF), SD((n, 2, HP, TOK), F32),
                   SD((D, 3 * LP), BF)],
        scratch_shapes=[pltpu.SemaphoreType.DMA((len(plan),))],
        compiler_params=params(),
        cost_estimate=cost(1.3e10, 12 * MB, 1.4e6),
        name="attend",
    )


def gelu_parts(h):
    d = 1.0 + (0.3275911 * 0.5**0.5) * jnp.abs(h)
    t = pl.reciprocal(d, approx=True)
    t = t * (2.0 - d * t)
    e = jnp.exp2(h * h * (-0.5 * LOG2E))
    p = (((0.5 * 1.061405429) * t - 0.5 * 1.453152027) * t + 0.5 * 1.421413741) * t - 0.5 * 0.284496736
    p = (p * t + 0.5 * 0.254829592) * t * e
    cdf = jnp.where(h >= 0, 1.0 - p, p)
    return cdf, cdf + h * (e * ((2 * math.pi) ** -0.5))


def middle_kernel(plan, count, spot_ref, tok_ref, att0_ref, att1_ref, att2_ref, gin_ref, pmt_ref, vec_ref, eb_ref,
                  at_ref, *rest):
    pieces = rest[:count]
    (stay_ref, send_ref, gmid_ref, datt_ref, os_ref, ok_ref, es_ref, ek_ref, rs_ref, rk_ref, geb_ref, small_ref,
     wo, we, wr, mid, n2, g, n2t, acc, e2, act, gh, sems) = rest[count:]
    j = pl.program_id(0)
    n = tok_ref.shape[0]
    N = n * ROWS
    me = spot_ref[0]
    core = spot_ref[1]
    early = [k for k, entry in enumerate(plan) if entry[5] == 0]
    out_b, red_b, gain, shift = vec_ref[0:1, :], vec_ref[1:2, :], vec_ref[3:4, :], vec_ref[4:5, :]

    def attended(i):
        return jnp.concatenate([att0_ref[i], att1_ref[i], att2_ref[i]], axis=-1)

    @pl.when(j == 0)
    def _():
        moves = list(copies(plan, pieces, at_ref, (wo, we, wr), sems))
        for c in moves:
            c.start()
        for k in early:
            moves[k].wait()
        for i in range(n):
            s = slice(i * ROWS, (i + 1) * ROWS)
            g[s, :] = gin_ref[i]
            m = tok_ref[i].astype(F32) + nn(attended(i), wo[...]) + out_b
            mid[s, :] = m
            xh, _ = norm_parts(m)
            x2 = (xh * gain + shift).astype(BF)
            n2[s, :] = x2
            n2t[:, s] = x2.T
            acc[s, :] = m + red_b
            e2[s, :] = jnp.zeros((ROWS, D), F32)
        for k, c in enumerate(moves):
            if k not in early:
                c.wait()

    at = pl.multiple_of((2 * jnp.bitwise_xor(core, 1 - j // 2) + j % 2) * 2 * CH, 2 * CH)
    cols = pl.ds(at, 2 * CH)
    tot = jnp.zeros((1, 2 * CH), F32)
    for s0 in range(0, N, NB):
        s = slice(s0, s0 + NB)
        h = nn(n2[s, :], we[:, cols]) + eb_ref[0]
        cdf, dg = gelu_parts(h)
        act[s, :] = (h * cdf).astype(BF)
        x = (nt(g[s, :], wr[cols, :]) * dg).astype(BF)
        gh[s, :] = x
        tot = tot + colsum(x.astype(F32))
    geb_ref[0] = tot
    ge = nn(n2t[...], gh[...]).astype(BF)
    gr = tn(act[...], g[...]).astype(BF)

    def put(e_ref, r_ref):
        for t in range(2):
            for b in range(4):
                e_ref[crossed(jnp.bitwise_xor(me, b)), t] = ge[b * OWN : (b + 1) * OWN, t * CH : (t + 1) * CH]
                r_ref[jnp.bitwise_xor(me % 2, t), b] = gr[
                    t * CH + (b // 2) * OWN : t * CH + (b // 2 + 1) * OWN, (b % 2) * CH : (b % 2 + 1) * CH
                ]

    @pl.when(j < 2)
    def _():
        put(es_ref, rs_ref)

    @pl.when(j >= 2)
    def _():
        put(ek_ref, rk_ref)

    for s0 in range(0, N, NB):
        s = slice(s0, s0 + NB)
        acc[s, :] += nn(act[s, :], wr[cols, :])
        e2[s, :] += nt(gh[s, :], we[:, cols])

    @pl.when(j == 3)
    def _():
        gn = jnp.zeros((1, D), F32)
        shf = gn
        ob = gn
        for i in range(n):
            s = slice(i * ROWS, (i + 1) * ROWS)
            o = nn(pmt_ref[...], acc[s, :].astype(BF)).astype(BF)
            stay_ref[i] = o[:TOK]
            send_ref[i] = o[TOK:]
            xh, r = norm_parts(mid[s, :])
            d = e2[s, :]
            gn = gn + colsum(d * xh)
            shf = shf + colsum(d)
            d = d * gain
            gm = g[s, :].astype(F32) + r * (
                d - jnp.mean(d, axis=-1, keepdims=True) - xh * jnp.mean(d * xh, axis=-1, keepdims=True)
            )
            gmid_ref[i] = gm
            gb = gm.astype(BF)
            ob = ob + colsum(gb.astype(F32))
            g[s, :] = gb
            datt_ref[i] = nt(gb, wo[...]).astype(BF)
            n2[s, :] = attended(i)
        for c, ref in ((1 - core, os_ref), (core, ok_ref)):
            go = tn(n2[...], g[:, pl.ds(pl.multiple_of(c * CH, 128), CH)]).astype(BF)
            for b in range(4):
                ref[jnp.bitwise_xor(me, b), 0] = go[b * OWN : (b + 1) * OWN, :]
        small_ref[1:2, :] = gn
        small_ref[2:3, :] = shf
        small_ref[3:4, :] = ob


def crossed(r):
    return 2 * (r % 2) + r // 2


def middle_call(spot, tok, atts, g, pmt, vecs, eb, at, plan, pieces, after):
    n = tok.shape[0]
    N = n * ROWS
    blocks = SD((4, 4, OWN, CH), BF)

    def chunk(j, spot):
        return 2 * jnp.bitwise_xor(spot[1], 1 - j // 2) + j % 2

    def early(j):
        return jnp.minimum(j, 1)

    def late(j):
        return jnp.maximum(j, 2) - 2

    rows = full((n, ROWS, D), **ONE)
    third = full((n, ROWS, LP), **ONE)
    cut = full((n, TOK, D), **ONE)
    outer = full((4, 1, OWN, CH), **ONE)
    args = (spot, tok, *atts, g, pmt, vecs, eb, at, *pieces)

    def body(*refs):
        middle_kernel(plan, len(pieces), *refs[: len(args)], *refs[len(args) + len(after) :])

    grid_spec = pltpu.PrefetchScalarGridSpec(
        num_scalar_prefetch=1,
        grid=(4,),
        in_specs=[rows, third, third, third, rows, full((ROWS, ROWS)), full((8, D)),
                  pl.BlockSpec((1, 1, 2 * CH), lambda j, spot: (chunk(j, spot), 0, 0)), smem()]
        + [any_space()] * (len(pieces) + len(after)),
        out_specs=[cut, cut, rows, rows, outer, outer,
                   pl.BlockSpec((4, 2, OWN, CH), lambda j, spot: (0, early(j), 0, 0)),
                   pl.BlockSpec((4, 2, OWN, CH), lambda j, spot: (0, late(j), 0, 0)),
                   pl.BlockSpec((2, 4, OWN, CH), lambda j, spot: (jnp.bitwise_xor(early(j), spot[0] // 2), 0, 0, 0)),
                   pl.BlockSpec((2, 4, OWN, CH), lambda j, spot: (jnp.bitwise_xor(late(j), spot[0] // 2), 0, 0, 0)),
                   pl.BlockSpec((1, 1, 2 * CH), lambda j, spot: (chunk(j, spot), 0, 0)), full((8, D))],
        scratch_shapes=[pltpu.VMEM((D, D), BF), pltpu.VMEM((D, FF), BF), pltpu.VMEM((FF, D), BF),
                        pltpu.VMEM((N, D), F32), pltpu.VMEM((N, D), BF), pltpu.VMEM((N, D), BF), pltpu.VMEM((D, N), BF),
                        pltpu.VMEM((N, D), F32), pltpu.VMEM((N, D), F32), pltpu.VMEM((N, 2 * CH), BF), pltpu.VMEM((N, 2 * CH), BF),
                        pltpu.SemaphoreType.DMA((len(plan),))],
    )
    return pl.pallas_call(
        body,
        grid_spec=grid_spec,
        out_shape=[SD((n, TOK, D), BF), SD((n, TOK, D), BF), SD((n, ROWS, D), F32), SD((n, ROWS, D), BF),
                   SD((4, 1, OWN, CH), BF), SD((4, 1, OWN, CH), BF), blocks, blocks, blocks, blocks,
                   SD((4, 1, 2 * CH), F32), SD((8, D), F32)],
        compiler_params=params(62),
        cost_estimate=cost(6e10, 40 * MB, 7e6),
        name="middle",
    )(*args, *after)


def back_kernel(proj_ref, pt_ref, da_ref, gp_ref, db_ref):
    @pl.when(pl.program_id(0) == 0)
    def _():
        db_ref[...] = jnp.zeros_like(db_ref)

    hid = lane_head((TOK, LB))
    scale = HD**-0.5
    for w in range(2):
        r = slice(w * TOK, (w + 1) * TOK)
        for blk in range(LP // LB):
            l = blk * LB
            q = proj_ref[0, r, l : l + LB]
            k = proj_ref[0, r, LP + l : LP + l + LB]
            v = proj_ref[0, r, 2 * LP + l : 2 * LP + l + LB]
            do = da_ref[0, r, l : l + LB]
            qt, kt, dt = q.T, k.T, do.T
            dq, dk, dv = [], [], []
            dps = nn(jnp.concatenate([jnp.where(hid == h, v, jnp.zeros_like(v)) for h in range(HB)], axis=0), dt)
            for h in range(HB):
                hh = blk * HB + h
                s = slice(HD * h, HD * h + HD)
                dp = dps[h * TOK : (h + 1) * TOK]
                pb = pt_ref[0, w, hh]
                p = pb.astype(F32)
                pd = p * dp
                ds = pd - p * colsum(pd)
                db_ref[hh] += ds
                dsb = ds.astype(BF)
                dq.append(nn(kt[s, :], dsb))
                dk.append(nt(qt[s, :], dsb))
                dv.append(nt(dt[s, :], pb))
            gp_ref[0, r, l : l + LB] = (jnp.concatenate(dq, axis=0) * scale).astype(BF).T
            gp_ref[0, r, LP + l : LP + l + LB] = (jnp.concatenate(dk, axis=0) * scale).astype(BF).T
            gp_ref[0, r, 2 * LP + l : 2 * LP + l + LB] = jnp.concatenate(dv, axis=0).astype(BF).T


def back_call(group, proj, pt, da, after):
    n = proj.shape[0]

    def blk(*s):
        return pl.BlockSpec((1,) + s, lambda i: (i,) + (0,) * len(s))

    return run(
        back_kernel, 3, (proj, pt, da), after,
        grid=(n,),
        in_specs=[blk(ROWS, 3 * LP), blk(2, HP, TOK, TOK), pl.BlockSpec((1, ROWS, LP), lambda i: (i, 0, group))],
        out_specs=[blk(ROWS, 3 * LP), full((HP, TOK, TOK))],
        out_shape=[SD((n, ROWS, 3 * LP), BF), SD((HP, TOK, TOK), F32)],
        compiler_params=params(),
        cost_estimate=cost(1.8e10, 10 * MB),
        name="attend_back",
    )


def inner_kernel(spot_ref, n1t_ref, gp0_ref, gp1_ref, gp2_ref, os_ref, ok_ref, xs_ref, xk_ref, ys_ref, yk_ref, sum_ref):
    me = spot_ref[0]
    core = spot_ref[1]
    n = gp0_ref.shape[0]
    ys_ref[:, 1:2] = os_ref[...]
    yk_ref[:, 1:2] = ok_ref[...]
    for p, gp_ref, send, keep, m in ((0, gp0_ref, xs_ref, xk_ref, 0), (1, gp1_ref, ys_ref, yk_ref, 0), (2, gp2_ref, xs_ref, xk_ref, 1)):
        gp = gp_ref[...].reshape(n * ROWS, 3 * LP)
        sum_ref[p] = colsum(gp.astype(F32))
        gi = nn(n1t_ref[...], gp).astype(BF)

        for c in range(2):
            @pl.when(core == c)
            def _():
                for b in range(4):
                    r = slice(b * OWN, (b + 1) * OWN)
                    rel = jnp.bitwise_xor(me, b)
                    rel = rel if p == 1 else crossed(rel)
                    keep[rel, m] = gi[r, c * CH : (c + 1) * CH]
                    send[rel, m] = gi[r, (1 - c) * CH : (2 - c) * CH]


def inner_call(spot, n1t, gps, outer, after):
    block = SD((4, 2, OWN, CH), BF)
    return single(
        inner_kernel, (spot, n1t, *gps, *outer), [block] * 4 + [SD((3, 1, 3 * LP), F32)], after,
        cost_estimate=cost(1.2e10, 12 * MB), name="inner_grad",
    )


def last_kernel(tok_ref, gmid_ref, vec_ref, pmt_ref, gp0_ref, gp1_ref, gp2_ref, w0_ref, w1_ref, w2_ref,
                small_ref, stay_ref, send_ref):
    @pl.when(pl.program_id(0) == 0)
    def _():
        small_ref[...] = jnp.zeros_like(small_ref)

    d = nt(gp0_ref[0], w0_ref[...]) + nt(gp1_ref[0], w1_ref[...]) + nt(gp2_ref[0], w2_ref[...])
    xh, r = norm_parts(tok_ref[0].astype(F32))
    small_ref[0:1, :] += colsum(d * xh)
    small_ref[1:2, :] += colsum(d)
    d = d * vec_ref[2:3, :]
    gm = gmid_ref[0] + r * (d - jnp.mean(d, axis=-1, keepdims=True) - xh * jnp.mean(d * xh, axis=-1, keepdims=True))
    o = nn(pmt_ref[...], gm.astype(BF)).astype(BF)
    stay_ref[0] = o[:TOK]
    send_ref[0] = o[TOK:]


def last_call(first, n, tok, gmid, gain, pmt, gps, ws, after):
    def blk(*s):
        return pl.BlockSpec((1,) + s, lambda i: (first + i,) + (0,) * len(s))

    cut = pl.BlockSpec((1, TOK, D), lambda i: (i, 0, 0))

    return run(
        last_kernel, 10, (tok, gmid, gain, pmt, *gps, *ws), after,
        grid=(n,),
        in_specs=[blk(ROWS, D), blk(ROWS, D), full((8, D)), full((ROWS, ROWS))] + [blk(ROWS, 3 * LP)] * 3
        + [full((D, 3 * LP), **ONE)] * 3,
        out_specs=[full((8, D)), cut, cut],
        out_shape=[SD((8, D), F32), SD((n, TOK, D), BF), SD((n, TOK, D), BF)],
        compiler_params=params(),
        cost_estimate=cost(2e10, 20 * MB),
        name="last",
    )


def vector_finish_kernel(count, spot_ref, mine_ref, other_ref, thr_ref, inner_ref, inb_ref, outb_ref, upb_ref, downb_ref, g1_ref, s1_ref,
                         g2_ref, s2_ref, table_ref, clip_ref, factor_ref, max_ref, sums_ref):
    shard = spot_ref[2]
    sums_ref[...] = join_vectors(mine_ref[...], other_ref[...])

    def part(ref, rows, step=1):
        size = ref.shape[0]
        start = shard * size
        row = sums_ref[pl.ds(rows + step * (start // D), 1), :]
        row = jnp.broadcast_to(row, (8, D))
        ref[...] = pltpu.roll(row, (D - start % D) % D, 1)[0:1, :size].reshape(size)

    part(inb_ref, V_IN, 2)
    part(upb_ref, V_UP)
    for i, ref in enumerate((downb_ref, g2_ref, s2_ref, outb_ref)):
        part(ref, V_SMALL + i)
    part(g1_ref, V_ONE)
    part(s1_ref, V_ONE + 1)
    table_ref[...] = sums_ref[V_TABLE : V_TABLE + HEADS, : SPAN * SPAN]
    top = sums_ref[V_PEAK : V_PEAK + 1, :HEADS]
    factor = thr_ref[...].reshape(1, HEADS)
    factor = factor / jnp.maximum(top, factor)
    max_ref[...] = top.reshape(HEADS)
    factor_ref[...] = factor.reshape(HEADS)
    root = jnp.broadcast_to(jnp.sqrt(factor), (8, HEADS))
    head = lax.broadcasted_iota(jnp.int32, (HEADS, D), 0)
    col = lax.broadcasted_iota(jnp.int32, (HEADS, D), 1) // HD
    scale = lax.dot_general(root, (head == col).astype(F32), (((1,), (0,)), ((), ())), preferred_element_type=F32,
                            precision=lax.Precision.HIGHEST)[0:1, :]
    for k in range(2):
        clip_ref[:, k * D : (k + 1) * D] = (inner_ref[:, k * D : (k + 1) * D].astype(F32) * scale).astype(BF)
    clip_ref[:, 2 * D :] = inner_ref[:, 2 * D :]


def vector_finish(place, mine, other, threshold, inner, count):
    line = SD((D // count,), F32)
    return single(
        functools.partial(vector_finish_kernel, count), (place, mine, other, threshold, inner),
        [SD((2 * D // count,), F32), line, SD((FF // count,), F32), line, line, line, line, line,
         SD((HEADS, SPAN * SPAN), F32), SD(inner.shape, BF), SD((HEADS,), F32), SD((HEADS,), F32)],
        scratch=[pltpu.VMEM((V_ROWS, D), F32)],
        cost_estimate=cost(1e7, 3 * MB), name="vector_finish",
    )


def feed_finish_kernel(spot_ref, mine_ref, other_ref, ge_ref, gr_ref):
    for core in range(2):
        @pl.when(spot_ref[1] == core)
        def _():
            for c, ref in ((core, mine_ref), (1 - core, other_ref)):
                for b in range(4):
                    ge_ref[:, (2 * b + c) * CH : (2 * b + c + 1) * CH] = ref[b].astype(F32)
                    r = c * CH + (b // 2) * OWN
                    gr_ref[r : r + OWN, (b % 2) * CH : (b % 2 + 1) * CH] = ref[4 + b].astype(F32)


def inner_columns(p, c):
    if c == 0:
        return [(0, LP, p * LP), (LP, LP // 2, D + p * LP)]
    return [(0, LP // 2, D + p * LP + LP // 2), (LP // 2, LP, 2 * D + p * LP)]


def inner_finish_kernel(spot_ref, mine_ref, other_ref, gi_ref, go_ref):
    for core in range(2):
        @pl.when(spot_ref[1] == core)
        def _():
            for c, ref in ((core, mine_ref), (1 - core, other_ref)):
                for k, p in enumerate((0, 2, 1)):
                    for at, size, put in inner_columns(p, c):
                        gi_ref[:, put : put + size] = ref[k, :, at : at + size].astype(F32)
                go_ref[:, c * CH : (c + 1) * CH] = ref[3].astype(F32)


def finish_kernel(count, place_ref, mine_ref, other_ref, thr_ref, inner_ref, fm_ref, fo_ref, im_ref, io_ref, *outs):
    vectors, (ge_ref, gr_ref, gi_ref, go_ref, sums_ref) = outs[:12], outs[12:]
    inner_finish_kernel(place_ref, im_ref, io_ref, gi_ref, go_ref)
    feed_finish_kernel(place_ref, fm_ref, fo_ref, ge_ref, gr_ref)
    vector_finish_kernel(count, place_ref, mine_ref, other_ref, thr_ref, inner_ref, *vectors, sums_ref)


def finish(place, vectors, threshold, inner, feed, rest):
    line = SD((D // 4,), F32)
    return single(
        functools.partial(finish_kernel, 4), (place, *vectors, threshold, inner, *feed, *rest),
        [SD((2 * D // 4,), F32), line, SD((FF // 4,), F32), line, line, line, line, line,
         SD((HEADS, SPAN * SPAN), F32), SD(inner.shape, BF), SD((HEADS,), F32), SD((HEADS,), F32),
         SD((OWN, FF), F32), SD((2 * CH, D), F32), SD((OWN, 3 * D), F32), SD((OWN, D), F32)],
        scratch=[pltpu.VMEM((V_ROWS, D), F32)], cost_estimate=cost(1e7, 12 * MB), name="finish",
    )


def swap(block, axis, bit):
    count = lax.axis_size(axis)
    return lax.ppermute(block, axis, [(i, i ^ bit) for i in range(count) if i ^ bit < count])


def join_vectors(a, b):
    row = lax.broadcasted_iota(jnp.int32, a.shape, 0)
    return jnp.where(row == V_PEAK, jnp.maximum(a, b), a + b)


class Everywhere:
    def __init__(self, sums, ones, direct):
        self.value = [sums, *ones]
        self.flying = []
        self.hops = [("replica", (1,)), ("shard", (1, 2, 3)), ("replica", (2,)), ("half", (1,))]
        if not direct:
            self.hops = [
                (axis, (1 << k,))
                for axis in ("shard", "replica", "half") for k in range((lax.axis_size(axis) - 1).bit_length())
            ]
        self.done = False

    def inputs(self):
        return self.value + self.flying

    def compute(self, values, low, low2):
        v, *others = values
        if not self.flying:
            ones = others[0] + others[1]
            return [jnp.concatenate([v[:V_ONE], ones[:2], v[V_ONE + 2 :]], axis=0)]
        if len(others) == 3:
            return [join_vectors(join_vectors(v, others[0]), join_vectors(others[1], others[2]))]
        return [join_vectors(v, others[0])]

    def launch(self, outs):
        self.value = outs
        self.done = not self.hops
        if self.hops:
            axis, bits = self.hops.pop(0)
            self.flying = [swap(outs[0], axis, bit) for bit in bits]


def near(block):
    return [swap(block, "shard", 1), swap(block, "shard", 2)]


def fence(*values):
    return lax.optimization_barrier(values)


def add(a, b):
    return (a.astype(F32) + b.astype(F32)).astype(BF)


class Reduction:
    def __init__(self, sends, keeps, quarters):
        self.quarters = quarters
        self.keep = keeps
        self.stage = 0
        self.sent = sends
        self.flying = [swap(v, "half", 1) for v in sends]

    def inputs(self):
        return list(self.keep) + list(self.flying)

    def compute(self, values, low, low2):
        hlf = OWN // 2
        kept, got = values[: len(self.keep)], values[len(self.keep) :]
        if self.stage == 0:
            return [add(k[:2], g[:2]) for k, g in zip(kept, got)] + [add(k[2:], g[2:]) for k, g in zip(kept, got)]
        if self.stage == 1:
            return [add(k[0], g[0]) for k, g in zip(kept, got)] + [add(k[1], g[1]) for k, g in zip(kept, got)]
        if self.stage == 2:
            if self.quarters:
                u, v = (add(k, g) for k, g in zip(kept, got))
                return [jnp.where(low, u, v), jnp.where(low, v, u)]
            v = jnp.concatenate([add(k, g) for k, g in zip(kept, got)], axis=0)
            return [jnp.where(low, v[:, :hlf], v[:, hlf:]), jnp.where(low, v[:, hlf:], v[:, :hlf])]
        v = kept[0]
        if self.quarters and self.stage == 3:
            v = add(v, got[0])
            return [jnp.where(low2, v[:, :hlf], v[:, hlf:]), jnp.where(low2, v[:, hlf:], v[:, :hlf])]
        if self.quarters and self.stage == 5:
            return [jnp.concatenate([jnp.where(low2, v, got[0]), jnp.where(low2, got[0], v)], axis=1)]
        if self.quarters and self.stage == 6:
            return [jnp.concatenate([jnp.where(low, v, got[0]), jnp.where(low, got[0], v)], axis=0)]
        if self.stage in (3, 4):
            return [add(v, got[0])]
        return [jnp.concatenate([jnp.where(low, v, got[0]), jnp.where(low, got[0], v)], axis=1)]

    def launch(self, outs):
        if self.stage < 2:
            half = len(outs) // 2
            self.keep, self.sent = outs[:half], outs[half:]
            bits = (1, 2) if self.stage == 0 else (2, 1)
            self.flying = [swap(v, "shard", bit) for v, bit in zip(self.sent, bits)]
        else:
            self.keep, self.sent = outs[:1], outs[-1:]
            if self.stage == (6 if self.quarters else 5):
                self.flying = [swap(self.keep[0], "half", 1)]
            else:
                far = (3, 4) if self.quarters else (3,)
                self.flying = [swap(self.sent[0], "replica", 2 if self.stage in far else 1)]
        self.stage += 1


def hop_kernel(chains, counts, place_ref, *refs):
    replica = place_ref[3]
    low, low2 = (replica & 1) == 0, (replica & 2) == 0
    refs = list(refs)
    inputs = [[refs.pop(0)[...] for _ in range(count)] for count in counts]
    for chain, values in zip(chains, inputs):
        for out in chain.compute(values, low, low2):
            refs.pop(0)[...] = out


def together(place, chains, *others, plain=False):
    flying, others = fence([c.flying for c in chains], others)
    for c, v in zip(chains, flying):
        c.flying = v
    inputs = [c.inputs() for c in chains]
    low, low2 = (place[3] & 1) == 0, (place[3] & 2) == 0
    shapes = [jax.eval_shape(c.compute, v, low, low2) for c, v in zip(chains, inputs)]
    if plain:
        outs = [c.compute(v, low, low2) for c, v in zip(chains, inputs)]
    else:
        flat = [x for v in inputs for x in v]
        results = list(single(
            functools.partial(hop_kernel, chains, [len(v) for v in inputs]), (place, *flat),
            [SD(x.shape, x.dtype) for v in shapes for x in v], cost_estimate=cost(1e7, 4 * MB), name="hop",
        ))
        outs = [[results.pop(0) for _ in v] for v in shapes]
    for c, v in zip(chains, outs):
        c.launch(v)
    return others


def shards(images, cotangent, present, threshold, inner_weight, inner_bias, outer_weight, outer_bias, expand_weight,
           expand_bias, reduce_weight, reduce_bias, first_gain, first_shift, second_gain, second_shift, bias_table):
    n = images.shape[0]
    core = lax.axis_index("half")
    shard = lax.axis_index("shard")
    replica = lax.axis_index("replica")
    shard_count = lax.axis_size("shard")
    quick = shard_count == 4 and lax.axis_size("replica") == 4
    me = shard if quick else jnp.int32(0)
    spot = jnp.stack([me, core]).astype(jnp.int32)
    place = jnp.stack([me, core, shard, replica]).astype(jnp.int32)
    own_images = images.reshape(n, ROWS, D)
    own_grad = cotangent.reshape(n, ROWS, D)
    vectors = (inner_bias, outer_bias, expand_bias, reduce_bias, first_gain, first_shift, second_gain, second_shift)
    order = jnp.asarray(row_order(), BF)
    back_order = jnp.asarray(row_order().T, BF)
    alive = present.astype(F32).reshape(1, n)
    table_rows = jnp.pad(bias_table.astype(F32).T, ((0, 0), (0, WIDE - bias_table.shape[0])))
    if quick:
        first, others, others_half, up = first_call(spot, vectors, inner_weight, own_images, own_grad)
        first, up, spot, others_half = fence(first, up, spot, others_half)
        get_first = near(first)
        upper = swap(up, "half", 1)
        masks_0 = bias_call(0, spot, table_rows)
        get_first, upper, masks_0, others_half = fence(get_first, upper, masks_0, others_half)
        get_first.append(swap(get_first[0], "shard", 2))
        get_others = near(others_half)
        tok, g, grad_down = prep_call(own_images, own_grad, upper, alive, order)
        big = cut_call(spot, outer_weight, expand_weight, reduce_weight)
        get_first, get_others, tok, spot, big = fence(get_first, get_others, tok, spot, big)
        first_pieces = [first] + get_first
        get_others.append(swap(get_others[1], "shard", 1))
        in_bias, up_bias, vecs, n1, n1t = vector_call(spot, first_pieces, tok)
        get_others, n1, big = fence(get_others, n1, big)
        others_back = [swap(v, "half", 1) for v in get_others]
        get_big = near(big)
    else:
        masks_0 = bias_call(0, spot, table_rows)
        upper = jnp.concatenate([swap(own_images[:, :TOK], "half", 1), swap(own_grad[:, :TOK], "half", 1)])
        whole_vectors = [lax.all_gather(v, "shard", axis=0, tiled=True).reshape(4, -1) for v in vectors]
        parts = jnp.stack([jnp.pad(v, ((0, 0), (0, D - v.shape[1]))) for v in whole_vectors], axis=1)
        parts = [jnp.pad(parts[r], ((0, 8), (0, 0))) for r in range(4)]
        thirds = inner_weight.reshape(-1, 3, 3, LP).transpose(0, 2, 1, 3).reshape(-1, 3, 3 * LP)
        first = thirds[:, 0]
        others = thirds[:, 1:].reshape(-1, 6 * LP)

        tok, g, grad_down = prep_call(own_images, own_grad, upper, alive, order)
        in_bias, up_bias, vecs, n1, n1t = vector_call(spot, parts, tok)

    if quick:
        def places(rows):
            at = [me * rows]
            for c in (core, 1 - core):
                at += [(me ^ 1) * rows + c * (rows // 2), (me ^ 2) * rows + c * (rows // 2), (me ^ 3) * rows + c * (rows // 2)]
            return at

        first_at = jnp.stack([(me ^ r) * OWN for r in range(4)]).astype(jnp.int32)
        in_at = jnp.stack(places(OWN)).astype(jnp.int32)

        def in_plan(columns):
            return [(k, 0, OWN if k == 0 else OWN // 2, columns, 3 * LP, 0, 0) for k in range(7)]

        in_plans = [[(k, 0, OWN, 0, 3 * LP, 0, 0) for k in range(4)], in_plan(0), in_plan(3 * LP)]
    else:
        first_at = in_at = jnp.zeros((1,), jnp.int32)
        first_pieces = [lax.all_gather(first, "shard", axis=0, tiled=True)]
        others_pieces = [lax.all_gather(others, "shard", axis=0, tiled=True)]
        in_plans = [[(0, 0, D, k, 3 * LP, 0, 0)] for k in (0, 0, 3 * LP)]

    results = [attend_call(0, n1, in_bias, masks_0, first_at, in_plans[0], first_pieces, [])]
    if quick:
        others_back, results, spot = fence(others_back, results, spot)
    masks_1 = bias_call(1, spot, table_rows)
    if quick:
        masks_1, spot = fence(masks_1, spot)
        others_pieces = [others] + get_others + others_back
    results.append(attend_call(1, n1, in_bias, masks_1, in_at, in_plans[1], others_pieces, []))
    if quick:
        get_big, results, spot = fence(get_big, results, spot)
        far = [swap(get_big[0][: BIG // 2], "shard", 2), swap(get_big[1][BIG // 2 :], "shard", 1)]
        big_back = [swap(v, "half", 1) for v in get_big]
    masks_2 = bias_call(2, spot, table_rows)
    results.append(attend_call(2, n1, in_bias, masks_2, in_at, in_plans[2], others_pieces, []))
    if quick:
        far, big_back, results = fence(far, big_back, results)
        far_back = [swap(v, "half", 1) for v in far]
        far_back, results = fence(far_back, results)
        pieces = [outer_weight, expand_weight, reduce_weight] + get_big + far + big_back + far_back
        hlf = OWN // 2
        plan = [(0, 0, OWN, 0, D, 0, 0)]
        short = places(OWN)
        long = [None] + [c * 4 * CH + (me ^ r) * CH for c in (core, 1 - core) for r in (1, 2, 3)]
        at = [short[0]]
        for k in range(8):
            plan.append((1, 0, OWN, hidden_block(k) * CH, CH, 1, k * CH))
            at.append(short[0])
        for c in range(2):
            plan.append((2, c * CH, CH, 0, D, 2, 0))
            at.append(c * 4 * CH + me * CH)
        parts = [(b * hlf, hlf, 1, b * D) for b in range(4)] + [(4 * hlf, hlf, 0, 0), (5 * hlf, 4 * hlf, 2, 0)]

        def add_piece(source, lo, hi, place):
            for row, rows, target, column in parts:
                a, b = max(row, lo), min(row + rows, hi)
                if a < b and target == 1:
                    for c in range(2):
                        plan.append((source, a - lo, b - a, c * CH, CH, 1, c * 4 * CH + column // 2))
                        at.append(short[place] + (a - row))
                elif a < b:
                    plan.append((source, a - lo, b - a, 0, D, target, column))
                    at.append((long if target == 2 else short)[place] + (a - row))

        for side in range(2):
            for k in range(2):
                add_piece(3 + 4 * side + k, 0, BIG, 1 + 3 * side + k)
            add_piece(5 + 4 * side, 0, BIG // 2, 3 + 3 * side)
            add_piece(6 + 4 * side, BIG // 2, BIG, 3 + 3 * side)
        at = jnp.stack(at).astype(jnp.int32)
    else:
        pieces = [lax.all_gather(v, "shard", axis=0, tiled=True) for v in (outer_weight, expand_weight, reduce_weight)]
        plan, at = [(0, 0, D, 0, D, 0, 0)], [0]
        for k in range(8):
            plan += [(1, 0, D, hidden_block(k) * CH, CH, 1, k * CH), (2, hidden_block(k) * CH, CH, 0, D, 2, 0)]
            at += [0, k * CH]
        at = jnp.asarray(at, jnp.int32)
    projs, pts, atts, peak, ws = zip(*results)
    (stay, send, gmid, datt, out_send, out_keep, e_send, e_keep, r_send, r_keep, grad_up, small) = middle_call(
        spot, tok, atts, g, back_order, vecs, up_bias, at, plan, pieces, []
    )
    def wait_for(chains):
        return [v for c in chains for v in c.sent]

    after = []
    if quick:
        feed = Reduction([e_send, r_send], [e_keep, r_keep], True)
    lower_out = swap(send, "half", 1)
    gp0, db0 = back_call(0, projs[0], pts[0], datt, [])
    if quick:
        gp0, lower_out, projs = together(place, [feed], gp0, lower_out, projs)
        after = wait_for([feed])
    gp1, db1 = back_call(1, projs[1], pts[1], datt, after)
    gp2, db2 = back_call(2, projs[2], pts[2], datt, [gp1])
    x_send, x_keep, y_send, y_keep, sums_in = inner_call(spot, n1t, (gp0, gp1, gp2), (out_send, out_keep), [])
    peak = jnp.concatenate(peak, axis=2)
    peaks = jnp.max(jnp.where((present > 0)[:, None, None, None], peak, NEGATIVE), axis=(0, 1, 3)).reshape(1, HEADS)
    after = [x_send]
    if quick:
        x_send, y_send, gp2 = together(place, [feed], x_send, y_send, gp2)
        rest = Reduction([x_send, y_send], [x_keep, y_keep], False)
        after = wait_for([feed])
    half = n // 2
    one_a, gstay_a, gsend_a = last_call(0, half, tok, gmid, vecs, back_order, (gp0, gp1, gp2), ws, after)
    after = [gsend_a]
    if quick:
        gsend_a, one_a = together(place, [rest, feed], gsend_a, one_a)
        after = wait_for([rest, feed])
    lower_a = swap(gsend_a, "half", 1)
    one_b, gstay_b, gsend_b = last_call(half, n - half, tok, gmid, vecs, back_order, (gp0, gp1, gp2), ws, after)
    after = [gsend_b]
    if quick:
        gsend_b, lower_a = together(place, [rest, feed], gsend_b, lower_a)
        after = wait_for([rest, feed])
    lower_b = swap(gsend_b, "half", 1)
    sums = table_call((db0, db1, db2), grad_up, grad_down, small, sums_in, peaks, after)
    every = Everywhere(sums, (one_a, one_b), quick)
    if quick:
        rest.flying, feed.flying, lower_b = fence(rest.flying, feed.flying, lower_b)
        together(place, [rest, every, feed])
        block_out = jnp.concatenate([lower_out, stay], axis=1)
        (block_out,) = together(place, [rest, every, feed], block_out)
        grad_images = jnp.concatenate([jnp.concatenate([lower_a, lower_b]), jnp.concatenate([gstay_a, gstay_b])], axis=1)
        (grad_images,) = together(place, [rest, every], grad_images)
        rest.flying, every.flying, feed.flying = fence(rest.flying, every.flying, feed.flying)
        together(place, [rest, every, feed])
    else:
        while every.hops:
            together(place, [every])
        block_out = jnp.concatenate([lower_out, stay], axis=1)
        grad_images = jnp.concatenate([jnp.concatenate([lower_a, lower_b]), jnp.concatenate([gstay_a, gstay_b])], axis=1)

    vectors = (every.value[0], every.flying[0])
    if quick:
        *vectors, grad_expand, grad_reduce, grad_inner, grad_outer = finish(
            place, vectors, threshold, inner_weight, feed.keep + feed.flying, rest.keep + rest.flying
        )
    else:
        def halves(keep, send, axis):
            lo = jnp.where(core == 0, keep, send)
            hi = jnp.where(core == 0, send, keep)
            return jnp.concatenate([lo, hi], axis=axis)

        def whole(keep, send):
            both = halves(keep[:, :, :, None], send[:, :, :, None], 3)
            return both.transpose(0, 2, 1, 3, 4).reshape(D, -1)

        def settle(v):
            v = lax.psum_scatter(v.astype(BF), "shard", scatter_dimension=0, tiled=True)
            return lax.psum(v, ("replica", "half")).astype(F32)

        def rows_of(v):
            return v.reshape(4, 1, 2, 2, OWN, CH).transpose(0, 1, 2, 4, 3, 5).reshape(4, 1, CH, D)

        def straight(v):
            return jnp.stack([v[0], v[2], v[1], v[3]])

        grad_reduce = settle(halves(rows_of(r_keep), rows_of(r_send), 1).reshape(FF, D))
        grad_expand = settle(whole(straight(e_keep), straight(e_send)))
        grad_outer = settle(whole(out_keep, out_send))
        x_keep, x_send = straight(x_keep), straight(x_send)
        by_third = [
            whole(x_keep[:, :1], x_send[:, :1]), whole(y_keep[:, :1], y_send[:, :1]), whole(x_keep[:, 1:], x_send[:, 1:])
        ]
        by_third = jnp.stack(by_third, axis=1).reshape(D, 3, 3, LP).transpose(0, 2, 1, 3).reshape(D, 3 * D)
        grad_inner = settle(by_third)

        vectors = vector_finish(place, *vectors, threshold, inner_weight, shard_count)
    (grad_inbias, grad_outbias, grad_upbias, grad_downbias, grad_gain_1, grad_shift_1, grad_gain_2, grad_shift_2, grad_table,
     clipped, factors, maxima) = vectors
    block_out = block_out.reshape(images.shape)
    grad_images = grad_images.reshape(images.shape)
    return (
        block_out,
        grad_images,
        grad_inner,
        grad_inbias,
        grad_outer,
        grad_outbias,
        grad_expand,
        grad_upbias,
        grad_reduce,
        grad_downbias,
        grad_gain_1,
        grad_shift_1,
        grad_gain_2,
        grad_shift_2,
        grad_table.T,
        clipped,
        factors,
        maxima,
    )


def solution(mesh):
    rows = P(("replica", "shard"), "half", None, None)
    cut = P("shard", None)
    line = P("shard")
    return jax.shard_map(
        shards,
        mesh=mesh,
        in_specs=(rows, rows, P(("replica", "shard")), P(), cut, line, cut, line, cut, line, cut, line, line, line, line,
                  line, P()),
        out_specs=(rows, rows, cut, line, cut, line, cut, line, cut, line, line, line, line, line, P(), cut, P(), P()),
        check_vma=False,
    )
```

```python
import functools
import math

import numpy as np
import jax
import jax.numpy as jnp
from jax import lax
from jax.experimental import pallas as pl
from jax.experimental.pallas import tpu as pltpu
from jax.sharding import PartitionSpec as P

D = 768
HEADS = 24
HD = 32
WIN = 12
GRID = 24
SHIFT = 6
FF = 3072
TOK = WIN * WIN
ROWS = WIN * GRID
SPAN = 2 * WIN - 1
EPS = 1e-5
MASKED = -100.0
NEGATIVE = -1e30
LOG2E = math.log2(math.e)
BF = jnp.bfloat16
F32 = jnp.float32
MB = 1 << 20
OWN = 192
CH = 384
WIDE = 640
NARROW = 384
TALL = WIN * 16
HB = 8
LB = HB * HD
HP = 8
LP = HP * HD
NB = 576
SCALE = 1e-3
ONE = dict(pipeline_mode=pl.Buffered(1))
SD = jax.ShapeDtypeStruct


def nn(a, b):
    return lax.dot_general(a, b, (((1,), (0,)), ((), ())), preferred_element_type=F32)


def nt(a, b):
    return lax.dot_general(a, b, (((1,), (1,)), ((), ())), preferred_element_type=F32)


def tn(a, b):
    return lax.dot_general(a, b, (((0,), (0,)), ((), ())), preferred_element_type=F32)


def full(shape, **kw):
    return pl.BlockSpec(shape, lambda *_: (0,) * len(shape), **kw)


def any_space():
    return pl.BlockSpec(memory_space=pl.ANY)


def smem():
    return pl.BlockSpec(memory_space=pltpu.SMEM)


def run(kernel, count, args, after, in_specs, **kw):
    def body(*refs):
        kernel(*refs[:count], *refs[count + len(after) :])

    return pl.pallas_call(body, in_specs=list(in_specs) + [any_space()] * len(after), **kw)(*args, *after)


def params(limit=63):
    return pltpu.CompilerParams(vmem_limit_bytes=limit * MB)


def cost(flops, moved, exps=0):
    return pl.CostEstimate(flops=int(flops * SCALE), bytes_accessed=int(moved * SCALE), transcendentals=0)


def whole(array):
    return full(array.shape, **ONE)


def single(kernel, args, out_shape, after=(), scratch=(), **kw):
    specs = [smem() if v.dtype == jnp.int32 else whole(v) for v in args]
    shapes = out_shape if isinstance(out_shape, (list, tuple)) else [out_shape]
    out = run(
        kernel, len(args), args, after, grid=(1,), in_specs=specs, out_specs=[whole(v) for v in shapes], out_shape=list(shapes),
        scratch_shapes=list(scratch), compiler_params=params(), **kw
    )
    return out if isinstance(out_shape, (list, tuple)) else out[0]


def colsum(v):
    return jnp.sum(v, axis=0, keepdims=True)


def norm_parts(x):
    c = x - jnp.mean(x, axis=-1, keepdims=True)
    r = lax.rsqrt(jnp.mean(c * c, axis=-1, keepdims=True) + EPS)
    return c * r, r


def row_order():
    cells = np.arange(ROWS)
    win, rest = cells // TOK, cells % TOK
    a, b = rest // WIN, rest % WIN
    m = np.zeros((ROWS, ROWS), np.float32)
    m[cells, a * GRID + (win * WIN + b + SHIFT) % GRID] = 1
    return m


def spread_q():
    q = np.arange(TOK)
    m = np.zeros((TOK, NARROW), np.float32)
    m[q, SPAN * (q // WIN) + q % WIN] = 1
    return m


def spread_k(reverse):
    k = np.arange(TOK)
    b = k % WIN
    m = np.zeros((TALL, TOK), np.float32)
    m[16 * (k // WIN) + (WIN - 1 - b if reverse else b), k] = 1
    return m


def copies(plan, refs, at, targets, sems):
    base, entries = plan
    for i, (src, row, rows, col, cols, dst, put) in enumerate(entries):
        place = pl.ds(pl.multiple_of(at[base + i], 16), rows)
        yield pltpu.make_async_copy(
            refs[src].at[pl.ds(row, rows), pl.ds(col, cols)], targets[dst].at[place, pl.ds(put, cols)], sems.at[i]
        )


def hidden_block(k):
    return 2 * (k % 4) + k // 4


def region_masks():
    line = np.arange(GRID)
    region = (line >= GRID - WIN).astype(np.int32) + (line >= GRID - SHIFT).astype(np.int32)
    lab = 3 * region[:, None] + region[None, :]
    lab = lab.reshape(2, WIN, 2, WIN).transpose(0, 2, 1, 3).reshape(2, 2, TOK)
    return np.where(lab[:, :, :, None] != lab[:, :, None, :], MASKED, 0.0).astype(np.float32)


def bias_kernel(table_ref, sq_ref, sk_ref, out_ref, tall):
    for h in range(HP):
        row = pltpu.roll(jnp.broadcast_to(table_ref[h : h + 1, :], (16, WIDE)), 0, 1, stride=1, stride_axis=0)
        for a in range(WIN):
            off = (SPAN * a - SPAN * (WIN - 1) - (WIN - 1)) % WIDE
            tall[16 * a : 16 * a + 16, :] = pltpu.roll(row, off, 1)[:, :NARROW].astype(BF)
        wide = nn(tall[...], sq_ref[...]).astype(BF)
        out_ref[h] = nn(sk_ref[...], wide).astype(BF)


def bias_call(group, table):
    args = (table, jnp.asarray(spread_q().T, BF), jnp.asarray(spread_k(False).T, BF))
    out = SD((HP, TOK, TOK), BF)
    return pl.pallas_call(
        bias_kernel,
        grid=(1,),
        in_specs=[pl.BlockSpec((HP, WIDE), lambda i: (group, 0))] + [whole(v) for v in args[1:]],
        out_specs=whole(out),
        out_shape=out,
        scratch_shapes=[pltpu.VMEM((TALL, NARROW), BF)],
        compiler_params=params(),
        cost_estimate=cost(2e9, 2 * MB),
        name="bias",
    )(*args)


V_UP, V_SMALL, V_IN, V_ONE, V_PEAK, V_TABLE, V_ROWS = 0, 4, 8, 11, 13, 16, 40


def table_kernel(db0_ref, db1_ref, db2_ref, up_ref, down_ref, small_ref, in_ref, peak_ref, sq_ref, sk_ref, out_ref):
    def split(v):
        hi = v.astype(BF)
        return hi, (v - hi.astype(F32)).astype(BF)

    out_ref[...] = jnp.zeros_like(out_ref)
    for k in range(8):
        b = hidden_block(k)
        out_ref[V_UP + b // 2 : V_UP + b // 2 + 1, (b % 2) * CH : (b % 2 + 1) * CH] = up_ref[
            k // 2, :, (k % 2) * CH : (k % 2 + 1) * CH
        ]
    out_ref[V_SMALL : V_SMALL + 1, :] = down_ref[...]
    out_ref[V_SMALL + 1 : V_SMALL + 4, :] = small_ref[1:4, :]
    for p in range(3):
        row = in_ref[p]
        for k in range(3):
            out_ref[V_IN + k : V_IN + k + 1, p * LP : (p + 1) * LP] = row[:, k * LP : (k + 1) * LP]
    out_ref[V_PEAK : V_PEAK + 1, :HEADS] = peak_ref[...]
    for h in range(HEADS):
        hi, lo = split((db0_ref, db1_ref, db2_ref)[h // HP][h % HP])
        tall = nn(sk_ref[...], hi) + nn(sk_ref[...], lo)
        hi, lo = split(tall)
        wide = nn(hi, sq_ref[...]) + nn(lo, sq_ref[...])
        wide = jnp.concatenate([wide, jnp.zeros((TALL, WIDE - NARROW), F32)], axis=1)
        tot = jnp.zeros((16, WIDE), F32)
        for a in range(WIN):
            tot = tot + pltpu.roll(wide[16 * a : 16 * a + 16, :], SPAN * (WIN - 1 - a), 1)
        tot = pltpu.roll(tot, 0, 1, stride=1, stride_axis=0)
        out_ref[V_TABLE + h : V_TABLE + h + 1, :WIDE] = colsum(tot)


def table_call(dbs, up, down, small, sums_in, peaks, after):
    args = (*dbs, up, down, small, sums_in, peaks, jnp.asarray(spread_q(), BF), jnp.asarray(spread_k(True), BF))
    return single(table_kernel, args, SD((V_ROWS, D), F32), after, cost_estimate=cost(6e9, 4 * MB), name="table")


def lane_head(shape):
    return lax.broadcasted_iota(jnp.int32, shape, len(shape) - 1) // HD


VECTORS = (2 * D, D, FF, D, D, D, D, D)


def first_kernel(spot_ref, *refs):
    vecs, (inner_ref, own_ref, gown_ref, first_ref, others_ref, half_ref, up_ref) = refs[:8], refs[8:]
    n = own_ref.shape[0]
    up_ref[:n] = own_ref[...]
    up_ref[n:] = gown_ref[...]
    mine = pl.ds(pl.multiple_of(spot_ref[1] * (OWN // 2), 16), OWN // 2)
    for k in range(3):
        first_ref[:OWN, k * LP : (k + 1) * LP] = inner_ref[:, k * D : k * D + LP]
        for p in (1, 2):
            src = slice(k * D + p * LP, k * D + (p + 1) * LP)
            dst = slice(((p - 1) * 3 + k) * LP, ((p - 1) * 3 + k + 1) * LP)
            others_ref[:, dst] = inner_ref[:, src]
            half_ref[:, dst] = inner_ref[mine, src]
    rows = [jnp.zeros((8, D), F32)]
    for v in vecs:
        row = v[...].astype(F32).reshape(1, v.shape[0])
        if v.shape[0] < D:
            row = jnp.concatenate([row, jnp.zeros((1, D - v.shape[0]), F32)], axis=1)
        rows.insert(-1, row)
    first_ref[OWN:, :] = jnp.concatenate(rows, axis=0).astype(BF)


def first_call(spot, vectors, inner, own, gown):
    n = own.shape[0]
    top = full((n, TOK, D))
    shapes = [SD((OWN + 16, D), BF), SD((OWN, 6 * LP), BF), SD((OWN // 2, 6 * LP), BF), SD((2 * n, TOK, D), BF)]
    return pl.pallas_call(
        first_kernel,
        grid=(1,),
        in_specs=[smem()] + [whole(v) for v in vectors] + [whole(inner), top, top],
        out_specs=[whole(v) for v in shapes],
        out_shape=shapes,
        compiler_params=params(),
        cost_estimate=cost(1e6, 6 * MB),
        name="first",
    )(spot, *vectors, inner, own, gown)


BIG = 4 * (OWN // 2) + OWN // 2 + 2 * OWN


def cut_kernel(spot_ref, outer_ref, expand_ref, reduce_ref, big_ref):
    core = spot_ref[1]
    hlf = OWN // 2
    mine = pl.ds(pl.multiple_of(core * hlf, 16), hlf)
    for k in range(4):
        big_ref[k * hlf : (k + 1) * hlf, :] = expand_ref[mine, k * D : (k + 1) * D]
    big_ref[4 * hlf : 5 * hlf, :] = outer_ref[mine, :]
    big_ref[5 * hlf :, :] = reduce_ref[pl.ds(pl.multiple_of(core * 2 * OWN, 16), 2 * OWN), :]


def cut_call(spot, outer, expand, reduce):
    return single(
        cut_kernel, (spot, outer, expand, reduce), [SD((BIG, D), BF)], cost_estimate=cost(1e6, 3 * MB), name="cut"
    )[0]


def prep_kernel(own_ref, gown_ref, recv_ref, alive_ref, pm_ref, tok_ref, g_ref, sum_ref):
    n = own_ref.shape[0]
    tot = jnp.zeros((1, D), F32)
    for i in range(n):
        tok_ref[i] = nn(pm_ref[...], jnp.concatenate([own_ref[i, TOK:, :], recv_ref[i]], axis=0)).astype(BF)
        g = nn(pm_ref[...], jnp.concatenate([gown_ref[i, TOK:, :], recv_ref[n + i]], axis=0)) * alive_ref[0:1, i : i + 1]
        g_ref[i] = g.astype(BF)
        tot = tot + colsum(g)
    sum_ref[...] = tot


def prep_call(own, gown, recv, alive, pm):
    rows = SD(own.shape, BF)
    return single(
        prep_kernel, (own, gown, recv, alive, pm), [rows, rows, SD((1, D), F32)], cost_estimate=cost(3e9, 16 * MB), name="prep"
    )


def vector_kernel(spot_ref, pa_ref, pb_ref, pc_ref, pd_ref, tok_ref, inb_ref, up_ref, vec_ref, n1_ref, n1t_ref, parts):
    n = tok_ref.shape[0]
    for r, ref in enumerate((pa_ref, pb_ref, pc_ref, pd_ref)):
        parts[jnp.bitwise_xor(spot_ref[0], r)] = ref[:8, :].astype(F32)

    def vector(i):
        size = VECTORS[i] // 4
        return jnp.concatenate([parts[s][i : i + 1, :size] for s in range(4)], axis=1)

    vin = vector(0)
    for p in range(3):
        inb_ref[p] = jnp.concatenate(
            [vin[:, p * LP : (p + 1) * LP], jnp.zeros((1, LP), F32), vin[:, D + p * LP : D + (p + 1) * LP]], axis=1
        )
    vup = vector(2)
    for k in range(8):
        up_ref[k // 2, :, (k % 2) * CH : (k % 2 + 1) * CH] = vup[:, hidden_block(k) * CH : (hidden_block(k) + 1) * CH]
    gain, shift = vector(4), vector(5)
    vec_ref[...] = jnp.zeros_like(vec_ref)
    for r, v in enumerate((vector(1), vector(3), gain, vector(6), vector(7))):
        vec_ref[r : r + 1, :] = v
    for i in range(n):
        xh, _ = norm_parts(tok_ref[i].astype(F32))
        n1 = (xh * gain + shift).astype(BF)
        n1_ref[i] = n1
        n1t_ref[:, i * ROWS : (i + 1) * ROWS] = n1.T


def vector_call(spot, parts, tok):
    n = tok.shape[0]
    last = parts[0].shape[0] // 16 - 1
    shapes = [SD((3, 1, 3 * LP), F32), SD((4, 1, 2 * CH), F32), SD((8, D), F32), SD(tok.shape, BF), SD((D, n * ROWS), BF)]
    return pl.pallas_call(
        vector_kernel,
        grid=(1,),
        in_specs=[smem()] + [pl.BlockSpec((16, D), lambda i: (last, 0))] * 4 + [whole(tok)],
        out_specs=[whole(v) for v in shapes],
        out_shape=shapes,
        scratch_shapes=[pltpu.VMEM((4, 8, D), F32)],
        compiler_params=params(),
        cost_estimate=cost(5e9, 8 * MB),
        name="vectors",
    )(spot, *parts, tok)


def attend_kernel(plan, count, spot_ref, n1_ref, b_ref, bias_ref, mask_ref, at_ref, *rest):
    pieces = rest[:count]
    proj_ref, pt_ref, att_ref, peak_ref, w_ref, sems = rest[count:]

    @pl.when(pl.program_id(0) == 0)
    def _():
        for c in copies(plan, pieces, at_ref, (w_ref,), sems):
            c.start()
        for c in copies(plan, pieces, at_ref, (w_ref,), sems):
            c.wait()

    proj_ref[0] = (nn(n1_ref[0], w_ref[...]) + b_ref[0]).astype(BF)
    hid = lane_head((TOK, LB))
    scale = HD**-0.5
    for w in range(2):
        r = slice(w * TOK, (w + 1) * TOK)
        mask = mask_ref[spot_ref[1], w].astype(F32)
        for blk in range(LP // LB):
            l = blk * LB
            q = proj_ref[0, r, l : l + LB]
            k = proj_ref[0, r, LP + l : LP + l + LB]
            v = proj_ref[0, r, 2 * LP + l : 2 * LP + l + LB]
            vt = v.T
            apart = jnp.concatenate([jnp.where(hid == h, k, jnp.zeros_like(k)) for h in range(HB)], axis=0)
            sts = nn(apart, q.T)
            outs = []
            for h in range(HB):
                hh = blk * HB + h
                st = sts[h * TOK : (h + 1) * TOK]
                peak_ref[0, w, hh : hh + 1, :] = jnp.max(st, axis=0, keepdims=True) * scale
                t = st * scale + (bias_ref[hh].astype(F32) + mask)
                e = jnp.exp(t - jnp.max(t, axis=0, keepdims=True))
                p = (e * (1.0 / colsum(e))).astype(BF)
                pt_ref[0, w, hh] = p
                outs.append(nn(vt[HD * h : HD * h + HD, :], p))
            att_ref[0, r, l : l + LB] = jnp.concatenate(outs, axis=0).astype(BF).T


def attend_call(group, spot, n1, b, bias, at, plan, pieces, after):
    n = n1.shape[0]

    def blk(*s):
        return pl.BlockSpec((1,) + s, lambda i: (i,) + (0,) * len(s))

    return run(
        functools.partial(attend_kernel, plan, len(pieces)), 6 + len(pieces),
        (spot, n1, b, bias, jnp.asarray(region_masks(), BF), at, *pieces), after,
        grid=(n,),
        in_specs=[smem(), blk(ROWS, D), pl.BlockSpec((1, 1, 3 * LP), lambda i: (group, 0, 0)), full((HP, TOK, TOK), **ONE),
                  full((2, 2, TOK, TOK), **ONE), smem()]
        + [any_space()] * len(pieces),
        out_specs=[blk(ROWS, 3 * LP), blk(2, HP, TOK, TOK), blk(ROWS, LP), blk(2, HP, TOK), full((D, 3 * LP), **ONE)],
        out_shape=[SD((n, ROWS, 3 * LP), BF), SD((n, 2, HP, TOK, TOK), BF), SD((n, ROWS, LP), BF), SD((n, 2, HP, TOK), F32),
                   SD((D, 3 * LP), BF)],
        scratch_shapes=[pltpu.SemaphoreType.DMA((len(plan[1]),))],
        compiler_params=params(),
        cost_estimate=cost(1.3e10, 12 * MB, 1.4e6),
        name="attend",
    )


def gelu_parts(h):
    d = 1.0 + (0.3275911 * 0.5**0.5) * jnp.abs(h)
    t = pl.reciprocal(d, approx=True)
    t = t * (2.0 - d * t)
    e = jnp.exp2(h * h * (-0.5 * LOG2E))
    p = (((0.5 * 1.061405429) * t - 0.5 * 1.453152027) * t + 0.5 * 1.421413741) * t - 0.5 * 0.284496736
    p = (p * t + 0.5 * 0.254829592) * t * e
    cdf = jnp.where(h >= 0, 1.0 - p, p)
    return cdf, cdf + h * (e * ((2 * math.pi) ** -0.5))


def middle_kernel(plan, count, spot_ref, tok_ref, att0_ref, att1_ref, att2_ref, gin_ref, pmt_ref, vec_ref, eb_ref,
                  at_ref, *rest):
    pieces = rest[:count]
    (stay_ref, send_ref, gmid_ref, datt_ref, os_ref, ok_ref, es_ref, ek_ref, rs_ref, rk_ref, geb_ref, small_ref,
     wo, we, wr, mid, n2, g, n2t, acc, e2, act, gh, sems) = rest[count:]
    j = pl.program_id(0)
    n = tok_ref.shape[0]
    N = n * ROWS
    me = spot_ref[0]
    core = spot_ref[1]
    early = [k for k, entry in enumerate(plan[1]) if entry[5] == 0]
    out_b, red_b, gain, shift = vec_ref[0:1, :], vec_ref[1:2, :], vec_ref[3:4, :], vec_ref[4:5, :]

    def attended(i):
        return jnp.concatenate([att0_ref[i], att1_ref[i], att2_ref[i]], axis=-1)

    @pl.when(j == 0)
    def _():
        moves = list(copies(plan, pieces, at_ref, (wo, we, wr), sems))
        for c in moves:
            c.start()
        for k in early:
            moves[k].wait()
        for i in range(n):
            s = slice(i * ROWS, (i + 1) * ROWS)
            g[s, :] = gin_ref[i]
            m = tok_ref[i].astype(F32) + nn(attended(i), wo[...]) + out_b
            mid[s, :] = m
            xh, _ = norm_parts(m)
            x2 = (xh * gain + shift).astype(BF)
            n2[s, :] = x2
            n2t[:, s] = x2.T
            acc[s, :] = m + red_b
            e2[s, :] = jnp.zeros((ROWS, D), F32)
        for k, c in enumerate(moves):
            if k not in early:
                c.wait()

    at = pl.multiple_of((2 * jnp.bitwise_xor(core, 1 - j // 2) + j % 2) * 2 * CH, 2 * CH)
    cols = pl.ds(at, 2 * CH)
    tot = jnp.zeros((1, 2 * CH), F32)
    for s0 in range(0, N, NB):
        s = slice(s0, s0 + NB)
        h = nn(n2[s, :], we[:, cols]) + eb_ref[0]
        cdf, dg = gelu_parts(h)
        act[s, :] = (h * cdf).astype(BF)
        x = (nt(g[s, :], wr[cols, :]) * dg).astype(BF)
        gh[s, :] = x
        tot = tot + colsum(x.astype(F32))
    geb_ref[0] = tot
    ge = nn(n2t[...], gh[...]).astype(BF)
    gr = tn(act[...], g[...]).astype(BF)

    def put(e_ref, r_ref):
        for t in range(2):
            for b in range(4):
                e_ref[crossed(jnp.bitwise_xor(me, b)), t] = ge[b * OWN : (b + 1) * OWN, t * CH : (t + 1) * CH]
                r_ref[jnp.bitwise_xor(me % 2, t), b] = gr[
                    t * CH + (b // 2) * OWN : t * CH + (b // 2 + 1) * OWN, (b % 2) * CH : (b % 2 + 1) * CH
                ]

    @pl.when(j < 2)
    def _():
        put(es_ref, rs_ref)

    @pl.when(j >= 2)
    def _():
        put(ek_ref, rk_ref)

    for s0 in range(0, N, NB):
        s = slice(s0, s0 + NB)
        acc[s, :] += nn(act[s, :], wr[cols, :])
        e2[s, :] += nt(gh[s, :], we[:, cols])

    @pl.when(j == 3)
    def _():
        gn = jnp.zeros((1, D), F32)
        shf = gn
        ob = gn
        for i in range(n):
            s = slice(i * ROWS, (i + 1) * ROWS)
            o = nn(pmt_ref[...], acc[s, :].astype(BF)).astype(BF)
            stay_ref[i] = o[:TOK]
            send_ref[i] = o[TOK:]
            xh, r = norm_parts(mid[s, :])
            d = e2[s, :]
            gn = gn + colsum(d * xh)
            shf = shf + colsum(d)
            d = d * gain
            gm = g[s, :].astype(F32) + r * (
                d - jnp.mean(d, axis=-1, keepdims=True) - xh * jnp.mean(d * xh, axis=-1, keepdims=True)
            )
            gb = gm.astype(BF)
            gmid_ref[i] = gb
            ob = ob + colsum(gb.astype(F32))
            g[s, :] = gb
            datt_ref[i] = nt(gb, wo[...]).astype(BF)
            n2[s, :] = attended(i)
        for c, ref in ((1 - core, os_ref), (core, ok_ref)):
            go = tn(n2[...], g[:, pl.ds(pl.multiple_of(c * CH, 128), CH)]).astype(BF)
            for b in range(4):
                ref[jnp.bitwise_xor(me, b), 0] = go[b * OWN : (b + 1) * OWN, :]
        small_ref[1:2, :] = gn
        small_ref[2:3, :] = shf
        small_ref[3:4, :] = ob


def crossed(r):
    return 2 * (r % 2) + r // 2


def middle_call(spot, tok, atts, g, pmt, vecs, eb, at, plan, pieces, after):
    n = tok.shape[0]
    N = n * ROWS
    blocks = SD((4, 4, OWN, CH), BF)

    def chunk(j, spot):
        return 2 * jnp.bitwise_xor(spot[1], 1 - j // 2) + j % 2

    def early(j):
        return jnp.minimum(j, 1)

    def late(j):
        return jnp.maximum(j, 2) - 2

    rows = full((n, ROWS, D), **ONE)
    third = full((n, ROWS, LP), **ONE)
    cut = full((n, TOK, D), **ONE)
    outer = full((4, 1, OWN, CH), **ONE)
    args = (spot, tok, *atts, g, pmt, vecs, eb, at, *pieces)

    def body(*refs):
        middle_kernel(plan, len(pieces), *refs[: len(args)], *refs[len(args) + len(after) :])

    grid_spec = pltpu.PrefetchScalarGridSpec(
        num_scalar_prefetch=1,
        grid=(4,),
        in_specs=[rows, third, third, third, rows, full((ROWS, ROWS)), full((8, D)),
                  pl.BlockSpec((1, 1, 2 * CH), lambda j, spot: (chunk(j, spot), 0, 0)), smem()]
        + [any_space()] * (len(pieces) + len(after)),
        out_specs=[cut, cut, rows, rows, outer, outer,
                   pl.BlockSpec((4, 2, OWN, CH), lambda j, spot: (0, early(j), 0, 0)),
                   pl.BlockSpec((4, 2, OWN, CH), lambda j, spot: (0, late(j), 0, 0)),
                   pl.BlockSpec((2, 4, OWN, CH), lambda j, spot: (jnp.bitwise_xor(early(j), spot[0] // 2), 0, 0, 0)),
                   pl.BlockSpec((2, 4, OWN, CH), lambda j, spot: (jnp.bitwise_xor(late(j), spot[0] // 2), 0, 0, 0)),
                   pl.BlockSpec((1, 1, 2 * CH), lambda j, spot: (chunk(j, spot), 0, 0)), full((8, D))],
        scratch_shapes=[pltpu.VMEM((D, D), BF), pltpu.VMEM((D, FF), BF), pltpu.VMEM((FF, D), BF),
                        pltpu.VMEM((N, D), F32), pltpu.VMEM((N, D), BF), pltpu.VMEM((N, D), BF), pltpu.VMEM((D, N), BF),
                        pltpu.VMEM((N, D), F32), pltpu.VMEM((N, D), F32), pltpu.VMEM((N, 2 * CH), BF), pltpu.VMEM((N, 2 * CH), BF),
                        pltpu.SemaphoreType.DMA((len(plan[1]),))],
    )
    return pl.pallas_call(
        body,
        grid_spec=grid_spec,
        out_shape=[SD((n, TOK, D), BF), SD((n, TOK, D), BF), SD((n, ROWS, D), BF), SD((n, ROWS, D), BF),
                   SD((4, 1, OWN, CH), BF), SD((4, 1, OWN, CH), BF), blocks, blocks, blocks, blocks,
                   SD((4, 1, 2 * CH), F32), SD((8, D), F32)],
        compiler_params=params(62),
        cost_estimate=cost(6e10, 40 * MB, 7e6),
        name="middle",
    )(*args, *after)


def back_kernel(proj_ref, pt_ref, da_ref, gp_ref, db_ref):
    @pl.when(pl.program_id(0) == 0)
    def _():
        db_ref[...] = jnp.zeros_like(db_ref)

    hid = lane_head((TOK, LB))
    scale = HD**-0.5
    for w in range(2):
        r = slice(w * TOK, (w + 1) * TOK)
        for blk in range(LP // LB):
            l = blk * LB
            q = proj_ref[0, r, l : l + LB]
            k = proj_ref[0, r, LP + l : LP + l + LB]
            v = proj_ref[0, r, 2 * LP + l : 2 * LP + l + LB]
            do = da_ref[0, r, l : l + LB]
            qt, kt, dt = q.T, k.T, do.T
            dq, dk, dv = [], [], []
            dps = nn(jnp.concatenate([jnp.where(hid == h, v, jnp.zeros_like(v)) for h in range(HB)], axis=0), dt)
            for h in range(HB):
                hh = blk * HB + h
                s = slice(HD * h, HD * h + HD)
                dp = dps[h * TOK : (h + 1) * TOK]
                pb = pt_ref[0, w, hh]
                p = pb.astype(F32)
                pd = p * dp
                ds = pd - p * colsum(pd)
                db_ref[hh] += ds
                dsb = ds.astype(BF)
                dq.append(nn(kt[s, :], dsb))
                dk.append(nt(qt[s, :], dsb))
                dv.append(nt(dt[s, :], pb))
            gp_ref[0, r, l : l + LB] = (jnp.concatenate(dq, axis=0) * scale).astype(BF).T
            gp_ref[0, r, LP + l : LP + l + LB] = (jnp.concatenate(dk, axis=0) * scale).astype(BF).T
            gp_ref[0, r, 2 * LP + l : 2 * LP + l + LB] = jnp.concatenate(dv, axis=0).astype(BF).T


def back_call(group, proj, pt, da, after):
    n = proj.shape[0]

    def blk(*s):
        return pl.BlockSpec((1,) + s, lambda i: (i,) + (0,) * len(s))

    return run(
        back_kernel, 3, (proj, pt, da), after,
        grid=(n,),
        in_specs=[blk(ROWS, 3 * LP), blk(2, HP, TOK, TOK), pl.BlockSpec((1, ROWS, LP), lambda i: (i, 0, group))],
        out_specs=[blk(ROWS, 3 * LP), full((HP, TOK, TOK))],
        out_shape=[SD((n, ROWS, 3 * LP), BF), SD((HP, TOK, TOK), F32)],
        compiler_params=params(),
        cost_estimate=cost(1.8e10, 10 * MB),
        name="attend_back",
    )


def inner_kernel(spot_ref, n1t_ref, gp0_ref, gp1_ref, gp2_ref, os_ref, ok_ref, xs_ref, xk_ref, ys_ref, yk_ref, sum_ref):
    me = spot_ref[0]
    core = spot_ref[1]
    n = gp0_ref.shape[0]
    ys_ref[:, 1:2] = os_ref[...]
    yk_ref[:, 1:2] = ok_ref[...]
    for p, gp_ref, send, keep, m in ((0, gp0_ref, xs_ref, xk_ref, 0), (1, gp1_ref, ys_ref, yk_ref, 0), (2, gp2_ref, xs_ref, xk_ref, 1)):
        gp = gp_ref[...].reshape(n * ROWS, 3 * LP)
        sum_ref[p] = colsum(gp.astype(F32))
        gi = nn(n1t_ref[...], gp).astype(BF)

        for c in range(2):
            @pl.when(core == c)
            def _():
                for b in range(4):
                    r = slice(b * OWN, (b + 1) * OWN)
                    rel = jnp.bitwise_xor(me, b)
                    rel = rel if p == 1 else crossed(rel)
                    keep[rel, m] = gi[r, c * CH : (c + 1) * CH]
                    send[rel, m] = gi[r, (1 - c) * CH : (2 - c) * CH]


def inner_call(spot, n1t, gps, outer, after):
    block = SD((4, 2, OWN, CH), BF)
    return single(
        inner_kernel, (spot, n1t, *gps, *outer), [block] * 4 + [SD((3, 1, 3 * LP), F32)], after,
        cost_estimate=cost(1.2e10, 12 * MB), name="inner_grad",
    )


def last_kernel(tok_ref, gmid_ref, vec_ref, pmt_ref, gp0_ref, gp1_ref, gp2_ref, w0_ref, w1_ref, w2_ref,
                small_ref, stay_ref, send_ref):
    @pl.when(pl.program_id(0) == 0)
    def _():
        small_ref[...] = jnp.zeros_like(small_ref)

    d = nt(gp0_ref[0], w0_ref[...]) + nt(gp1_ref[0], w1_ref[...]) + nt(gp2_ref[0], w2_ref[...])
    xh, r = norm_parts(tok_ref[0].astype(F32))
    small_ref[0:1, :] += colsum(d * xh)
    small_ref[1:2, :] += colsum(d)
    d = d * vec_ref[2:3, :]
    gm = gmid_ref[0].astype(F32) + r * (d - jnp.mean(d, axis=-1, keepdims=True) - xh * jnp.mean(d * xh, axis=-1, keepdims=True))
    o = nn(pmt_ref[...], gm.astype(BF)).astype(BF)
    stay_ref[0] = o[:TOK]
    send_ref[0] = o[TOK:]


def last_call(first, n, tok, gmid, gain, pmt, gps, ws, after):
    def blk(*s):
        return pl.BlockSpec((1,) + s, lambda i: (first + i,) + (0,) * len(s))

    cut = pl.BlockSpec((1, TOK, D), lambda i: (i, 0, 0))

    return run(
        last_kernel, 10, (tok, gmid, gain, pmt, *gps, *ws), after,
        grid=(n,),
        in_specs=[blk(ROWS, D), blk(ROWS, D), full((8, D)), full((ROWS, ROWS))] + [blk(ROWS, 3 * LP)] * 3
        + [full((D, 3 * LP), **ONE)] * 3,
        out_specs=[full((8, D)), cut, cut],
        out_shape=[SD((8, D), F32), SD((n, TOK, D), BF), SD((n, TOK, D), BF)],
        compiler_params=params(),
        cost_estimate=cost(2e10, 20 * MB),
        name="last",
    )


def vector_finish_kernel(count, spot_ref, mine_ref, other_ref, thr_ref, inner_ref, inb_ref, outb_ref, upb_ref, downb_ref, g1_ref, s1_ref,
                         g2_ref, s2_ref, table_ref, clip_ref, factor_ref, max_ref, sums_ref):
    shard = spot_ref[2]
    sums_ref[...] = join_vectors(mine_ref[...], other_ref[...])

    def part(ref, rows, step=1):
        size = ref.shape[0]
        start = shard * size
        row = sums_ref[pl.ds(rows + step * (start // D), 1), :]
        row = jnp.broadcast_to(row, (8, D))
        ref[...] = pltpu.roll(row, (D - start % D) % D, 1)[0:1, :size].reshape(size)

    part(inb_ref, V_IN, 2)
    part(upb_ref, V_UP)
    for i, ref in enumerate((downb_ref, g2_ref, s2_ref, outb_ref)):
        part(ref, V_SMALL + i)
    part(g1_ref, V_ONE)
    part(s1_ref, V_ONE + 1)
    table_ref[...] = sums_ref[V_TABLE : V_TABLE + HEADS, : SPAN * SPAN]
    top = sums_ref[V_PEAK : V_PEAK + 1, :HEADS]
    factor = thr_ref[...].reshape(1, HEADS)
    factor = factor / jnp.maximum(top, factor)
    max_ref[...] = top.reshape(HEADS)
    factor_ref[...] = factor.reshape(HEADS)
    root = jnp.broadcast_to(jnp.sqrt(factor), (8, HEADS))
    head = lax.broadcasted_iota(jnp.int32, (HEADS, D), 0)
    col = lax.broadcasted_iota(jnp.int32, (HEADS, D), 1) // HD
    scale = lax.dot_general(root, (head == col).astype(F32), (((1,), (0,)), ((), ())), preferred_element_type=F32,
                            precision=lax.Precision.HIGHEST)[0:1, :]
    for k in range(2):
        clip_ref[:, k * D : (k + 1) * D] = (inner_ref[:, k * D : (k + 1) * D].astype(F32) * scale).astype(BF)
    clip_ref[:, 2 * D :] = inner_ref[:, 2 * D :]


def vector_finish(place, mine, other, threshold, inner, count):
    line = SD((D // count,), F32)
    return single(
        functools.partial(vector_finish_kernel, count), (place, mine, other, threshold, inner),
        [SD((2 * D // count,), F32), line, SD((FF // count,), F32), line, line, line, line, line,
         SD((HEADS, SPAN * SPAN), F32), SD(inner.shape, BF), SD((HEADS,), F32), SD((HEADS,), F32)],
        scratch=[pltpu.VMEM((V_ROWS, D), F32)],
        cost_estimate=cost(1e7, 3 * MB), name="vector_finish",
    )


def feed_finish_kernel(spot_ref, mine_ref, other_ref, ge_ref, gr_ref):
    for core in range(2):
        @pl.when(spot_ref[1] == core)
        def _():
            for c, ref in ((core, mine_ref), (1 - core, other_ref)):
                for b in range(4):
                    ge_ref[:, (2 * b + c) * CH : (2 * b + c + 1) * CH] = ref[b].astype(F32)
                    r = c * CH + (b // 2) * OWN
                    gr_ref[r : r + OWN, (b % 2) * CH : (b % 2 + 1) * CH] = ref[4 + b].astype(F32)


def inner_columns(p, c):
    if c == 0:
        return [(0, LP, p * LP), (LP, LP // 2, D + p * LP)]
    return [(0, LP // 2, D + p * LP + LP // 2), (LP // 2, LP, 2 * D + p * LP)]


def inner_finish_kernel(spot_ref, mine_ref, other_ref, gi_ref, go_ref):
    for core in range(2):
        @pl.when(spot_ref[1] == core)
        def _():
            for c, ref in ((core, mine_ref), (1 - core, other_ref)):
                for k, p in enumerate((0, 2, 1)):
                    for at, size, put in inner_columns(p, c):
                        gi_ref[:, put : put + size] = ref[k, :, at : at + size].astype(F32)
                go_ref[:, c * CH : (c + 1) * CH] = ref[3].astype(F32)


def finish_kernel(count, place_ref, mine_ref, other_ref, thr_ref, inner_ref, fm_ref, fo_ref, im_ref, io_ref, *outs):
    vectors, (ge_ref, gr_ref, gi_ref, go_ref, sums_ref) = outs[:12], outs[12:]
    inner_finish_kernel(place_ref, im_ref, io_ref, gi_ref, go_ref)
    feed_finish_kernel(place_ref, fm_ref, fo_ref, ge_ref, gr_ref)
    vector_finish_kernel(count, place_ref, mine_ref, other_ref, thr_ref, inner_ref, *vectors, sums_ref)


def finish(place, vectors, threshold, inner, feed, rest):
    line = SD((D // 4,), F32)
    return single(
        functools.partial(finish_kernel, 4), (place, *vectors, threshold, inner, *feed, *rest),
        [SD((2 * D // 4,), F32), line, SD((FF // 4,), F32), line, line, line, line, line,
         SD((HEADS, SPAN * SPAN), F32), SD(inner.shape, BF), SD((HEADS,), F32), SD((HEADS,), F32),
         SD((OWN, FF), F32), SD((2 * CH, D), F32), SD((OWN, 3 * D), F32), SD((OWN, D), F32)],
        scratch=[pltpu.VMEM((V_ROWS, D), F32)], cost_estimate=cost(1e7, 12 * MB), name="finish",
    )


def swap(block, axis, bit):
    count = lax.axis_size(axis)
    return lax.ppermute(block, axis, [(i, i ^ bit) for i in range(count) if i ^ bit < count])


def join_vectors(a, b):
    row = lax.broadcasted_iota(jnp.int32, a.shape, 0)
    return jnp.where(row == V_PEAK, jnp.maximum(a, b), a + b)


class Everywhere:
    def __init__(self, sums, ones, direct):
        self.value = [sums, *ones]
        self.flying = []
        self.hops = [("replica", (1,)), ("shard", (1, 2, 3)), ("replica", (2,)), ("half", (1,))]
        if not direct:
            self.hops = [
                (axis, (1 << k,))
                for axis in ("shard", "replica", "half") for k in range((lax.axis_size(axis) - 1).bit_length())
            ]
        self.done = False

    def inputs(self):
        return self.value + self.flying

    def compute(self, values, low, low2):
        v, *others = values
        if not self.flying:
            ones = others[0] + others[1]
            return [jnp.concatenate([v[:V_ONE], ones[:2], v[V_ONE + 2 :]], axis=0)]
        if len(others) == 3:
            return [join_vectors(join_vectors(v, others[0]), join_vectors(others[1], others[2]))]
        return [join_vectors(v, others[0])]

    def launch(self, outs):
        self.value = outs
        self.done = not self.hops
        if self.hops:
            axis, bits = self.hops.pop(0)
            self.flying = [swap(outs[0], axis, bit) for bit in bits]


def near(block):
    return [swap(block, "shard", 1), swap(block, "shard", 2)]


def fence(*values):
    return lax.optimization_barrier(values)


def add(a, b):
    return (a.astype(F32) + b.astype(F32)).astype(BF)


class Reduction:
    def __init__(self, sends, keeps, quarters):
        self.quarters = quarters
        self.keep = keeps
        self.stage = 0
        self.sent = sends
        self.flying = [swap(v, "half", 1) for v in sends]

    def inputs(self):
        return list(self.keep) + list(self.flying)

    def compute(self, values, low, low2):
        hlf = OWN // 2
        kept, got = values[: len(self.keep)], values[len(self.keep) :]
        if self.stage == 0:
            return [add(k[:2], g[:2]) for k, g in zip(kept, got)] + [add(k[2:], g[2:]) for k, g in zip(kept, got)]
        if self.stage == 1:
            return [add(k[0], g[0]) for k, g in zip(kept, got)] + [add(k[1], g[1]) for k, g in zip(kept, got)]
        if self.stage == 2:
            if self.quarters:
                u, v = (add(k, g) for k, g in zip(kept, got))
                return [jnp.where(low, u, v), jnp.where(low, v, u)]
            v = jnp.concatenate([add(k, g) for k, g in zip(kept, got)], axis=0)
            return [jnp.where(low, v[:, :hlf], v[:, hlf:]), jnp.where(low, v[:, hlf:], v[:, :hlf])]
        v = kept[0]
        if self.quarters and self.stage == 3:
            v = add(v, got[0])
            return [jnp.where(low2, v[:, :hlf], v[:, hlf:]), jnp.where(low2, v[:, hlf:], v[:, :hlf])]
        if self.quarters and self.stage == 5:
            return [jnp.concatenate([jnp.where(low2, v, got[0]), jnp.where(low2, got[0], v)], axis=1)]
        if self.quarters and self.stage == 6:
            return [jnp.concatenate([jnp.where(low, v, got[0]), jnp.where(low, got[0], v)], axis=0)]
        if self.stage in (3, 4):
            return [add(v, got[0])]
        return [jnp.concatenate([jnp.where(low, v, got[0]), jnp.where(low, got[0], v)], axis=1)]

    def launch(self, outs):
        if self.stage < 2:
            half = len(outs) // 2
            self.keep, self.sent = outs[:half], outs[half:]
            bits = (1, 2) if self.stage == 0 else (2, 1)
            self.flying = [swap(v, "shard", bit) for v, bit in zip(self.sent, bits)]
        else:
            self.keep, self.sent = outs[:1], outs[-1:]
            if self.stage == (6 if self.quarters else 5):
                self.flying = [swap(self.keep[0], "half", 1)]
            else:
                far = (3, 4) if self.quarters else (3,)
                self.flying = [swap(self.sent[0], "replica", 2 if self.stage in far else 1)]
        self.stage += 1


def hop_kernel(chains, counts, place_ref, *refs):
    replica = place_ref[3]
    low, low2 = (replica & 1) == 0, (replica & 2) == 0
    refs = list(refs)
    inputs = [[refs.pop(0)[...] for _ in range(count)] for count in counts]
    for chain, values in zip(chains, inputs):
        for out in chain.compute(values, low, low2):
            refs.pop(0)[...] = out


def together(place, chains, *others, plain=False):
    flying, others = fence([c.flying for c in chains], others)
    for c, v in zip(chains, flying):
        c.flying = v
    inputs = [c.inputs() for c in chains]
    low, low2 = (place[3] & 1) == 0, (place[3] & 2) == 0
    shapes = [jax.eval_shape(c.compute, v, low, low2) for c, v in zip(chains, inputs)]
    if plain:
        outs = [c.compute(v, low, low2) for c, v in zip(chains, inputs)]
    else:
        flat = [x for v in inputs for x in v]
        results = list(single(
            functools.partial(hop_kernel, chains, [len(v) for v in inputs]), (place, *flat),
            [SD(x.shape, x.dtype) for v in shapes for x in v], cost_estimate=cost(1e7, 4 * MB), name="hop",
        ))
        outs = [[results.pop(0) for _ in v] for v in shapes]
    for c, v in zip(chains, outs):
        c.launch(v)
    return others


def quick_layout(me, core):
    def places(rows):
        at = [me * rows]
        for c in (core, 1 - core):
            at += [(me ^ r) * rows + c * (rows // 2) for r in (1, 2, 3)]
        return at

    first = [(k, 0, OWN, 0, 3 * LP, 0, 0) for k in range(4)], [(me ^ r) * OWN for r in range(4)]
    others = [
        ([(k, 0, OWN if k == 0 else OWN // 2, c, 3 * LP, 0, 0) for k in range(7)], places(OWN)) for c in (0, 3 * LP)
    ]
    hlf = OWN // 2
    short = places(OWN)
    long = [None] + [c * 4 * CH + (me ^ r) * CH for c in (core, 1 - core) for r in (1, 2, 3)]
    plan, at = [(0, 0, OWN, 0, D, 0, 0)], [short[0]]
    for k in range(8):
        plan.append((1, 0, OWN, hidden_block(k) * CH, CH, 1, k * CH))
        at.append(short[0])
    for c in range(2):
        plan.append((2, c * CH, CH, 0, D, 2, 0))
        at.append(c * 4 * CH + me * CH)
    parts = [(b * hlf, hlf, 1, b * D) for b in range(4)] + [(4 * hlf, hlf, 0, 0), (5 * hlf, 4 * hlf, 2, 0)]

    def add_piece(source, lo, hi, place):
        for row, rows, target, column in parts:
            a, b = max(row, lo), min(row + rows, hi)
            if a < b and target == 1:
                for c in range(2):
                    plan.append((source, a - lo, b - a, c * CH, CH, 1, c * 4 * CH + column // 2))
                    at.append(short[place] + (a - row))
            elif a < b:
                plan.append((source, a - lo, b - a, 0, D, target, column))
                at.append((long if target == 2 else short)[place] + (a - row))

    for side in range(2):
        for k in range(2):
            add_piece(3 + 4 * side + k, 0, BIG, 1 + 3 * side + k)
        add_piece(5 + 4 * side, 0, BIG // 2, 3 + 3 * side)
        add_piece(6 + 4 * side, BIG // 2, BIG, 3 + 3 * side)
    return [first, *others, (plan, at)]


def fallback_layout():
    first = [([(0, 0, D, c, 3 * LP, 0, 0)], [0]) for c in (0, 0, 3 * LP)]
    plan, at = [(0, 0, D, 0, D, 0, 0)], [0]
    for k in range(8):
        plan += [(1, 0, D, hidden_block(k) * CH, CH, 1, k * CH), (2, hidden_block(k) * CH, CH, 0, D, 2, 0)]
        at += [0, k * CH]
    return first + [(plan, at)]


def plans_of(layout):
    base, plans = 4, []
    for entries, rows in layout:
        plans.append((base, entries))
        base += len(rows)
    return plans


def quick_plans():
    return plans_of(quick_layout(0, 0))


def fallback_plans():
    return plans_of(fallback_layout())


def fallback_places():
    return [jnp.int32(v) for _, rows in fallback_layout() for v in rows]


def index_table():
    return np.array(
        [
            [me, core, me, replica] + [v for _, rows in quick_layout(me, core) for v in rows]
            for replica in range(4) for me in range(4) for core in range(2)
        ],
        np.int32,
    )


def shards(images, cotangent, present, threshold, inner_weight, inner_bias, outer_weight, outer_bias, expand_weight,
           expand_bias, reduce_weight, reduce_bias, first_gain, first_shift, second_gain, second_shift, bias_table):
    n = images.shape[0]
    core = lax.axis_index("half")
    shard = lax.axis_index("shard")
    replica = lax.axis_index("replica")
    shard_count = lax.axis_size("shard")
    quick = shard_count == 4 and lax.axis_size("replica") == 4
    me = shard if quick else jnp.int32(0)
    if quick:
        spot = lax.dynamic_index_in_dim(jnp.asarray(index_table()), (replica * 4 + shard) * 2 + core, 0, False)
    else:
        spot = jnp.stack([me, core, shard, replica] + fallback_places()).astype(jnp.int32)
    place = spot
    own_images = images.reshape(n, ROWS, D)
    own_grad = cotangent.reshape(n, ROWS, D)
    vectors = (inner_bias, outer_bias, expand_bias, reduce_bias, first_gain, first_shift, second_gain, second_shift)
    order = jnp.asarray(row_order(), BF)
    back_order = jnp.asarray(row_order().T, BF)
    alive = present.astype(F32).reshape(1, n)
    table_rows = jnp.pad(bias_table.astype(F32).T, ((0, 0), (0, WIDE - bias_table.shape[0])))
    if quick:
        first, others, others_half, up = first_call(spot, vectors, inner_weight, own_images, own_grad)
        first, up, spot, others_half = fence(first, up, spot, others_half)
        get_first = near(first)
        upper = swap(up, "half", 1)
        masks_0 = bias_call(0, table_rows)
        big = cut_call(spot, outer_weight, expand_weight, reduce_weight)
        get_first, upper, masks_0, others_half, big = fence(get_first, upper, masks_0, others_half, big)
        get_first.append(swap(get_first[0], "shard", 2))
        get_others = near(others_half)
        tok, g, grad_down = prep_call(own_images, own_grad, upper, alive, order)
        get_first, get_others, tok, spot, big = fence(get_first, get_others, tok, spot, big)
        first_pieces = [first] + get_first
        get_others.append(swap(get_others[1], "shard", 1))
        in_bias, up_bias, vecs, n1, n1t = vector_call(spot, first_pieces, tok)
        get_others, n1, big = fence(get_others, n1, big)
        others_back = [swap(v, "half", 1) for v in get_others]
        get_big = near(big)
    else:
        masks_0 = bias_call(0, table_rows)
        upper = jnp.concatenate([swap(own_images[:, :TOK], "half", 1), swap(own_grad[:, :TOK], "half", 1)])
        whole_vectors = [lax.all_gather(v, "shard", axis=0, tiled=True).reshape(4, -1) for v in vectors]
        parts = jnp.stack([jnp.pad(v, ((0, 0), (0, D - v.shape[1]))) for v in whole_vectors], axis=1)
        parts = [jnp.pad(parts[r], ((0, 8), (0, 0))) for r in range(4)]
        thirds = inner_weight.reshape(-1, 3, 3, LP).transpose(0, 2, 1, 3).reshape(-1, 3, 3 * LP)
        first = thirds[:, 0]
        others = thirds[:, 1:].reshape(-1, 6 * LP)

        tok, g, grad_down = prep_call(own_images, own_grad, upper, alive, order)
        in_bias, up_bias, vecs, n1, n1t = vector_call(spot, parts, tok)

    if quick:
        first_at = in_at = spot
        in_plans = quick_plans()[:3]
    else:
        first_at = in_at = spot
        first_pieces = [lax.all_gather(first, "shard", axis=0, tiled=True)]
        others_pieces = [lax.all_gather(others, "shard", axis=0, tiled=True)]
        in_plans = fallback_plans()[:3]

    results = [attend_call(0, spot, n1, in_bias, masks_0, first_at, in_plans[0], first_pieces, [])]
    if quick:
        others_back, results, table_rows = fence(others_back, results, table_rows)
    masks_1 = bias_call(1, table_rows)
    if quick:
        masks_1, spot, table_rows = fence(masks_1, spot, table_rows)
        others_pieces = [others] + get_others + others_back
    results.append(attend_call(1, spot, n1, in_bias, masks_1, in_at, in_plans[1], others_pieces, []))
    if quick:
        get_big, results, table_rows = fence(get_big, results, table_rows)
        far = [swap(get_big[0][: BIG // 2], "shard", 2), swap(get_big[1][BIG // 2 :], "shard", 1)]
        big_back = [swap(v, "half", 1) for v in get_big]
    masks_2 = bias_call(2, table_rows)
    results.append(attend_call(2, spot, n1, in_bias, masks_2, in_at, in_plans[2], others_pieces, []))
    if quick:
        far, big_back, results = fence(far, big_back, results)
        far_back = [swap(v, "half", 1) for v in far]
        far_back, results = fence(far_back, results)
        pieces = [outer_weight, expand_weight, reduce_weight] + get_big + far + big_back + far_back
        plan = quick_plans()[3]
    else:
        pieces = [lax.all_gather(v, "shard", axis=0, tiled=True) for v in (outer_weight, expand_weight, reduce_weight)]
        plan = fallback_plans()[3]
    at = spot
    projs, pts, atts, peak, ws = zip(*results)
    (stay, send, gmid, datt, out_send, out_keep, e_send, e_keep, r_send, r_keep, grad_up, small) = middle_call(
        spot, tok, atts, g, back_order, vecs, up_bias, at, plan, pieces, []
    )
    def wait_for(chains):
        return [v for c in chains for v in c.sent]

    after = []
    if quick:
        feed = Reduction([e_send, r_send], [e_keep, r_keep], True)
    lower_out = swap(send, "half", 1)
    gp0, db0 = back_call(0, projs[0], pts[0], datt, [])
    if quick:
        gp0, lower_out, projs = together(place, [feed], gp0, lower_out, projs)
        after = wait_for([feed])
    gp1, db1 = back_call(1, projs[1], pts[1], datt, after)
    gp2, db2 = back_call(2, projs[2], pts[2], datt, [gp1])
    x_send, x_keep, y_send, y_keep, sums_in = inner_call(spot, n1t, (gp0, gp1, gp2), (out_send, out_keep), [])
    peak = jnp.concatenate(peak, axis=2)
    peaks = jnp.max(jnp.where((present > 0)[:, None, None, None], peak, NEGATIVE), axis=(0, 1, 3)).reshape(1, HEADS)
    after = [x_send]
    if quick:
        x_send, y_send, gp2 = together(place, [feed], x_send, y_send, gp2)
        rest = Reduction([x_send, y_send], [x_keep, y_keep], False)
        after = wait_for([feed])
    half = n // 2
    one_a, gstay_a, gsend_a = last_call(0, half, tok, gmid, vecs, back_order, (gp0, gp1, gp2), ws, after)
    after = [gsend_a]
    if quick:
        gsend_a, one_a = together(place, [rest, feed], gsend_a, one_a)
        after = wait_for([rest, feed])
    lower_a = swap(gsend_a, "half", 1)
    one_b, gstay_b, gsend_b = last_call(half, n - half, tok, gmid, vecs, back_order, (gp0, gp1, gp2), ws, after)
    after = [gsend_b]
    if quick:
        gsend_b, lower_a = together(place, [rest, feed], gsend_b, lower_a)
        after = wait_for([rest, feed])
    lower_b = swap(gsend_b, "half", 1)
    sums = table_call((db0, db1, db2), grad_up, grad_down, small, sums_in, peaks, after)
    every = Everywhere(sums, (one_a, one_b), quick)
    if quick:
        rest.flying, feed.flying, lower_b = fence(rest.flying, feed.flying, lower_b)
        together(place, [rest, every, feed])
        block_out = jnp.concatenate([lower_out, stay], axis=1)
        (block_out,) = together(place, [rest, every, feed], block_out)
        grad_images = jnp.concatenate([jnp.concatenate([lower_a, lower_b]), jnp.concatenate([gstay_a, gstay_b])], axis=1)
        (grad_images,) = together(place, [rest, every], grad_images)
        rest.flying, every.flying, feed.flying = fence(rest.flying, every.flying, feed.flying)
        together(place, [rest, every, feed])
    else:
        while every.hops:
            together(place, [every])
        block_out = jnp.concatenate([lower_out, stay], axis=1)
        grad_images = jnp.concatenate([jnp.concatenate([lower_a, lower_b]), jnp.concatenate([gstay_a, gstay_b])], axis=1)

    vectors = (every.value[0], every.flying[0])
    if quick:
        *vectors, grad_expand, grad_reduce, grad_inner, grad_outer = finish(
            place, vectors, threshold, inner_weight, feed.keep + feed.flying, rest.keep + rest.flying
        )
    else:
        def halves(keep, send, axis):
            lo = jnp.where(core == 0, keep, send)
            hi = jnp.where(core == 0, send, keep)
            return jnp.concatenate([lo, hi], axis=axis)

        def whole(keep, send):
            both = halves(keep[:, :, :, None], send[:, :, :, None], 3)
            return both.transpose(0, 2, 1, 3, 4).reshape(D, -1)

        def settle(v):
            v = lax.psum_scatter(v.astype(BF), "shard", scatter_dimension=0, tiled=True)
            return lax.psum(v, ("replica", "half")).astype(F32)

        def rows_of(v):
            return v.reshape(4, 1, 2, 2, OWN, CH).transpose(0, 1, 2, 4, 3, 5).reshape(4, 1, CH, D)

        def straight(v):
            return jnp.stack([v[0], v[2], v[1], v[3]])

        grad_reduce = settle(halves(rows_of(r_keep), rows_of(r_send), 1).reshape(FF, D))
        grad_expand = settle(whole(straight(e_keep), straight(e_send)))
        grad_outer = settle(whole(out_keep, out_send))
        x_keep, x_send = straight(x_keep), straight(x_send)
        by_third = [
            whole(x_keep[:, :1], x_send[:, :1]), whole(y_keep[:, :1], y_send[:, :1]), whole(x_keep[:, 1:], x_send[:, 1:])
        ]
        by_third = jnp.stack(by_third, axis=1).reshape(D, 3, 3, LP).transpose(0, 2, 1, 3).reshape(D, 3 * D)
        grad_inner = settle(by_third)

        vectors = vector_finish(place, *vectors, threshold, inner_weight, shard_count)
    (grad_inbias, grad_outbias, grad_upbias, grad_downbias, grad_gain_1, grad_shift_1, grad_gain_2, grad_shift_2, grad_table,
     clipped, factors, maxima) = vectors
    block_out = block_out.reshape(images.shape)
    grad_images = grad_images.reshape(images.shape)
    return (
        block_out,
        grad_images,
        grad_inner,
        grad_inbias,
        grad_outer,
        grad_outbias,
        grad_expand,
        grad_upbias,
        grad_reduce,
        grad_downbias,
        grad_gain_1,
        grad_shift_1,
        grad_gain_2,
        grad_shift_2,
        grad_table.T,
        clipped,
        factors,
        maxima,
    )


def solution(mesh):
    rows = P(("replica", "shard"), "half", None, None)
    cut = P("shard", None)
    line = P("shard")
    return jax.shard_map(
        shards,
        mesh=mesh,
        in_specs=(rows, rows, P(("replica", "shard")), P(), cut, line, cut, line, cut, line, cut, line, line, line, line,
                  line, P()),
        out_specs=(rows, rows, cut, line, cut, line, cut, line, cut, line, line, line, line, line, P(), cut, P(), P()),
        check_vma=False,
    )
```

```python
import functools
import math

import numpy as np
import jax
import jax.numpy as jnp
from jax import lax
from jax.experimental import pallas as pl
from jax.experimental.pallas import tpu as pltpu
from jax.sharding import PartitionSpec as P

D = 768
HEADS = 24
HD = 32
WIN = 12
GRID = 24
SHIFT = 6
FF = 3072
TOK = WIN * WIN
ROWS = WIN * GRID
SPAN = 2 * WIN - 1
EPS = 1e-5
MASKED = -100.0
NEGATIVE = -1e30
LOG2E = math.log2(math.e)
BF = jnp.bfloat16
F32 = jnp.float32
MB = 1 << 20
OWN = 192
CH = 384
WIDE = 640
NARROW = 384
TALL = WIN * 16
HB = 8
LB = HB * HD
HP = 8
LP = HP * HD
NB = 576
SCALE = 1e-3
ONE = dict(pipeline_mode=pl.Buffered(1))
SD = jax.ShapeDtypeStruct


def nn(a, b):
    return lax.dot_general(a, b, (((1,), (0,)), ((), ())), preferred_element_type=F32)


def nt(a, b):
    return lax.dot_general(a, b, (((1,), (1,)), ((), ())), preferred_element_type=F32)


def tn(a, b):
    return lax.dot_general(a, b, (((0,), (0,)), ((), ())), preferred_element_type=F32)


def full(shape, **kw):
    return pl.BlockSpec(shape, lambda *_: (0,) * len(shape), **kw)


def any_space():
    return pl.BlockSpec(memory_space=pl.ANY)


def smem():
    return pl.BlockSpec(memory_space=pltpu.SMEM)


def run(kernel, count, args, after, in_specs, **kw):
    def body(*refs):
        kernel(*refs[:count], *refs[count + len(after) :])

    return pl.pallas_call(body, in_specs=list(in_specs) + [any_space()] * len(after), **kw)(*args, *after)


def params(limit=63):
    return pltpu.CompilerParams(vmem_limit_bytes=limit * MB)


def cost(flops, moved, exps=0):
    return pl.CostEstimate(flops=int(flops * SCALE), bytes_accessed=int(moved * SCALE), transcendentals=0)


def whole(array):
    return full(array.shape, **ONE)


def single(kernel, args, out_shape, after=(), scratch=(), **kw):
    specs = [smem() if v.dtype == jnp.int32 else whole(v) for v in args]
    shapes = out_shape if isinstance(out_shape, (list, tuple)) else [out_shape]
    out = run(
        kernel, len(args), args, after, grid=(1,), in_specs=specs, out_specs=[whole(v) for v in shapes], out_shape=list(shapes),
        scratch_shapes=list(scratch), compiler_params=params(), **kw
    )
    return out if isinstance(out_shape, (list, tuple)) else out[0]


def colsum(v):
    return jnp.sum(v, axis=0, keepdims=True)


def norm_parts(x):
    c = x - jnp.mean(x, axis=-1, keepdims=True)
    r = lax.rsqrt(jnp.mean(c * c, axis=-1, keepdims=True) + EPS)
    return c * r, r


def row_order():
    cells = np.arange(ROWS)
    win, rest = cells // TOK, cells % TOK
    a, b = rest // WIN, rest % WIN
    m = np.zeros((ROWS, ROWS), np.float32)
    m[cells, a * GRID + (win * WIN + b + SHIFT) % GRID] = 1
    return m


def spread_q():
    q = np.arange(TOK)
    m = np.zeros((TOK, NARROW), np.float32)
    m[q, SPAN * (q // WIN) + q % WIN] = 1
    return m


def spread_k(reverse):
    k = np.arange(TOK)
    b = k % WIN
    m = np.zeros((TALL, TOK), np.float32)
    m[16 * (k // WIN) + (WIN - 1 - b if reverse else b), k] = 1
    return m


def copies(plan, refs, at, targets, sems):
    base, entries = plan
    for i, (src, row, rows, col, cols, dst, put) in enumerate(entries):
        place = pl.ds(pl.multiple_of(at[base + i], 16), rows)
        yield pltpu.make_async_copy(
            refs[src].at[pl.ds(row, rows), pl.ds(col, cols)], targets[dst].at[place, pl.ds(put, cols)], sems.at[i]
        )


def hidden_block(k):
    return 2 * (k % 4) + k // 4


def region_masks():
    line = np.arange(GRID)
    region = (line >= GRID - WIN).astype(np.int32) + (line >= GRID - SHIFT).astype(np.int32)
    lab = 3 * region[:, None] + region[None, :]
    lab = lab.reshape(2, WIN, 2, WIN).transpose(0, 2, 1, 3).reshape(2, 2, TOK)
    return np.where(lab[:, :, :, None] != lab[:, :, None, :], MASKED, 0.0).astype(np.float32)


def bias_kernel(table_ref, sq_ref, sk_ref, out_ref, tall):
    for h in range(HP):
        row = pltpu.roll(jnp.broadcast_to(table_ref[h : h + 1, :], (16, WIDE)), 0, 1, stride=1, stride_axis=0)
        for a in range(WIN):
            off = (SPAN * a - SPAN * (WIN - 1) - (WIN - 1)) % WIDE
            tall[16 * a : 16 * a + 16, :] = pltpu.roll(row, off, 1)[:, :NARROW].astype(BF)
        wide = nn(tall[...], sq_ref[...]).astype(BF)
        out_ref[h] = nn(sk_ref[...], wide).astype(BF)


def bias_call(group, table):
    args = (table, jnp.asarray(spread_q().T, BF), jnp.asarray(spread_k(False).T, BF))
    out = SD((HP, TOK, TOK), BF)
    return pl.pallas_call(
        bias_kernel,
        grid=(1,),
        in_specs=[pl.BlockSpec((HP, WIDE), lambda i: (group, 0))] + [whole(v) for v in args[1:]],
        out_specs=whole(out),
        out_shape=out,
        scratch_shapes=[pltpu.VMEM((TALL, NARROW), BF)],
        compiler_params=params(),
        cost_estimate=cost(2e9, 2 * MB),
        name="bias",
    )(*args)


V_UP, V_SMALL, V_IN, V_ONE, V_PEAK, V_TABLE, V_ROWS = 0, 4, 8, 11, 13, 16, 40


def table_kernel(db0_ref, db1_ref, db2_ref, up_ref, down_ref, small_ref, in_ref, peak_ref, sq_ref, sk_ref, out_ref):
    def split(v):
        hi = v.astype(BF)
        return hi, (v - hi.astype(F32)).astype(BF)

    out_ref[...] = jnp.zeros_like(out_ref)
    for k in range(8):
        b = hidden_block(k)
        out_ref[V_UP + b // 2 : V_UP + b // 2 + 1, (b % 2) * CH : (b % 2 + 1) * CH] = up_ref[
            k // 2, :, (k % 2) * CH : (k % 2 + 1) * CH
        ]
    out_ref[V_SMALL : V_SMALL + 1, :] = down_ref[...]
    out_ref[V_SMALL + 1 : V_SMALL + 4, :] = small_ref[1:4, :]
    for p in range(3):
        row = in_ref[p]
        for k in range(3):
            out_ref[V_IN + k : V_IN + k + 1, p * LP : (p + 1) * LP] = row[:, k * LP : (k + 1) * LP]
    out_ref[V_PEAK : V_PEAK + 1, :HEADS] = peak_ref[...]
    for h in range(HEADS):
        hi, lo = split((db0_ref, db1_ref, db2_ref)[h // HP][h % HP])
        tall = nn(sk_ref[...], hi) + nn(sk_ref[...], lo)
        hi, lo = split(tall)
        wide = nn(hi, sq_ref[...]) + nn(lo, sq_ref[...])
        wide = jnp.concatenate([wide, jnp.zeros((TALL, WIDE - NARROW), F32)], axis=1)
        tot = jnp.zeros((16, WIDE), F32)
        for a in range(WIN):
            tot = tot + pltpu.roll(wide[16 * a : 16 * a + 16, :], SPAN * (WIN - 1 - a), 1)
        tot = pltpu.roll(tot, 0, 1, stride=1, stride_axis=0)
        out_ref[V_TABLE + h : V_TABLE + h + 1, :WIDE] = colsum(tot)


def table_call(dbs, up, down, small, sums_in, peaks, after):
    args = (*dbs, up, down, small, sums_in, peaks, jnp.asarray(spread_q(), BF), jnp.asarray(spread_k(True), BF))
    return single(table_kernel, args, SD((V_ROWS, D), F32), after, cost_estimate=cost(6e9, 4 * MB), name="table")


def lane_head(shape):
    return lax.broadcasted_iota(jnp.int32, shape, len(shape) - 1) // HD


VECTORS = (2 * D, D, FF, D, D, D, D, D)


def first_kernel(spot_ref, *refs):
    vecs, (inner_ref, own_ref, gown_ref, first_ref, others_ref, half_ref, up_ref) = refs[:8], refs[8:]
    n = own_ref.shape[0]
    up_ref[:n] = own_ref[...]
    up_ref[n:] = gown_ref[...]
    mine = pl.ds(pl.multiple_of(spot_ref[1] * (OWN // 2), 16), OWN // 2)
    for k in range(3):
        first_ref[:OWN, k * LP : (k + 1) * LP] = inner_ref[:, k * D : k * D + LP]
        for p in (1, 2):
            src = slice(k * D + p * LP, k * D + (p + 1) * LP)
            dst = slice(((p - 1) * 3 + k) * LP, ((p - 1) * 3 + k + 1) * LP)
            others_ref[:, dst] = inner_ref[:, src]
            half_ref[:, dst] = inner_ref[mine, src]
    rows = [jnp.zeros((8, D), F32)]
    for v in vecs:
        row = v[...].astype(F32).reshape(1, v.shape[0])
        if v.shape[0] < D:
            row = jnp.concatenate([row, jnp.zeros((1, D - v.shape[0]), F32)], axis=1)
        rows.insert(-1, row)
    first_ref[OWN:, :] = jnp.concatenate(rows, axis=0).astype(BF)


def first_call(spot, vectors, inner, own, gown):
    n = own.shape[0]
    top = full((n, TOK, D))
    shapes = [SD((OWN + 16, D), BF), SD((OWN, 6 * LP), BF), SD((OWN // 2, 6 * LP), BF), SD((2 * n, TOK, D), BF)]
    return pl.pallas_call(
        first_kernel,
        grid=(1,),
        in_specs=[smem()] + [whole(v) for v in vectors] + [whole(inner), top, top],
        out_specs=[whole(v) for v in shapes],
        out_shape=shapes,
        compiler_params=params(),
        cost_estimate=cost(1e6, 6 * MB),
        name="first",
    )(spot, *vectors, inner, own, gown)


BIG = 4 * (OWN // 2) + OWN // 2 + 2 * OWN


def cut_kernel(spot_ref, outer_ref, expand_ref, reduce_ref, big_ref):
    core = spot_ref[1]
    hlf = OWN // 2
    mine = pl.ds(pl.multiple_of(core * hlf, 16), hlf)
    for k in range(4):
        big_ref[k * hlf : (k + 1) * hlf, :] = expand_ref[mine, k * D : (k + 1) * D]
    big_ref[4 * hlf : 5 * hlf, :] = outer_ref[mine, :]
    big_ref[5 * hlf :, :] = reduce_ref[pl.ds(pl.multiple_of(core * 2 * OWN, 16), 2 * OWN), :]


def cut_call(spot, outer, expand, reduce):
    return single(
        cut_kernel, (spot, outer, expand, reduce), [SD((BIG, D), BF)], cost_estimate=cost(1e6, 3 * MB), name="cut"
    )[0]


def halves_kernel(a_ref, b_ref, lower_ref, upper_ref):
    lower_ref[...] = a_ref[...]
    upper_ref[...] = b_ref[...]


def halves_call(a, b):
    rows, columns = a.shape
    half = SD((rows // 2, columns), BF)
    return pl.pallas_call(
        halves_kernel,
        grid=(1,),
        in_specs=[full((rows // 2, columns)), pl.BlockSpec((rows // 2, columns), lambda i: (1, 0))],
        out_specs=[full(half.shape), full(half.shape)],
        out_shape=[half, half],
        compiler_params=params(),
        cost_estimate=cost(1e6, 3 * MB),
        name="far_halves",
    )(a, b)


def prep_kernel(own_ref, gown_ref, recv_ref, alive_ref, pm_ref, tok_ref, g_ref, sum_ref):
    n = own_ref.shape[0]
    tot = jnp.zeros((1, D), F32)
    for i in range(n):
        tok_ref[i] = nn(pm_ref[...], jnp.concatenate([own_ref[i, TOK:, :], recv_ref[i]], axis=0)).astype(BF)
        g = nn(pm_ref[...], jnp.concatenate([gown_ref[i, TOK:, :], recv_ref[n + i]], axis=0)) * alive_ref[0:1, i : i + 1]
        g_ref[i] = g.astype(BF)
        tot = tot + colsum(g)
    sum_ref[...] = tot


def prep_call(own, gown, recv, alive, pm):
    rows = SD(own.shape, BF)
    return single(
        prep_kernel, (own, gown, recv, alive, pm), [rows, rows, SD((1, D), F32)], cost_estimate=cost(3e9, 16 * MB), name="prep"
    )


def vector_kernel(spot_ref, pa_ref, pb_ref, pc_ref, pd_ref, tok_ref, inb_ref, up_ref, vec_ref, n1_ref, n1t_ref, parts):
    n = tok_ref.shape[0]
    for r, ref in enumerate((pa_ref, pb_ref, pc_ref, pd_ref)):
        parts[jnp.bitwise_xor(spot_ref[0], r)] = ref[:8, :].astype(F32)

    def vector(i):
        size = VECTORS[i] // 4
        return jnp.concatenate([parts[s][i : i + 1, :size] for s in range(4)], axis=1)

    vin = vector(0)
    for p in range(3):
        inb_ref[p] = jnp.concatenate(
            [vin[:, p * LP : (p + 1) * LP], jnp.zeros((1, LP), F32), vin[:, D + p * LP : D + (p + 1) * LP]], axis=1
        )
    vup = vector(2)
    for k in range(8):
        up_ref[k // 2, :, (k % 2) * CH : (k % 2 + 1) * CH] = vup[:, hidden_block(k) * CH : (hidden_block(k) + 1) * CH]
    gain, shift = vector(4), vector(5)
    vec_ref[...] = jnp.zeros_like(vec_ref)
    for r, v in enumerate((vector(1), vector(3), gain, vector(6), vector(7))):
        vec_ref[r : r + 1, :] = v
    for i in range(n):
        xh, _ = norm_parts(tok_ref[i].astype(F32))
        n1 = (xh * gain + shift).astype(BF)
        n1_ref[i] = n1
        n1t_ref[:, i * ROWS : (i + 1) * ROWS] = n1.T


def vector_call(spot, parts, tok):
    n = tok.shape[0]
    last = parts[0].shape[0] // 16 - 1
    shapes = [SD((3, 1, 3 * LP), F32), SD((4, 1, 2 * CH), F32), SD((8, D), F32), SD(tok.shape, BF), SD((D, n * ROWS), BF)]
    return pl.pallas_call(
        vector_kernel,
        grid=(1,),
        in_specs=[smem()] + [pl.BlockSpec((16, D), lambda i: (last, 0))] * 4 + [whole(tok)],
        out_specs=[whole(v) for v in shapes],
        out_shape=shapes,
        scratch_shapes=[pltpu.VMEM((4, 8, D), F32)],
        compiler_params=params(),
        cost_estimate=cost(5e9, 8 * MB),
        name="vectors",
    )(spot, *parts, tok)


def attend_kernel(plan, count, spot_ref, n1_ref, b_ref, bias_ref, mask_ref, at_ref, *rest):
    pieces = rest[:count]
    proj_ref, pt_ref, att_ref, peak_ref, w_ref, sems = rest[count:]

    @pl.when(pl.program_id(0) == 0)
    def _():
        for c in copies(plan, pieces, at_ref, (w_ref,), sems):
            c.start()
        for c in copies(plan, pieces, at_ref, (w_ref,), sems):
            c.wait()

    proj_ref[0] = (nn(n1_ref[0], w_ref[...]) + b_ref[0]).astype(BF)
    hid = lane_head((TOK, LB))
    scale = HD**-0.5
    for w in range(2):
        r = slice(w * TOK, (w + 1) * TOK)
        mask = mask_ref[spot_ref[1], w].astype(F32)
        for blk in range(LP // LB):
            l = blk * LB
            q = proj_ref[0, r, l : l + LB]
            k = proj_ref[0, r, LP + l : LP + l + LB]
            v = proj_ref[0, r, 2 * LP + l : 2 * LP + l + LB]
            vt = v.T
            apart = jnp.concatenate([jnp.where(hid == h, k, jnp.zeros_like(k)) for h in range(HB)], axis=0)
            sts = nn(apart, q.T)
            outs = []
            for h in range(HB):
                hh = blk * HB + h
                st = sts[h * TOK : (h + 1) * TOK]
                peak_ref[0, w, hh : hh + 1, :] = jnp.max(st, axis=0, keepdims=True) * scale
                t = st * scale + (bias_ref[hh].astype(F32) + mask)
                e = jnp.exp(t - jnp.max(t, axis=0, keepdims=True))
                p = (e * (1.0 / colsum(e))).astype(BF)
                pt_ref[0, w, hh] = p
                outs.append(nn(vt[HD * h : HD * h + HD, :], p))
            att_ref[0, r, l : l + LB] = jnp.concatenate(outs, axis=0).astype(BF).T


def attend_call(group, spot, n1, b, bias, at, plan, pieces, after):
    n = n1.shape[0]

    def blk(*s):
        return pl.BlockSpec((1,) + s, lambda i: (i,) + (0,) * len(s))

    return run(
        functools.partial(attend_kernel, plan, len(pieces)), 6 + len(pieces),
        (spot, n1, b, bias, jnp.asarray(region_masks(), BF), at, *pieces), after,
        grid=(n,),
        in_specs=[smem(), blk(ROWS, D), pl.BlockSpec((1, 1, 3 * LP), lambda i: (group, 0, 0)), full((HP, TOK, TOK), **ONE),
                  full((2, 2, TOK, TOK), **ONE), smem()]
        + [any_space()] * len(pieces),
        out_specs=[blk(ROWS, 3 * LP), blk(2, HP, TOK, TOK), blk(ROWS, LP), blk(2, HP, TOK), full((D, 3 * LP), **ONE)],
        out_shape=[SD((n, ROWS, 3 * LP), BF), SD((n, 2, HP, TOK, TOK), BF), SD((n, ROWS, LP), BF), SD((n, 2, HP, TOK), F32),
                   SD((D, 3 * LP), BF)],
        scratch_shapes=[pltpu.SemaphoreType.DMA((len(plan[1]),))],
        compiler_params=params(),
        cost_estimate=cost(1.3e10, 12 * MB, 1.4e6),
        name="attend",
    )


def gelu_parts(h):
    d = 1.0 + (0.3275911 * 0.5**0.5) * jnp.abs(h)
    t = pl.reciprocal(d, approx=True)
    t = t * (2.0 - d * t)
    e = jnp.exp2(h * h * (-0.5 * LOG2E))
    p = (((0.5 * 1.061405429) * t - 0.5 * 1.453152027) * t + 0.5 * 1.421413741) * t - 0.5 * 0.284496736
    p = (p * t + 0.5 * 0.254829592) * t * e
    cdf = jnp.where(h >= 0, 1.0 - p, p)
    return cdf, cdf + h * (e * ((2 * math.pi) ** -0.5))


def middle_kernel(plan, count, spot_ref, tok_ref, att0_ref, att1_ref, att2_ref, gin_ref, pmt_ref, vec_ref, eb_ref,
                  at_ref, *rest):
    pieces = rest[:count]
    (stay_ref, send_ref, gmid_ref, datt_ref, os_ref, ok_ref, es_ref, ek_ref, rs_ref, rk_ref, geb_ref, small_ref,
     wo, we, wr, mid, n2, g, n2t, acc, e2, act, gh, sems) = rest[count:]
    j = pl.program_id(0)
    n = tok_ref.shape[0]
    N = n * ROWS
    me = spot_ref[0]
    core = spot_ref[1]
    early = [k for k, entry in enumerate(plan[1]) if entry[5] == 0]
    out_b, red_b, gain, shift = vec_ref[0:1, :], vec_ref[1:2, :], vec_ref[3:4, :], vec_ref[4:5, :]

    def attended(i):
        return jnp.concatenate([att0_ref[i], att1_ref[i], att2_ref[i]], axis=-1)

    @pl.when(j == 0)
    def _():
        moves = list(copies(plan, pieces, at_ref, (wo, we, wr), sems))
        for c in moves:
            c.start()
        for k in early:
            moves[k].wait()
        for i in range(n):
            s = slice(i * ROWS, (i + 1) * ROWS)
            g[s, :] = gin_ref[i]
            m = tok_ref[i].astype(F32) + nn(attended(i), wo[...]) + out_b
            mid[s, :] = m
            xh, _ = norm_parts(m)
            x2 = (xh * gain + shift).astype(BF)
            n2[s, :] = x2
            n2t[:, s] = x2.T
            acc[s, :] = m + red_b
            e2[s, :] = jnp.zeros((ROWS, D), F32)
        for k, c in enumerate(moves):
            if k not in early:
                c.wait()

    at = pl.multiple_of((2 * jnp.bitwise_xor(core, 1 - j // 2) + j % 2) * 2 * CH, 2 * CH)
    cols = pl.ds(at, 2 * CH)
    tot = jnp.zeros((1, 2 * CH), F32)
    for s0 in range(0, N, NB):
        s = slice(s0, s0 + NB)
        h = nn(n2[s, :], we[:, cols]) + eb_ref[0]
        cdf, dg = gelu_parts(h)
        act[s, :] = (h * cdf).astype(BF)
        x = (nt(g[s, :], wr[cols, :]) * dg).astype(BF)
        gh[s, :] = x
        tot = tot + colsum(x.astype(F32))
    geb_ref[0] = tot
    ge = nn(n2t[...], gh[...]).astype(BF)
    gr = tn(act[...], g[...]).astype(BF)

    def put(e_ref, r_ref):
        for t in range(2):
            for b in range(4):
                e_ref[crossed(jnp.bitwise_xor(me, b)), t] = ge[b * OWN : (b + 1) * OWN, t * CH : (t + 1) * CH]
                r_ref[jnp.bitwise_xor(me % 2, t), b] = gr[
                    t * CH + (b // 2) * OWN : t * CH + (b // 2 + 1) * OWN, (b % 2) * CH : (b % 2 + 1) * CH
                ]

    @pl.when(j < 2)
    def _():
        put(es_ref, rs_ref)

    @pl.when(j >= 2)
    def _():
        put(ek_ref, rk_ref)

    for s0 in range(0, N, NB):
        s = slice(s0, s0 + NB)
        acc[s, :] += nn(act[s, :], wr[cols, :])
        e2[s, :] += nt(gh[s, :], we[:, cols])

    @pl.when(j == 3)
    def _():
        gn = jnp.zeros((1, D), F32)
        shf = gn
        ob = gn
        for i in range(n):
            s = slice(i * ROWS, (i + 1) * ROWS)
            o = nn(pmt_ref[...], acc[s, :].astype(BF)).astype(BF)
            stay_ref[i] = o[:TOK]
            send_ref[i] = o[TOK:]
            xh, r = norm_parts(mid[s, :])
            d = e2[s, :]
            gn = gn + colsum(d * xh)
            shf = shf + colsum(d)
            d = d * gain
            gm = g[s, :].astype(F32) + r * (
                d - jnp.mean(d, axis=-1, keepdims=True) - xh * jnp.mean(d * xh, axis=-1, keepdims=True)
            )
            gb = gm.astype(BF)
            gmid_ref[i] = gb
            ob = ob + colsum(gb.astype(F32))
            g[s, :] = gb
            datt_ref[i] = nt(gb, wo[...]).astype(BF)
            n2[s, :] = attended(i)
        for c, ref in ((1 - core, os_ref), (core, ok_ref)):
            go = tn(n2[...], g[:, pl.ds(pl.multiple_of(c * CH, 128), CH)]).astype(BF)
            for b in range(4):
                ref[jnp.bitwise_xor(me, b), 0] = go[b * OWN : (b + 1) * OWN, :]
        small_ref[1:2, :] = gn
        small_ref[2:3, :] = shf
        small_ref[3:4, :] = ob


def crossed(r):
    return 2 * (r % 2) + r // 2


def middle_call(spot, tok, atts, g, pmt, vecs, eb, at, plan, pieces, after):
    n = tok.shape[0]
    N = n * ROWS
    blocks = SD((4, 4, OWN, CH), BF)

    def chunk(j, spot):
        return 2 * jnp.bitwise_xor(spot[1], 1 - j // 2) + j % 2

    def early(j):
        return jnp.minimum(j, 1)

    def late(j):
        return jnp.maximum(j, 2) - 2

    rows = full((n, ROWS, D), **ONE)
    third = full((n, ROWS, LP), **ONE)
    cut = full((n, TOK, D), **ONE)
    outer = full((4, 1, OWN, CH), **ONE)
    args = (spot, tok, *atts, g, pmt, vecs, eb, at, *pieces)

    def body(*refs):
        middle_kernel(plan, len(pieces), *refs[: len(args)], *refs[len(args) + len(after) :])

    grid_spec = pltpu.PrefetchScalarGridSpec(
        num_scalar_prefetch=1,
        grid=(4,),
        in_specs=[rows, third, third, third, rows, full((ROWS, ROWS)), full((8, D)),
                  pl.BlockSpec((1, 1, 2 * CH), lambda j, spot: (chunk(j, spot), 0, 0)), smem()]
        + [any_space()] * (len(pieces) + len(after)),
        out_specs=[cut, cut, rows, rows, outer, outer,
                   pl.BlockSpec((4, 2, OWN, CH), lambda j, spot: (0, early(j), 0, 0)),
                   pl.BlockSpec((4, 2, OWN, CH), lambda j, spot: (0, late(j), 0, 0)),
                   pl.BlockSpec((2, 4, OWN, CH), lambda j, spot: (jnp.bitwise_xor(early(j), spot[0] // 2), 0, 0, 0)),
                   pl.BlockSpec((2, 4, OWN, CH), lambda j, spot: (jnp.bitwise_xor(late(j), spot[0] // 2), 0, 0, 0)),
                   pl.BlockSpec((1, 1, 2 * CH), lambda j, spot: (chunk(j, spot), 0, 0)), full((8, D))],
        scratch_shapes=[pltpu.VMEM((D, D), BF), pltpu.VMEM((D, FF), BF), pltpu.VMEM((FF, D), BF),
                        pltpu.VMEM((N, D), F32), pltpu.VMEM((N, D), BF), pltpu.VMEM((N, D), BF), pltpu.VMEM((D, N), BF),
                        pltpu.VMEM((N, D), F32), pltpu.VMEM((N, D), F32), pltpu.VMEM((N, 2 * CH), BF), pltpu.VMEM((N, 2 * CH), BF),
                        pltpu.SemaphoreType.DMA((len(plan[1]),))],
    )
    return pl.pallas_call(
        body,
        grid_spec=grid_spec,
        out_shape=[SD((n, TOK, D), BF), SD((n, TOK, D), BF), SD((n, ROWS, D), BF), SD((n, ROWS, D), BF),
                   SD((4, 1, OWN, CH), BF), SD((4, 1, OWN, CH), BF), blocks, blocks, blocks, blocks,
                   SD((4, 1, 2 * CH), F32), SD((8, D), F32)],
        compiler_params=params(62),
        cost_estimate=cost(6e10, 40 * MB, 7e6),
        name="middle",
    )(*args, *after)


def back_kernel(proj_ref, pt_ref, da_ref, gp_ref, db_ref):
    @pl.when(pl.program_id(0) == 0)
    def _():
        db_ref[...] = jnp.zeros_like(db_ref)

    hid = lane_head((TOK, LB))
    scale = HD**-0.5
    for w in range(2):
        r = slice(w * TOK, (w + 1) * TOK)
        for blk in range(LP // LB):
            l = blk * LB
            q = proj_ref[0, r, l : l + LB]
            k = proj_ref[0, r, LP + l : LP + l + LB]
            v = proj_ref[0, r, 2 * LP + l : 2 * LP + l + LB]
            do = da_ref[0, r, l : l + LB]
            qt, kt, dt = q.T, k.T, do.T
            dq, dk, dv = [], [], []
            dps = nn(jnp.concatenate([jnp.where(hid == h, v, jnp.zeros_like(v)) for h in range(HB)], axis=0), dt)
            for h in range(HB):
                hh = blk * HB + h
                s = slice(HD * h, HD * h + HD)
                dp = dps[h * TOK : (h + 1) * TOK]
                pb = pt_ref[0, w, hh]
                p = pb.astype(F32)
                pd = p * dp
                ds = pd - p * colsum(pd)
                db_ref[hh] += ds
                dsb = ds.astype(BF)
                dq.append(nn(kt[s, :], dsb))
                dk.append(nt(qt[s, :], dsb))
                dv.append(nt(dt[s, :], pb))
            gp_ref[0, r, l : l + LB] = (jnp.concatenate(dq, axis=0) * scale).astype(BF).T
            gp_ref[0, r, LP + l : LP + l + LB] = (jnp.concatenate(dk, axis=0) * scale).astype(BF).T
            gp_ref[0, r, 2 * LP + l : 2 * LP + l + LB] = jnp.concatenate(dv, axis=0).astype(BF).T


def back_call(group, proj, pt, da, after):
    n = proj.shape[0]

    def blk(*s):
        return pl.BlockSpec((1,) + s, lambda i: (i,) + (0,) * len(s))

    return run(
        back_kernel, 3, (proj, pt, da), after,
        grid=(n,),
        in_specs=[blk(ROWS, 3 * LP), blk(2, HP, TOK, TOK), pl.BlockSpec((1, ROWS, LP), lambda i: (i, 0, group))],
        out_specs=[blk(ROWS, 3 * LP), full((HP, TOK, TOK))],
        out_shape=[SD((n, ROWS, 3 * LP), BF), SD((HP, TOK, TOK), F32)],
        compiler_params=params(),
        cost_estimate=cost(1.8e10, 10 * MB),
        name="attend_back",
    )


def inner_kernel(spot_ref, n1t_ref, gp0_ref, gp1_ref, gp2_ref, os_ref, ok_ref, xs_ref, xk_ref, ys_ref, yk_ref, sum_ref):
    me = spot_ref[0]
    core = spot_ref[1]
    n = gp0_ref.shape[0]
    ys_ref[:, 1:2] = os_ref[...]
    yk_ref[:, 1:2] = ok_ref[...]
    for p, gp_ref, send, keep, m in ((0, gp0_ref, xs_ref, xk_ref, 0), (1, gp1_ref, ys_ref, yk_ref, 0), (2, gp2_ref, xs_ref, xk_ref, 1)):
        gp = gp_ref[...].reshape(n * ROWS, 3 * LP)
        sum_ref[p] = colsum(gp.astype(F32))
        gi = nn(n1t_ref[...], gp).astype(BF)

        for c in range(2):
            @pl.when(core == c)
            def _():
                for b in range(4):
                    r = slice(b * OWN, (b + 1) * OWN)
                    rel = jnp.bitwise_xor(me, b)
                    rel = rel if p == 1 else crossed(rel)
                    keep[rel, m] = gi[r, c * CH : (c + 1) * CH]
                    send[rel, m] = gi[r, (1 - c) * CH : (2 - c) * CH]


def inner_call(spot, n1t, gps, outer, after):
    block = SD((4, 2, OWN, CH), BF)
    return single(
        inner_kernel, (spot, n1t, *gps, *outer), [block] * 4 + [SD((3, 1, 3 * LP), F32)], after,
        cost_estimate=cost(1.2e10, 12 * MB), name="inner_grad",
    )


def last_kernel(tok_ref, gmid_ref, vec_ref, pmt_ref, gp0_ref, gp1_ref, gp2_ref, w0_ref, w1_ref, w2_ref,
                small_ref, stay_ref, send_ref):
    @pl.when(pl.program_id(0) == 0)
    def _():
        small_ref[...] = jnp.zeros_like(small_ref)

    d = nt(gp0_ref[0], w0_ref[...]) + nt(gp1_ref[0], w1_ref[...]) + nt(gp2_ref[0], w2_ref[...])
    xh, r = norm_parts(tok_ref[0].astype(F32))
    small_ref[0:1, :] += colsum(d * xh)
    small_ref[1:2, :] += colsum(d)
    d = d * vec_ref[2:3, :]
    gm = gmid_ref[0].astype(F32) + r * (d - jnp.mean(d, axis=-1, keepdims=True) - xh * jnp.mean(d * xh, axis=-1, keepdims=True))
    o = nn(pmt_ref[...], gm.astype(BF)).astype(BF)
    stay_ref[0] = o[:TOK]
    send_ref[0] = o[TOK:]


def last_call(first, n, tok, gmid, gain, pmt, gps, ws, after):
    def blk(*s):
        return pl.BlockSpec((1,) + s, lambda i: (first + i,) + (0,) * len(s))

    cut = pl.BlockSpec((1, TOK, D), lambda i: (i, 0, 0))

    return run(
        last_kernel, 10, (tok, gmid, gain, pmt, *gps, *ws), after,
        grid=(n,),
        in_specs=[blk(ROWS, D), blk(ROWS, D), full((8, D)), full((ROWS, ROWS))] + [blk(ROWS, 3 * LP)] * 3
        + [full((D, 3 * LP), **ONE)] * 3,
        out_specs=[full((8, D)), cut, cut],
        out_shape=[SD((8, D), F32), SD((n, TOK, D), BF), SD((n, TOK, D), BF)],
        compiler_params=params(),
        cost_estimate=cost(2e10, 20 * MB),
        name="last",
    )


def vector_finish_kernel(count, spot_ref, mine_ref, other_ref, thr_ref, inner_ref, inb_ref, outb_ref, upb_ref, downb_ref, g1_ref, s1_ref,
                         g2_ref, s2_ref, table_ref, clip_ref, factor_ref, max_ref, sums_ref):
    shard = spot_ref[2]
    sums_ref[...] = join_vectors(mine_ref[...], other_ref[...])

    def part(ref, rows, step=1):
        size = ref.shape[0]
        start = shard * size
        row = sums_ref[pl.ds(rows + step * (start // D), 1), :]
        row = jnp.broadcast_to(row, (8, D))
        ref[...] = pltpu.roll(row, (D - start % D) % D, 1)[0:1, :size].reshape(size)

    part(inb_ref, V_IN, 2)
    part(upb_ref, V_UP)
    for i, ref in enumerate((downb_ref, g2_ref, s2_ref, outb_ref)):
        part(ref, V_SMALL + i)
    part(g1_ref, V_ONE)
    part(s1_ref, V_ONE + 1)
    table_ref[...] = sums_ref[V_TABLE : V_TABLE + HEADS, : SPAN * SPAN]
    top = sums_ref[V_PEAK : V_PEAK + 1, :HEADS]
    factor = thr_ref[...].reshape(1, HEADS)
    factor = factor / jnp.maximum(top, factor)
    max_ref[...] = top.reshape(HEADS)
    factor_ref[...] = factor.reshape(HEADS)
    root = jnp.broadcast_to(jnp.sqrt(factor), (8, HEADS))
    head = lax.broadcasted_iota(jnp.int32, (HEADS, D), 0)
    col = lax.broadcasted_iota(jnp.int32, (HEADS, D), 1) // HD
    scale = lax.dot_general(root, (head == col).astype(F32), (((1,), (0,)), ((), ())), preferred_element_type=F32,
                            precision=lax.Precision.HIGHEST)[0:1, :]
    for k in range(2):
        clip_ref[:, k * D : (k + 1) * D] = (inner_ref[:, k * D : (k + 1) * D].astype(F32) * scale).astype(BF)
    clip_ref[:, 2 * D :] = inner_ref[:, 2 * D :]


def vector_finish(place, mine, other, threshold, inner, count):
    line = SD((D // count,), F32)
    return single(
        functools.partial(vector_finish_kernel, count), (place, mine, other, threshold, inner),
        [SD((2 * D // count,), F32), line, SD((FF // count,), F32), line, line, line, line, line,
         SD((HEADS, SPAN * SPAN), F32), SD(inner.shape, BF), SD((HEADS,), F32), SD((HEADS,), F32)],
        scratch=[pltpu.VMEM((V_ROWS, D), F32)],
        cost_estimate=cost(1e7, 3 * MB), name="vector_finish",
    )


def feed_finish_kernel(spot_ref, mine_ref, other_ref, ge_ref, gr_ref):
    for core in range(2):
        @pl.when(spot_ref[1] == core)
        def _():
            for c, ref in ((core, mine_ref), (1 - core, other_ref)):
                for b in range(4):
                    ge_ref[:, (2 * b + c) * CH : (2 * b + c + 1) * CH] = ref[b].astype(F32)
                    r = c * CH + (b // 2) * OWN
                    gr_ref[r : r + OWN, (b % 2) * CH : (b % 2 + 1) * CH] = ref[4 + b].astype(F32)


def inner_columns(p, c):
    if c == 0:
        return [(0, LP, p * LP), (LP, LP // 2, D + p * LP)]
    return [(0, LP // 2, D + p * LP + LP // 2), (LP // 2, LP, 2 * D + p * LP)]


def inner_finish_kernel(spot_ref, mine_ref, other_ref, gi_ref, go_ref):
    for core in range(2):
        @pl.when(spot_ref[1] == core)
        def _():
            for c, ref in ((core, mine_ref), (1 - core, other_ref)):
                for k, p in enumerate((0, 2, 1)):
                    for at, size, put in inner_columns(p, c):
                        gi_ref[:, put : put + size] = ref[k, :, at : at + size].astype(F32)
                go_ref[:, c * CH : (c + 1) * CH] = ref[3].astype(F32)


def finish_kernel(count, place_ref, mine_ref, other_ref, thr_ref, inner_ref, fm_ref, fo_ref, im_ref, io_ref, *outs):
    vectors, (ge_ref, gr_ref, gi_ref, go_ref, sums_ref) = outs[:12], outs[12:]
    inner_finish_kernel(place_ref, im_ref, io_ref, gi_ref, go_ref)
    feed_finish_kernel(place_ref, fm_ref, fo_ref, ge_ref, gr_ref)
    vector_finish_kernel(count, place_ref, mine_ref, other_ref, thr_ref, inner_ref, *vectors, sums_ref)


def finish(place, vectors, threshold, inner, feed, rest):
    line = SD((D // 4,), F32)
    return single(
        functools.partial(finish_kernel, 4), (place, *vectors, threshold, inner, *feed, *rest),
        [SD((2 * D // 4,), F32), line, SD((FF // 4,), F32), line, line, line, line, line,
         SD((HEADS, SPAN * SPAN), F32), SD(inner.shape, BF), SD((HEADS,), F32), SD((HEADS,), F32),
         SD((OWN, FF), F32), SD((2 * CH, D), F32), SD((OWN, 3 * D), F32), SD((OWN, D), F32)],
        scratch=[pltpu.VMEM((V_ROWS, D), F32)], cost_estimate=cost(1e7, 12 * MB), name="finish",
    )


def swap(block, axis, bit):
    count = lax.axis_size(axis)
    return lax.ppermute(block, axis, [(i, i ^ bit) for i in range(count) if i ^ bit < count])


def join_vectors(a, b):
    row = lax.broadcasted_iota(jnp.int32, a.shape, 0)
    return jnp.where(row == V_PEAK, jnp.maximum(a, b), a + b)


class Everywhere:
    def __init__(self, sums, ones, direct):
        self.value = [sums, *ones]
        self.flying = []
        self.hops = [("replica", (1,)), ("shard", (1, 2, 3)), ("replica", (2,)), ("half", (1,))]
        if not direct:
            self.hops = [
                (axis, (1 << k,))
                for axis in ("shard", "replica", "half") for k in range((lax.axis_size(axis) - 1).bit_length())
            ]
        self.done = False

    def inputs(self):
        return self.value + self.flying

    def compute(self, values, low, low2):
        v, *others = values
        if not self.flying:
            ones = others[0] + others[1]
            return [jnp.concatenate([v[:V_ONE], ones[:2], v[V_ONE + 2 :]], axis=0)]
        if len(others) == 3:
            return [join_vectors(join_vectors(v, others[0]), join_vectors(others[1], others[2]))]
        return [join_vectors(v, others[0])]

    def launch(self, outs):
        self.value = outs
        self.done = not self.hops
        if self.hops:
            axis, bits = self.hops.pop(0)
            self.flying = [swap(outs[0], axis, bit) for bit in bits]


def near(block):
    return [swap(block, "shard", 1), swap(block, "shard", 2)]


def fence(*values):
    return lax.optimization_barrier(values)


def add(a, b):
    return (a.astype(F32) + b.astype(F32)).astype(BF)


class Reduction:
    def __init__(self, sends, keeps, quarters):
        self.quarters = quarters
        self.keep = keeps
        self.stage = 0
        self.sent = sends
        self.flying = [swap(v, "half", 1) for v in sends]

    def inputs(self):
        return list(self.keep) + list(self.flying)

    def compute(self, values, low, low2):
        hlf = OWN // 2
        kept, got = values[: len(self.keep)], values[len(self.keep) :]
        if self.stage == 0:
            return [add(k[:2], g[:2]) for k, g in zip(kept, got)] + [add(k[2:], g[2:]) for k, g in zip(kept, got)]
        if self.stage == 1:
            return [add(k[0], g[0]) for k, g in zip(kept, got)] + [add(k[1], g[1]) for k, g in zip(kept, got)]
        if self.stage == 2:
            if self.quarters:
                u, v = (add(k, g) for k, g in zip(kept, got))
                return [jnp.where(low, u, v), jnp.where(low, v, u)]
            v = jnp.concatenate([add(k, g) for k, g in zip(kept, got)], axis=0)
            return [jnp.where(low, v[:, :hlf], v[:, hlf:]), jnp.where(low, v[:, hlf:], v[:, :hlf])]
        v = kept[0]
        if self.quarters and self.stage == 3:
            v = add(v, got[0])
            return [jnp.where(low2, v[:, :hlf], v[:, hlf:]), jnp.where(low2, v[:, hlf:], v[:, :hlf])]
        if self.quarters and self.stage == 5:
            return [jnp.concatenate([jnp.where(low2, v, got[0]), jnp.where(low2, got[0], v)], axis=1)]
        if self.quarters and self.stage == 6:
            return [jnp.concatenate([jnp.where(low, v, got[0]), jnp.where(low, got[0], v)], axis=0)]
        if self.stage in (3, 4):
            return [add(v, got[0])]
        return [jnp.concatenate([jnp.where(low, v, got[0]), jnp.where(low, got[0], v)], axis=1)]

    def launch(self, outs):
        if self.stage < 2:
            half = len(outs) // 2
            self.keep, self.sent = outs[:half], outs[half:]
            bits = (1, 2) if self.stage == 0 else (2, 1)
            self.flying = [swap(v, "shard", bit) for v, bit in zip(self.sent, bits)]
        else:
            self.keep, self.sent = outs[:1], outs[-1:]
            if self.stage == (6 if self.quarters else 5):
                self.flying = [swap(self.keep[0], "half", 1)]
            else:
                far = (3, 4) if self.quarters else (3,)
                self.flying = [swap(self.sent[0], "replica", 2 if self.stage in far else 1)]
        self.stage += 1


def hop_kernel(chains, counts, place_ref, *refs):
    replica = place_ref[3]
    low, low2 = (replica & 1) == 0, (replica & 2) == 0
    refs = list(refs)
    inputs = [[refs.pop(0)[...] for _ in range(count)] for count in counts]
    for chain, values in zip(chains, inputs):
        for out in chain.compute(values, low, low2):
            refs.pop(0)[...] = out


def together(place, chains, *others, plain=False):
    flying, others = fence([c.flying for c in chains], others)
    for c, v in zip(chains, flying):
        c.flying = v
    inputs = [c.inputs() for c in chains]
    low, low2 = (place[3] & 1) == 0, (place[3] & 2) == 0
    shapes = [jax.eval_shape(c.compute, v, low, low2) for c, v in zip(chains, inputs)]
    if plain:
        outs = [c.compute(v, low, low2) for c, v in zip(chains, inputs)]
    else:
        flat = [x for v in inputs for x in v]
        results = list(single(
            functools.partial(hop_kernel, chains, [len(v) for v in inputs]), (place, *flat),
            [SD(x.shape, x.dtype) for v in shapes for x in v], cost_estimate=cost(1e7, 4 * MB), name="hop",
        ))
        outs = [[results.pop(0) for _ in v] for v in shapes]
    for c, v in zip(chains, outs):
        c.launch(v)
    return others


def quick_layout(me, core):
    def places(rows):
        at = [me * rows]
        for c in (core, 1 - core):
            at += [(me ^ r) * rows + c * (rows // 2) for r in (1, 2, 3)]
        return at

    first = [(k, 0, OWN, 0, 3 * LP, 0, 0) for k in range(4)], [(me ^ r) * OWN for r in range(4)]
    others = [
        ([(k, 0, OWN if k == 0 else OWN // 2, c, 3 * LP, 0, 0) for k in range(7)], places(OWN)) for c in (0, 3 * LP)
    ]
    hlf = OWN // 2
    short = places(OWN)
    long = [None] + [c * 4 * CH + (me ^ r) * CH for c in (core, 1 - core) for r in (1, 2, 3)]
    plan, at = [(0, 0, OWN, 0, D, 0, 0)], [short[0]]
    for k in range(8):
        plan.append((1, 0, OWN, hidden_block(k) * CH, CH, 1, k * CH))
        at.append(short[0])
    for c in range(2):
        plan.append((2, c * CH, CH, 0, D, 2, 0))
        at.append(c * 4 * CH + me * CH)
    parts = [(b * hlf, hlf, 1, b * D) for b in range(4)] + [(4 * hlf, hlf, 0, 0), (5 * hlf, 4 * hlf, 2, 0)]

    def add_piece(source, lo, hi, place):
        for row, rows, target, column in parts:
            a, b = max(row, lo), min(row + rows, hi)
            if a < b and target == 1:
                for c in range(2):
                    plan.append((source, a - lo, b - a, c * CH, CH, 1, c * 4 * CH + column // 2))
                    at.append(short[place] + (a - row))
            elif a < b:
                plan.append((source, a - lo, b - a, 0, D, target, column))
                at.append((long if target == 2 else short)[place] + (a - row))

    for side in range(2):
        for k in range(2):
            add_piece(3 + 4 * side + k, 0, BIG, 1 + 3 * side + k)
        add_piece(5 + 4 * side, 0, BIG // 2, 3 + 3 * side)
        add_piece(6 + 4 * side, BIG // 2, BIG, 3 + 3 * side)
    return [first, *others, (plan, at)]


def fallback_layout():
    first = [([(0, 0, D, c, 3 * LP, 0, 0)], [0]) for c in (0, 0, 3 * LP)]
    plan, at = [(0, 0, D, 0, D, 0, 0)], [0]
    for k in range(8):
        plan += [(1, 0, D, hidden_block(k) * CH, CH, 1, k * CH), (2, hidden_block(k) * CH, CH, 0, D, 2, 0)]
        at += [0, k * CH]
    return first + [(plan, at)]


def plans_of(layout):
    base, plans = 4, []
    for entries, rows in layout:
        plans.append((base, entries))
        base += len(rows)
    return plans


def quick_plans():
    return plans_of(quick_layout(0, 0))


def fallback_plans():
    return plans_of(fallback_layout())


def fallback_places():
    return [jnp.int32(v) for _, rows in fallback_layout() for v in rows]


def index_table():
    return np.array(
        [
            [me, core, me, replica] + [v for _, rows in quick_layout(me, core) for v in rows]
            for replica in range(4) for me in range(4) for core in range(2)
        ],
        np.int32,
    )


def shards(images, cotangent, present, threshold, inner_weight, inner_bias, outer_weight, outer_bias, expand_weight,
           expand_bias, reduce_weight, reduce_bias, first_gain, first_shift, second_gain, second_shift, bias_table):
    n = images.shape[0]
    core = lax.axis_index("half")
    shard = lax.axis_index("shard")
    replica = lax.axis_index("replica")
    shard_count = lax.axis_size("shard")
    quick = shard_count == 4 and lax.axis_size("replica") == 4
    me = shard if quick else jnp.int32(0)
    if quick:
        spot = lax.dynamic_index_in_dim(jnp.asarray(index_table()), (replica * 4 + shard) * 2 + core, 0, False)
    else:
        spot = jnp.stack([me, core, shard, replica] + fallback_places()).astype(jnp.int32)
    place = spot
    own_images = images.reshape(n, ROWS, D)
    own_grad = cotangent.reshape(n, ROWS, D)
    vectors = (inner_bias, outer_bias, expand_bias, reduce_bias, first_gain, first_shift, second_gain, second_shift)
    order = jnp.asarray(row_order(), BF)
    back_order = jnp.asarray(row_order().T, BF)
    alive = present.astype(F32).reshape(1, n)
    table_rows = jnp.pad(bias_table.astype(F32).T, ((0, 0), (0, WIDE - bias_table.shape[0])))
    if quick:
        first, others, others_half, up = first_call(spot, vectors, inner_weight, own_images, own_grad)
        first, up, spot, others_half = fence(first, up, spot, others_half)
        get_first = near(first)
        upper = swap(up, "half", 1)
        masks_0 = bias_call(0, table_rows)
        big = cut_call(spot, outer_weight, expand_weight, reduce_weight)
        get_first, upper, masks_0, others_half, big = fence(get_first, upper, masks_0, others_half, big)
        get_first.append(swap(get_first[0], "shard", 2))
        get_others = near(others_half)
        tok, g, grad_down = prep_call(own_images, own_grad, upper, alive, order)
        get_first, get_others, tok, spot, big = fence(get_first, get_others, tok, spot, big)
        first_pieces = [first] + get_first
        get_others.append(swap(get_others[1], "shard", 1))
        in_bias, up_bias, vecs, n1, n1t = vector_call(spot, first_pieces, tok)
        get_others, n1, big = fence(get_others, n1, big)
        others_back = [swap(v, "half", 1) for v in get_others]
        get_big = near(big)
    else:
        masks_0 = bias_call(0, table_rows)
        upper = jnp.concatenate([swap(own_images[:, :TOK], "half", 1), swap(own_grad[:, :TOK], "half", 1)])
        whole_vectors = [lax.all_gather(v, "shard", axis=0, tiled=True).reshape(4, -1) for v in vectors]
        parts = jnp.stack([jnp.pad(v, ((0, 0), (0, D - v.shape[1]))) for v in whole_vectors], axis=1)
        parts = [jnp.pad(parts[r], ((0, 8), (0, 0))) for r in range(4)]
        thirds = inner_weight.reshape(-1, 3, 3, LP).transpose(0, 2, 1, 3).reshape(-1, 3, 3 * LP)
        first = thirds[:, 0]
        others = thirds[:, 1:].reshape(-1, 6 * LP)

        tok, g, grad_down = prep_call(own_images, own_grad, upper, alive, order)
        in_bias, up_bias, vecs, n1, n1t = vector_call(spot, parts, tok)

    if quick:
        first_at = in_at = spot
        in_plans = quick_plans()[:3]
    else:
        first_at = in_at = spot
        first_pieces = [lax.all_gather(first, "shard", axis=0, tiled=True)]
        others_pieces = [lax.all_gather(others, "shard", axis=0, tiled=True)]
        in_plans = fallback_plans()[:3]

    results = [attend_call(0, spot, n1, in_bias, masks_0, first_at, in_plans[0], first_pieces, [])]
    if quick:
        others_back, results, table_rows = fence(others_back, results, table_rows)
    masks_1 = bias_call(1, table_rows)
    if quick:
        masks_1, spot, table_rows = fence(masks_1, spot, table_rows)
        others_pieces = [others] + get_others + others_back
    results.append(attend_call(1, spot, n1, in_bias, masks_1, in_at, in_plans[1], others_pieces, []))
    if quick:
        get_big, results, table_rows = fence(get_big, results, table_rows)
        lower, upper_rows = halves_call(*get_big)
        far = [swap(lower, "shard", 2), swap(upper_rows, "shard", 1)]
        big_back = [swap(v, "half", 1) for v in get_big]
    masks_2 = bias_call(2, table_rows)
    results.append(attend_call(2, spot, n1, in_bias, masks_2, in_at, in_plans[2], others_pieces, []))
    if quick:
        far, big_back, results = fence(far, big_back, results)
        far_back = [swap(v, "half", 1) for v in far]
        far_back, results = fence(far_back, results)
        pieces = [outer_weight, expand_weight, reduce_weight] + get_big + far + big_back + far_back
        plan = quick_plans()[3]
    else:
        pieces = [lax.all_gather(v, "shard", axis=0, tiled=True) for v in (outer_weight, expand_weight, reduce_weight)]
        plan = fallback_plans()[3]
    at = spot
    projs, pts, atts, peak, ws = zip(*results)
    (stay, send, gmid, datt, out_send, out_keep, e_send, e_keep, r_send, r_keep, grad_up, small) = middle_call(
        spot, tok, atts, g, back_order, vecs, up_bias, at, plan, pieces, []
    )
    def wait_for(chains):
        return [v for c in chains for v in c.sent]

    after = []
    if quick:
        feed = Reduction([e_send, r_send], [e_keep, r_keep], True)
    lower_out = swap(send, "half", 1)
    gp0, db0 = back_call(0, projs[0], pts[0], datt, [])
    if quick:
        gp0, lower_out, projs = together(place, [feed], gp0, lower_out, projs)
        after = wait_for([feed])
    gp1, db1 = back_call(1, projs[1], pts[1], datt, after)
    gp2, db2 = back_call(2, projs[2], pts[2], datt, [gp1])
    x_send, x_keep, y_send, y_keep, sums_in = inner_call(spot, n1t, (gp0, gp1, gp2), (out_send, out_keep), [])
    peak = jnp.concatenate(peak, axis=2)
    peaks = jnp.max(jnp.where((present > 0)[:, None, None, None], peak, NEGATIVE), axis=(0, 1, 3)).reshape(1, HEADS)
    after = [x_send]
    if quick:
        x_send, y_send, gp2 = together(place, [feed], x_send, y_send, gp2)
        rest = Reduction([x_send, y_send], [x_keep, y_keep], False)
        after = wait_for([feed])
    half = n // 2
    one_a, gstay_a, gsend_a = last_call(0, half, tok, gmid, vecs, back_order, (gp0, gp1, gp2), ws, after)
    after = [gsend_a]
    if quick:
        gsend_a, one_a = together(place, [rest, feed], gsend_a, one_a)
        after = wait_for([rest, feed])
    lower_a = swap(gsend_a, "half", 1)
    one_b, gstay_b, gsend_b = last_call(half, n - half, tok, gmid, vecs, back_order, (gp0, gp1, gp2), ws, after)
    after = [gsend_b]
    if quick:
        gsend_b, lower_a = together(place, [rest, feed], gsend_b, lower_a)
        after = wait_for([rest, feed])
    lower_b = swap(gsend_b, "half", 1)
    sums = table_call((db0, db1, db2), grad_up, grad_down, small, sums_in, peaks, after)
    every = Everywhere(sums, (one_a, one_b), quick)
    if quick:
        rest.flying, feed.flying, lower_b = fence(rest.flying, feed.flying, lower_b)
        together(place, [rest, every, feed])
        block_out = jnp.concatenate([lower_out, stay], axis=1)
        (block_out,) = together(place, [rest, every, feed], block_out)
        grad_images = jnp.concatenate([jnp.concatenate([lower_a, lower_b]), jnp.concatenate([gstay_a, gstay_b])], axis=1)
        (grad_images,) = together(place, [rest, every], grad_images)
        rest.flying, every.flying, feed.flying = fence(rest.flying, every.flying, feed.flying)
        together(place, [rest, every, feed])
    else:
        while every.hops:
            together(place, [every])
        block_out = jnp.concatenate([lower_out, stay], axis=1)
        grad_images = jnp.concatenate([jnp.concatenate([lower_a, lower_b]), jnp.concatenate([gstay_a, gstay_b])], axis=1)

    vectors = (every.value[0], every.flying[0])
    if quick:
        *vectors, grad_expand, grad_reduce, grad_inner, grad_outer = finish(
            place, vectors, threshold, inner_weight, feed.keep + feed.flying, rest.keep + rest.flying
        )
    else:
        def halves(keep, send, axis):
            lo = jnp.where(core == 0, keep, send)
            hi = jnp.where(core == 0, send, keep)
            return jnp.concatenate([lo, hi], axis=axis)

        def whole(keep, send):
            both = halves(keep[:, :, :, None], send[:, :, :, None], 3)
            return both.transpose(0, 2, 1, 3, 4).reshape(D, -1)

        def settle(v):
            v = lax.psum_scatter(v.astype(BF), "shard", scatter_dimension=0, tiled=True)
            return lax.psum(v, ("replica", "half")).astype(F32)

        def rows_of(v):
            return v.reshape(4, 1, 2, 2, OWN, CH).transpose(0, 1, 2, 4, 3, 5).reshape(4, 1, CH, D)

        def straight(v):
            return jnp.stack([v[0], v[2], v[1], v[3]])

        grad_reduce = settle(halves(rows_of(r_keep), rows_of(r_send), 1).reshape(FF, D))
        grad_expand = settle(whole(straight(e_keep), straight(e_send)))
        grad_outer = settle(whole(out_keep, out_send))
        x_keep, x_send = straight(x_keep), straight(x_send)
        by_third = [
            whole(x_keep[:, :1], x_send[:, :1]), whole(y_keep[:, :1], y_send[:, :1]), whole(x_keep[:, 1:], x_send[:, 1:])
        ]
        by_third = jnp.stack(by_third, axis=1).reshape(D, 3, 3, LP).transpose(0, 2, 1, 3).reshape(D, 3 * D)
        grad_inner = settle(by_third)

        vectors = vector_finish(place, *vectors, threshold, inner_weight, shard_count)
    (grad_inbias, grad_outbias, grad_upbias, grad_downbias, grad_gain_1, grad_shift_1, grad_gain_2, grad_shift_2, grad_table,
     clipped, factors, maxima) = vectors
    block_out = block_out.reshape(images.shape)
    grad_images = grad_images.reshape(images.shape)
    return (
        block_out,
        grad_images,
        grad_inner,
        grad_inbias,
        grad_outer,
        grad_outbias,
        grad_expand,
        grad_upbias,
        grad_reduce,
        grad_downbias,
        grad_gain_1,
        grad_shift_1,
        grad_gain_2,
        grad_shift_2,
        grad_table.T,
        clipped,
        factors,
        maxima,
    )


def solution(mesh):
    rows = P(("replica", "shard"), "half", None, None)
    cut = P("shard", None)
    line = P("shard")
    return jax.shard_map(
        shards,
        mesh=mesh,
        in_specs=(rows, rows, P(("replica", "shard")), P(), cut, line, cut, line, cut, line, cut, line, line, line, line,
                  line, P()),
        out_specs=(rows, rows, cut, line, cut, line, cut, line, cut, line, line, line, line, line, P(), cut, P(), P()),
        check_vma=False,
    )
```
